128 devices in a mesh: lat: 16 (over z_lo, x, core), lon: 8 (over z_hi, y).
Axes of the slice: x: 4, y: 4, z: 4 (z_hi: 2, z_lo: 2; z = z_hi * 2 + z_lo), core: 2. Of those that a mesh axis runs over, the one named last changes fastest.
Arguments:
- inputs: bfloat16 [2, 192, 147456], P(None, 'lat', 'lon'), may hold values from -40 to 40
- cotangent: bfloat16 [2, 192, 147456], P(None, 'lat', 'lon'), may hold values from -4 to 4
- norm_gain: float32 [192], replicated, may hold values from 0.5 to 1.5
- norm_shift: float32 [192], replicated, may hold values from -2 to 2
- w_qkv: bfloat16 [192, 576], replicated, may hold values from -0.4375 to 0.4375
- w_proj: bfloat16 [192, 192], replicated, may hold values from -0.4375 to 0.4375
- bias_table: float32 [32, 6, 3312], P('lat'), may hold values from -4 to 284
Outputs:
- block_out: bfloat16 [2, 192, 147456], P(None, 'lat', 'lon')
- grad_in: bfloat16 [2, 192, 147456], P(None, 'lat', 'lon')
- grad_qkv: float32 [192, 576], replicated
- grad_proj: float32 [192, 192], replicated
- grad_bias: float32 [32, 6, 3312], P('lat')
The draws below stay inside these ranges and needn't reach their ends.
All inputs are finite; a program needn't handle non-finite values.
Results may differ from the reference program's by a relative error of at most 0.0085.
Values may be sent and summed in bfloat16 or wider, within the bound.
A program may use at most 128 MiB of HBM per device.

```python
import math
import jax
import jax.numpy as jnp
import numpy as np
from jax import lax

C = 192
HEADS = 6
Z = 2
WZ = 2
WLAT = 6
WLON = 12
WIN = 144
POS = 3312
LAT = 192
LON = 768
NWLAT = 32


def draw_inputs(key, part):
    key = jax.random.fold_in(key, 11)
    key_base, key_rows, key_chan = jax.random.split(key, 3)
    row_scale = jnp.exp(jax.random.uniform(key_rows, (Z, LAT, LON, 1), jnp.float32, math.log(0.3), math.log(3.0)))
    chan_scale = jnp.exp(jax.random.uniform(key_chan, (C,), jnp.float32, math.log(0.3), math.log(3.0)))
    base = jnp.clip(jax.random.normal(key_base, (Z, LAT, LON, C), jnp.float32), -4.0, 4.0)
    field_out = base * row_scale * chan_scale
    return field_out.reshape(Z, LAT, LON * C).astype(jnp.bfloat16)


def draw_bias_table(key, part):
    key = jax.random.fold_in(key, 23)
    key_base = jax.random.fold_in(key, 0)
    shape_all = (NWLAT, HEADS, POS)
    table_out = jnp.clip(jax.random.normal(key_base, shape_all, jnp.float32), -4.0, 4.0)
    return table_out.astype(jnp.float32)


def block_scale(stream_key, extent, pieces, least, high):
    gain = 1.0
    for axis_at, parts in pieces:
        steps = jax.random.uniform(jax.random.fold_in(jax.random.fold_in(stream_key, 6), axis_at), (parts,), jnp.float32, least / len(pieces), high / len(pieces))
        gain = gain * jnp.repeat(jnp.exp(steps), extent[axis_at] // parts).reshape((-1,) + (1,) * (len(extent) - 1 - axis_at))
    return gain


def noise(key, dims, deviation, limit, cuts=(), kind=jnp.bfloat16):
    loudness = block_scale(key, dims, cuts, -0.22, 0.18) if cuts else 1.0
    array = jax.random.normal(key, dims, jnp.float32) * deviation * loudness
    return jnp.minimum(jnp.maximum(array, -limit), limit).astype(kind)


def setup_inputs(seed: int = 0) -> dict:
    arg_keys = jax.random.split(jax.random.key(seed), 8)
    inputs = draw_inputs(jax.random.fold_in(arg_keys[7], 71), 0)
    cotangent = noise(arg_keys[1], (Z, LAT, LON * C), 1.0, 4.0, ((1, 16), (2, 8)))
    norm_gain = jnp.clip(1.0 + 0.1 * jax.random.normal(arg_keys[2], (C,), jnp.float32), 0.5, 1.5)
    norm_shift = noise(arg_keys[3], (C,), 0.5, 2.0, (), jnp.float32)
    w_qkv = noise(arg_keys[4], (C, 3 * C), C ** -0.5, 0.4375)
    w_proj = noise(arg_keys[5], (C, C), C ** -0.5, 0.4375)
    bias_table = draw_bias_table(jax.random.fold_in(arg_keys[7], 71), 0)
    return dict(inputs=inputs, cotangent=cotangent, norm_gain=norm_gain, norm_shift=norm_shift, w_qkv=w_qkv, w_proj=w_proj, bias_table=bias_table)


def offset_table():
    offsets = np.arange(WLON)[:, None] - np.arange(WLON)[None, :] + WLON - 1
    return offsets.reshape(-1)

def expand_bias(table_row):
    head_count = table_row.shape[0]
    shaped = table_row.reshape(head_count, WZ, WLAT, WZ, WLAT, 2 * WLON - 1)
    picked = jnp.take(shaped, jnp.asarray(offset_table(), jnp.int32), axis=5)
    picked = picked.reshape(head_count, WZ, WLAT, WZ, WLAT, WLON, WLON)
    picked = picked.transpose(0, 1, 2, 5, 3, 4, 6)
    return picked.reshape(head_count, WIN, WIN)

def collapse_bias(grid_grad):
    head_count = grid_grad.shape[0]
    shaped = grid_grad.reshape(head_count, WZ, WLAT, WLON, WZ, WLAT, WLON)
    shaped = shaped.transpose(0, 1, 2, 4, 5, 3, 6).reshape(head_count, WZ * WLAT * WZ * WLAT, WLON * WLON)
    onehot = jnp.asarray(offset_table()[:, None] == np.arange(2 * WLON - 1)[None, :], jnp.float32)
    summed = jnp.einsum('hpe,ef->hpf', shaped, onehot, precision=lax.Precision.HIGHEST)
    return summed.reshape(head_count, -1)

def window_pass(band_tokens, band_cotan, key_valid, table_row, norm_gain, norm_shift, w_qkv, w_proj):
    levels, band_rows, width, channels = band_tokens.shape
    windows = width // WLON
    head_count = table_row.shape[0]
    head_dim = channels // head_count
    f32 = jnp.float32

    def to_windows(field_in):
        shaped = field_in.reshape(levels, band_rows, windows, WLON, channels).transpose(2, 0, 1, 3, 4)
        return shaped.reshape(windows * WIN, channels)

    def from_windows(field_in):
        shaped = field_in.reshape(windows, levels, band_rows, WLON, channels).transpose(1, 2, 0, 3, 4)
        return shaped.reshape(levels, band_rows, width, channels)
    tokens = to_windows(band_tokens).astype(f32)
    cotan_rows = to_windows(band_cotan)
    center = tokens - lax.optimization_barrier(jnp.mean(tokens, axis=1, keepdims=True))
    inv_std = lax.rsqrt(lax.optimization_barrier(jnp.mean(center * center, axis=1, keepdims=True)) + 1e-05)
    normed = center * inv_std
    hidden = (normed * norm_gain + norm_shift).astype(jnp.bfloat16)
    packed = jnp.dot(hidden, w_qkv, preferred_element_type=f32).astype(jnp.bfloat16)
    packed = packed.reshape(windows, WIN, 3, head_count, head_dim)
    queries, key_block, values = (packed[:, :, 0], packed[:, :, 1], packed[:, :, 2])
    score_scale = head_dim ** (-0.5)
    key_mask = jnp.broadcast_to(key_valid[None, :, None], (levels, band_rows, WLON)).reshape(-1)
    scores = jnp.einsum('wqhd,wkhd->whqk', queries.astype(f32), key_block.astype(f32), preferred_element_type=f32)
    scores = scores * score_scale + expand_bias(table_row)[None]
    scores = jnp.where(key_mask[None, None, None, :], scores, -1000000000.0)
    row_peak = lax.optimization_barrier(jnp.max(scores, axis=-1, keepdims=True))
    weights = jnp.exp(scores - row_peak)
    attn_probs = weights / lax.optimization_barrier(jnp.sum(weights, axis=-1, keepdims=True))
    probs_low = attn_probs.astype(jnp.bfloat16)
    mixed_out = jnp.einsum('whqk,wkhd->wqhd', probs_low.astype(f32), values.astype(f32), preferred_element_type=f32)
    mixed_out = mixed_out.astype(jnp.bfloat16).reshape(windows * WIN, channels)
    branch = jnp.dot(mixed_out, w_proj, preferred_element_type=f32).astype(jnp.bfloat16)
    grad_two = lax.dot_general(mixed_out, cotan_rows, (((0,), (0,)), ((), ())), preferred_element_type=f32)
    d_mixed = lax.dot_general(cotan_rows, w_proj, (((1,), (1,)), ((), ())), preferred_element_type=f32)
    d_mixed = d_mixed.astype(jnp.bfloat16).reshape(windows, WIN, head_count, head_dim)
    d_probs = jnp.einsum('wqhd,wkhd->whqk', d_mixed.astype(f32), values.astype(f32), preferred_element_type=f32)
    d_values = jnp.einsum('whqk,wqhd->wkhd', probs_low.astype(f32), d_mixed.astype(f32), preferred_element_type=f32)
    d_values = d_values.astype(jnp.bfloat16)
    d_scores = attn_probs * (d_probs - lax.optimization_barrier(jnp.sum(attn_probs * d_probs, axis=-1, keepdims=True)))
    table_grad = collapse_bias(lax.optimization_barrier(jnp.sum(d_scores, axis=0)))
    d_scaled = (d_scores * score_scale).astype(jnp.bfloat16)
    d_query = jnp.einsum('whqk,wkhd->wqhd', d_scaled.astype(f32), key_block.astype(f32), preferred_element_type=f32)
    d_keys = jnp.einsum('whqk,wqhd->wkhd', d_scaled.astype(f32), queries.astype(f32), preferred_element_type=f32)
    d_packed = jnp.stack([d_query.astype(jnp.bfloat16), d_keys.astype(jnp.bfloat16), d_values], axis=2)
    d_packed = d_packed.reshape(windows * WIN, 3 * channels)
    grad_one = lax.dot_general(hidden, d_packed, (((0,), (0,)), ((), ())), preferred_element_type=f32)
    d_hidden = lax.dot_general(d_packed, w_qkv, (((1,), (1,)), ((), ())), preferred_element_type=f32)
    d_normed = d_hidden * norm_gain
    d_tokens = inv_std * (d_normed - lax.optimization_barrier(jnp.mean(d_normed, axis=1, keepdims=True)) - normed * lax.optimization_barrier(jnp.mean(d_normed * normed, axis=1, keepdims=True)))
    return (from_windows(branch), from_windows(d_tokens.astype(jnp.bfloat16)), table_grad, grad_one, grad_two)

def reference(inputs, cotangent, norm_gain, norm_shift, w_qkv, w_proj, bias_table):
    levels, lat_rows, flat_cols = inputs.shape
    channels = norm_gain.shape[0]
    lon_cols = flat_cols // channels
    half_rows = WLAT // 2
    half_cols = WLON // 2
    band_total = (lat_rows + 2 * half_rows) // WLAT

    def to_frame(field_in):
        shaped = field_in.reshape(levels, lat_rows, lon_cols, channels)
        shaped = jnp.roll(shaped, -half_cols, axis=2)
        shaped = jnp.pad(shaped, ((0, 0), (half_rows, half_rows), (0, 0), (0, 0)))
        return shaped.reshape(levels, band_total, WLAT, lon_cols, channels).transpose(1, 0, 2, 3, 4)

    def from_frame(field_in):
        shaped = field_in.transpose(1, 0, 2, 3, 4).reshape(levels, band_total * WLAT, lon_cols, channels)
        shaped = shaped[:, half_rows:half_rows + lat_rows]
        return jnp.roll(shaped, half_cols, axis=2)
    band_in = to_frame(inputs)
    band_cot = to_frame(cotangent)
    band_ids = jnp.arange(band_total, dtype=jnp.int32)
    row_global = band_ids[:, None] * WLAT + jnp.arange(WLAT, dtype=jnp.int32)[None, :] - half_rows
    key_valid = (row_global >= 0) & (row_global < lat_rows)
    table_index = jnp.maximum(band_ids - 1, 0).astype(jnp.int32)

    def band_step(totals, band_item):
        band_tokens, band_cotan, valid_rows, band_index = band_item
        table_row = lax.dynamic_index_in_dim(bias_table, band_index, 0, keepdims=False)
        branch, d_branch, table_grad, grad_one, grad_two = window_pass(band_tokens, band_cotan, valid_rows, table_row, norm_gain, norm_shift, w_qkv, w_proj)
        old_row = lax.dynamic_index_in_dim(totals[2], band_index, 0, keepdims=False)
        table_sum = lax.dynamic_update_index_in_dim(totals[2], old_row + table_grad, band_index, 0)
        return ((totals[0] + grad_one, totals[1] + grad_two, table_sum), (branch, d_branch))
    start = (jnp.zeros((channels, 3 * channels), jnp.float32), jnp.zeros((channels, channels), jnp.float32), jnp.zeros(bias_table.shape, jnp.float32))
    (raw_qkv, raw_proj, table_total), (branches, d_branches) = lax.scan(band_step, start, (band_in, band_cot, key_valid, table_index))
    branch_grid = from_frame(branches).reshape(levels, lat_rows, flat_cols)
    d_grid = from_frame(d_branches).reshape(levels, lat_rows, flat_cols)
    block_out = (inputs.astype(jnp.float32) + branch_grid.astype(jnp.float32)).astype(jnp.bfloat16)
    grad_in = (cotangent.astype(jnp.float32) + d_grid.astype(jnp.float32)).astype(jnp.bfloat16)
    weight_rms = jnp.sqrt((jnp.sum(raw_qkv * raw_qkv) + jnp.sum(raw_proj * raw_proj)) / (raw_qkv.size + raw_proj.size) + 1e-06)
    table_rms = jnp.sqrt(jnp.mean(table_total * table_total) + 1e-06)
    return (block_out, grad_in, raw_qkv / weight_rms, raw_proj / weight_rms, table_total / table_rms)
```

```python
import functools
import math

import jax
import jax.numpy as jnp
import numpy as np
from jax import lax
from jax.experimental import pallas as pl
from jax.experimental.pallas import tpu as pltpu
from jax.sharding import PartitionSpec as P

C = 192
HEADS = 6
HD = 32
WLON = 12
WIN = 144
HALF = 72
SPAN = 23
ROWLEN = 12 * SPAN
ROWPAD = 384
COLS = 96
HALO = 6 * C
WLANES = WLON * C
OWN = COLS * C
FRAME = OWN + HALO
FROWS = 24
QUART = OWN // 4
WPB = 8
POS = 3312
EPS = 1e-5
SCALE = HD**-0.5
LOG2E = math.log2(math.e)
F32 = jnp.float32
BF16 = jnp.bfloat16


def nn(a, b):
    return lax.dot_general(a, b, (((1,), (0,)), ((), ())), preferred_element_type=F32)


def nt(a, b):
    return lax.dot_general(a, b, (((1,), (1,)), ((), ())), preferred_element_type=F32)


def tn(a, b):
    return lax.dot_general(a, b, (((0,), (0,)), ((), ())), preferred_element_type=F32)


def pick_matrix():
    out = np.zeros((WIN, ROWPAD), np.float32)
    for pk in range(6):
        for zk in range(2):
            for lk in range(WLON):
                out[(pk * 2 + zk) * WLON + lk, (zk * 6 + pk) * SPAN + 11 - lk] = 1.0
    return out


def frame_in(own, halo_lat, halo_east, halo_corner, which, frame):
    def chunk(k, _):
        base = pl.multiple_of(k * HALO, HALO)
        for z in range(2):
            frame[z, 0:12, pl.ds(base, HALO)] = own[z, :, pl.ds(base, HALO)].astype(F32)
        return 0

    lax.fori_loop(0, OWN // HALO, chunk, 0)

    def strip(k, _):
        base = pl.multiple_of(k * HALO, HALO)
        rows = halo_lat[:, pl.ds(base, HALO)].astype(F32)
        for q in range(4):
            for z in range(2):
                r = q * 12 + (which * 2 + z) * 3
                frame[z, 12:15, pl.ds(pl.multiple_of(q * QUART + base, HALO), HALO)] = rows[r : r + 3]
        return 0

    lax.fori_loop(0, QUART // HALO, strip, 0)
    east = halo_east[...].astype(F32)
    corner = halo_corner[...].astype(F32)
    for z in range(2):
        r = (which * 2 + z) * 12
        frame[z, 0:12, OWN:FRAME] = east[r : r + 12]
        r = (which * 2 + z) * 3
        frame[z, 12:15, OWN:FRAME] = corner[r : r + 3]


def frame_out(frame, own, ret_lat, ret_east, ret_corner, which):
    def chunk(k, _):
        base = pl.multiple_of(k * HALO, HALO)
        for z in range(2):
            own[z, :, pl.ds(base, HALO)] = frame[z, 0:12, pl.ds(base, HALO)].astype(BF16)
        return 0

    lax.fori_loop(0, OWN // HALO, chunk, 0)


def strips_out(frames, ret_lat, ret_east, ret_corner):
    def strip(k, _):
        base = pl.multiple_of(k * HALO, HALO)
        pieces = []
        for q in range(4):
            for frame in frames:
                for z in range(2):
                    pieces.append(
                        frame[z, 12:15, pl.ds(pl.multiple_of(q * QUART + base, HALO), HALO)]
                    )
        ret_lat[:, pl.ds(base, HALO)] = jnp.concatenate(pieces, axis=0).astype(BF16)
        return 0

    lax.fori_loop(0, QUART // HALO, strip, 0)
    pieces = [frame[z, 0:12, OWN:FRAME] for frame in frames for z in range(2)]
    ret_east[...] = jnp.concatenate(pieces, axis=0).astype(BF16)
    pieces = [frame[z, 12:15, OWN:FRAME] for frame in frames for z in range(2)]
    pieces.append(jnp.zeros((4, HALO), F32))
    ret_corner[...] = jnp.concatenate(pieces, axis=0).astype(BF16)


def windows_in(frame, rows, count, tokens, first):
    def window(w, _):
        base = HALO + w * WLANES
        for z in range(2):
            for m in range(6):
                at = pl.multiple_of(base + m * 2 * C, 128)
                slab = frame[z, rows : rows + 8, pl.ds(at, 2 * C)]
                odd = pltpu.roll(slab[:, 128:384], 192, 1)
                for t in range(2):
                    lanes = slice(t * 128, t * 128 + 128)
                    slots = pl.ds(z * 12 + 2 * m, count, stride=24)
                    tokens[first + w, t, slots, :] = slab[:count, lanes]
                    slots = pl.ds(z * 12 + 2 * m + 1, count, stride=24)
                    tokens[first + w, t, slots, :] = odd[:count, lanes]
        return 0

    lax.fori_loop(0, WPB, window, 0)


def windows_out(frame, rows, count, tokens, first):
    lane = lax.broadcasted_iota(jnp.int32, (8, 128), 1)

    def window(w, _):
        base = HALO + w * WLANES
        for z in range(2):
            for m in range(6):
                at = pl.multiple_of(base + m * 2 * C, 128)
                slots = pl.ds(z * 12 + 2 * m, count, stride=24)
                even = [tokens[first + w, t, slots, :] for t in range(2)]
                slots = pl.ds(z * 12 + 2 * m + 1, count, stride=24)
                odd = [tokens[first + w, t, slots, :] for t in range(2)]
                odd.append(jnp.zeros((8 - count, 256), F32))
                odd = jnp.concatenate([jnp.concatenate(odd[:2], axis=1), odd[2]], axis=0)
                odd = pltpu.roll(odd, 64, 1)
                mid = jnp.where(lane[:count] < 64, even[1], odd[:count, :128])
                frame[z, rows : rows + count, pl.ds(at, 128)] = even[0]
                frame[z, rows : rows + count, pl.ds(at + 128, 128)] = mid
                frame[z, rows : rows + count, pl.ds(at + 256, 128)] = odd[:count, 128:]
        return 0

    lax.fori_loop(0, WPB, window, 0)


def bias_in(table, pick, rows_scratch, shifted, bias):
    for zq in range(2):
        for pq in range(6):
            at = (zq * 6 + pq) * ROWLEN
            part = table[:, at : at + ROWLEN]
            rows_scratch[pq * 2 + zq, 0:12, 0:ROWLEN] = part
    for bh in range(12):
        rows = rows_scratch[:, bh, :]
        rows = jnp.concatenate([rows, jnp.zeros((4, ROWPAD), F32)], axis=0)
        for lq in range(WLON):
            moved = pltpu.roll(rows, (ROWPAD - lq) % ROWPAD, 1) if lq else rows
            for t in range(3):
                shifted[t, pl.ds(lq, 12, stride=12), :] = moved[:12, t * 128 : t * 128 + 128]
        full = jnp.concatenate([shifted[t] for t in range(3)], axis=1)
        high = full.astype(BF16)
        rest = full - high.astype(F32)
        mid = rest.astype(BF16)
        low = (rest - mid.astype(F32)).astype(BF16)
        total = nt(pick, high) + nt(pick, mid) + nt(pick, low)
        bias[bh // HEADS, bh % HEADS] = total * LOG2E


def bias_out(grads, pick, shifted, out):
    for bh in range(12):
        full = grads[bh // HEADS, bh % HEADS].T
        high = full.astype(BF16)
        low = (full - high.astype(F32)).astype(BF16)
        full = nn(high, pick) + nn(low, pick)
        for t in range(3):
            shifted[t] = full[:, t * 128 : t * 128 + 128]
        total = jnp.zeros((16, ROWPAD), F32)
        for lq in range(WLON):
            rows = [shifted[t, pl.ds(lq, 12, stride=12), :] for t in range(3)]
            rows = jnp.concatenate(rows, axis=1)
            rows = jnp.concatenate([rows, jnp.zeros((4, ROWPAD), F32)], axis=0)
            total = total + (pltpu.roll(rows, lq, 1) if lq else rows)
        out[bh] = total


def attend(n, x_ref, g_ref, at, bias, dbias, band, gain, shift, wqkv, wqkv_t, wproj, wproj_t, eye, raw_q, raw_p):
    x = jnp.concatenate([x_ref[at, 0], x_ref[at, 1]], axis=1)[:, :C]
    g = jnp.concatenate([g_ref[at, 0], g_ref[at, 1]], axis=1)[:, :C]
    gb = g.astype(BF16)
    center = x - jnp.mean(x, axis=1, keepdims=True)
    rstd = lax.rsqrt(jnp.mean(center * center, axis=1, keepdims=True) + EPS)
    xn = center * rstd
    h = (xn * gain + shift).astype(BF16)
    qkv = nn(h, wqkv[...]).astype(BF16)
    kv_t = nt(wqkv_t[C:], h).astype(BF16)
    h_t = nt(eye[...], h).astype(BF16)
    do = nn(gb, wproj_t[...]).astype(BF16)
    o_t, dq_t, dks, dvs = [], [], [], []
    for i in range(HEADS):
        at_h = i * HD
        q = qkv[:, at_h : at_h + HD]
        k = qkv[:, C + at_h : C + at_h + HD]
        v = qkv[:, 2 * C + at_h : 2 * C + at_h + HD]
        k_t = kv_t[at_h : at_h + HD]
        v_t = kv_t[C + at_h : C + at_h + HD]
        do_h = do[:, at_h : at_h + HD]
        s = nt(k, q) * (SCALE * LOG2E) + bias[band, i]
        e = jnp.exp2(s - jnp.max(s, axis=0, keepdims=True))
        p = e * (1.0 / jnp.sum(e, axis=0, keepdims=True))
        pb = p.astype(BF16)
        o_t.append(nn(v_t, pb))
        dp = nt(v, do_h)
        dvs.append(nn(pb, do_h))
        ds = p * (dp - jnp.sum(p * dp, axis=0, keepdims=True))
        dbias[band, i] += ds
        dsb = (ds * SCALE).astype(BF16)
        dks.append(nn(dsb, q))
        dq_t.append(nn(k_t, dsb))
    o_t = jnp.concatenate(o_t, axis=0).astype(BF16)
    dq_t = jnp.concatenate(dq_t, axis=0).astype(BF16)
    o = nt(eye[:n, :n], o_t).astype(BF16)
    dq = nt(eye[:n, :n], dq_t).astype(BF16)
    a = nn(o, wproj[...]).astype(BF16)
    raw_p[...] += nn(o_t, gb)
    dk = jnp.concatenate(dks, axis=1).astype(BF16)
    dv = jnp.concatenate(dvs, axis=1).astype(BF16)
    raw_q[:, 0:C] += nn(h_t, dq)
    raw_q[:, C : 2 * C] += nn(h_t, dk)
    raw_q[:, 2 * C :] += nn(h_t, dv)
    dh = nn(dq, wqkv_t[0:C]) + nn(dk, wqkv_t[C : 2 * C]) + nn(dv, wqkv_t[2 * C :])
    dxn = dh * gain
    m1 = jnp.mean(dxn, axis=1, keepdims=True)
    m2 = jnp.mean(dxn * xn, axis=1, keepdims=True)
    dx = (rstd * (dxn - m1 - xn * m2)).astype(BF16)
    x = x + a.astype(F32)
    g = g + dx.astype(F32)
    x_ref[at, 0] = x[:, :128]
    x_ref[at, 1, :, 0:64] = x[:, 128:]
    g_ref[at, 0] = g[:, :128]
    g_ref[at, 1, :, 0:64] = g[:, 128:]


def window_kernel(
    last,
    lat_ref,
    x_own,
    g_own,
    halo_lat,
    halo_east,
    halo_corner,
    gain_ref,
    shift_ref,
    wqkv,
    wqkv_t,
    wproj,
    wproj_t,
    eye,
    pick,
    table,
    x_out,
    g_out,
    ret_lat,
    ret_east,
    ret_corner,
    raw_q,
    raw_p,
    dtable,
    fx,
    fg,
    xw,
    gw,
    xh,
    gh,
    bias,
    dbias,
    bias_h,
    dbias_h,
    rows_scratch,
    shifted,
):
    lat = lat_ref[0]
    first = lat == 0
    final = lat == last
    frame_in(x_own, halo_lat, halo_east, halo_corner, 0, fx)
    frame_in(g_own, halo_lat, halo_east, halo_corner, 1, fg)
    rows_scratch[...] = jnp.zeros_like(rows_scratch)
    bias_in(table, pick[...], rows_scratch, shifted, bias)
    dbias[...] = jnp.zeros_like(dbias)
    raw_q[...] = jnp.zeros_like(raw_q)
    raw_p[...] = jnp.zeros_like(raw_p)
    for band in range(2):
        windows_in(fx, 3 + 6 * band, 6, xw, band * WPB)
        windows_in(fg, 3 + 6 * band, 6, gw, band * WPB)
    gain = gain_ref[...]
    shift = shift_ref[...]
    rest = (gain, shift, wqkv, wqkv_t, wproj, wproj_t, eye, raw_q, raw_p)

    def full(u, _):
        attend(WIN, xw, gw, u, bias, dbias, u // WPB, *rest)
        return 0

    lax.fori_loop(0, jnp.where(final, WPB, 2 * WPB), full, 0)

    def halves(rows, band, lo):
        windows_in(fx, rows, 3, xh, 0)
        windows_in(fg, rows, 3, gh, 0)
        dbias_h[...] = jnp.zeros_like(dbias_h)
        for i in range(HEADS):
            bias_h[0, i] = bias[band, i][lo : lo + HALF, lo : lo + HALF]

        def half(u, _):
            attend(HALF, xh, gh, u, bias_h, dbias_h, 0, *rest)
            return 0

        lax.fori_loop(0, WPB, half, 0)
        zero = jnp.zeros((HALF, HALF), F32)
        for i in range(HEADS):
            part = dbias_h[0, i]
            part = jnp.concatenate([zero, part] if lo else [part, zero], axis=1)
            dbias[band, i, lo : lo + HALF, :] += part

    for band in range(2):
        windows_out(fx, 3 + 6 * band, 6, xw, band * WPB)
        windows_out(fg, 3 + 6 * band, 6, gw, band * WPB)

    @pl.when(first)
    def _():
        halves(0, 0, HALF)
        windows_out(fx, 0, 3, xh, 0)
        windows_out(fg, 0, 3, gh, 0)

    @pl.when(final)
    def _():
        halves(9, 1, 0)
        windows_out(fx, 9, 3, xh, 0)
        windows_out(fg, 9, 3, gh, 0)

    bias_out(dbias, pick[...], shifted, dtable)
    frame_out(fx, x_out, ret_lat, ret_east, ret_corner, 0)
    frame_out(fg, g_out, ret_lat, ret_east, ret_corner, 1)
    strips_out((fx, fg), ret_lat, ret_east, ret_corner)


def run_windows(last, lat, x_own, g_own, halos, gain, shift, wqkv, wproj, table):
    vmem = pl.BlockSpec(memory_space=pltpu.VMEM)
    shape = jax.ShapeDtypeStruct
    return pl.pallas_call(
        functools.partial(window_kernel, last),
        in_specs=[pl.BlockSpec(memory_space=pltpu.SMEM)] + [vmem] * 14,
        out_specs=[vmem] * 8,
        out_shape=[
            shape((2, 12, OWN), BF16),
            shape((2, 12, OWN), BF16),
            shape((48, QUART), BF16),
            shape((48, HALO), BF16),
            shape((16, HALO), BF16),
            shape((C, 3 * C), F32),
            shape((C, C), F32),
            shape((12, 16, ROWPAD), F32),
        ],
        scratch_shapes=[
            pltpu.VMEM((2, FROWS, FRAME), F32),
            pltpu.VMEM((2, FROWS, FRAME), F32),
            pltpu.VMEM((2 * WPB, 2, WIN, 128), F32),
            pltpu.VMEM((2 * WPB, 2, WIN, 128), F32),
            pltpu.VMEM((WPB, 2, HALF, 128), F32),
            pltpu.VMEM((WPB, 2, HALF, 128), F32),
            pltpu.VMEM((2, HEADS, WIN, WIN), F32),
            pltpu.VMEM((2, HEADS, WIN, WIN), F32),
            pltpu.VMEM((1, HEADS, HALF, HALF), F32),
            pltpu.VMEM((1, HEADS, HALF, HALF), F32),
            pltpu.VMEM((12, 16, ROWPAD), F32),
            pltpu.VMEM((3, WIN, 128), F32),
        ],
        compiler_params=pltpu.CompilerParams(vmem_limit_bytes=56 * 2**20),
        name="windows",
    )(
        lat.reshape(1),
        x_own,
        g_own,
        *halos,
        gain.reshape(1, C),
        shift.reshape(1, C),
        wqkv,
        wqkv.T,
        wproj,
        wproj.T,
        jnp.eye(C, dtype=BF16),
        jnp.asarray(pick_matrix(), BF16),
        table.reshape(2 * HEADS, POS),
    )


def on_device(inputs, cotangent, norm_gain, norm_shift, w_qkv, w_proj, bias_table):
    lat = lax.axis_index("lat")
    lats = lax.axis_size("lat")
    lons = lax.axis_size("lon")

    def north(v):
        return lax.ppermute(v, "lat", [(i + 1, i) for i in range(lats - 1)])

    def south(v):
        return lax.ppermute(v, "lat", [(i, i + 1) for i in range(lats - 1)])

    def along(v, by):
        return lax.ppermute(v, "lon", [(i, (i + by) % lons) for i in range(lons)])

    stacked = jnp.stack([inputs, cotangent])
    strip = stacked[:, :, :3].reshape(12, 4, QUART).transpose(1, 0, 2).reshape(48, QUART)
    halo_lat = north(strip)
    halo_east = along(stacked[:, :, :, :HALO].reshape(48, HALO), -1)
    corner = jnp.pad(strip[:12, :HALO], ((0, 4), (0, 0)))
    halo_corner = along(north(corner), -1)
    x_out, g_out, ret_lat, ret_east, ret_corner, raw_q, raw_p, dtable = run_windows(
        lats - 1,
        lat,
        inputs,
        cotangent,
        (halo_lat, halo_east, halo_corner),
        norm_gain,
        norm_shift,
        w_qkv,
        w_proj,
        bias_table,
    )
    got_lat = south(ret_lat).reshape(4, 2, 2, 3, QUART).transpose(1, 2, 3, 0, 4)
    got_lat = got_lat.reshape(2, 2, 3, OWN)
    got_east = along(ret_east, 1).reshape(2, 2, 12, HALO)
    got_corner = along(south(ret_corner), 1)[:12].reshape(2, 2, 3, HALO)
    own = jnp.stack([x_out, g_out])
    rows = jnp.where(lat == 0, own[:, :, :3], got_lat)
    corner = jnp.where(lat == 0, got_east[:, :, :3], got_corner)
    rows = jnp.concatenate([corner, rows[..., HALO:]], axis=3)
    below = jnp.concatenate([got_east[:, :, 3:], own[:, :, 3:, HALO:]], axis=3)
    own = jnp.concatenate([rows, below], axis=2)
    table = dtable[:, :12, :ROWLEN].reshape(2, HEADS, 6, 2, ROWLEN).transpose(0, 1, 3, 2, 4)
    table = lax.psum(table.reshape(2, HEADS, POS), "lon")
    raw_q, raw_p = lax.psum((raw_q, raw_p), ("lat", "lon"))
    squares = lax.psum(jnp.sum(table * table), "lat")
    rms = jnp.sqrt((jnp.sum(raw_q * raw_q) + jnp.sum(raw_p * raw_p)) / (4 * C * C) + 1e-6)
    table_rms = jnp.sqrt(squares / (table.size * lats) + 1e-6)
    return own[0], own[1], raw_q / rms, raw_p / rms, table / table_rms


def solution(mesh):
    return jax.shard_map(
        on_device,
        mesh=mesh,
        in_specs=(
            P(None, "lat", "lon"),
            P(None, "lat", "lon"),
            P(),
            P(),
            P(),
            P(),
            P("lat", None, None),
        ),
        out_specs=(P(None, "lat", "lon"), P(None, "lat", "lon"), P(), P(), P("lat", None, None)),
        check_vma=False,
    )
```

```python
import functools
import math

import jax
import jax.numpy as jnp
import numpy as np
from jax import lax
from jax.experimental import pallas as pl
from jax.experimental.pallas import tpu as pltpu
from jax.sharding import PartitionSpec as P

C = 192
HEADS = 6
HD = 32
WLON = 12
WIN = 144
HALF = 72
SPAN = 23
ROWLEN = 12 * SPAN
ROWPAD = 384
COLS = 96
HALO = 6 * C
WLANES = WLON * C
OWN = COLS * C
FRAME = OWN + HALO
FROWS = 24
QUART = OWN // 4
WPB = 8
POS = 3312
TABLE = 4096
WCHUNK = 12 * 768 // 8
TCHUNK = TABLE // 8
CHUNK = WCHUNK + TCHUNK
TILES = WCHUNK // 128
MESH = pl.DeviceIdType.MESH
EPS = 1e-5
SCALE = HD**-0.5
LOG2E = math.log2(math.e)
F32 = jnp.float32
BF16 = jnp.bfloat16


def nn(a, b):
    return lax.dot_general(a, b, (((1,), (0,)), ((), ())), preferred_element_type=F32)


def nt(a, b):
    return lax.dot_general(a, b, (((1,), (1,)), ((), ())), preferred_element_type=F32)


def tn(a, b):
    return lax.dot_general(a, b, (((0,), (0,)), ((), ())), preferred_element_type=F32)


def pick_matrix():
    out = np.zeros((WIN, ROWPAD), np.float32)
    for pk in range(6):
        for zk in range(2):
            for lk in range(WLON):
                out[(pk * 2 + zk) * WLON + lk, (zk * 6 + pk) * SPAN + 11 - lk] = 1.0
    return out


def frame_in(own, halo_lat, halo_east, halo_corner, which, frame):
    def chunk(k, _):
        base = pl.multiple_of(k * HALO, HALO)
        for z in range(2):
            frame[z, 0:12, pl.ds(base, HALO)] = own[z, :, pl.ds(base, HALO)].astype(F32)
        return 0

    lax.fori_loop(0, OWN // HALO, chunk, 0)

    def strip(k, _):
        base = pl.multiple_of(k * HALO, HALO)
        rows = halo_lat[:, pl.ds(base, HALO)].astype(F32)
        for q in range(4):
            for z in range(2):
                r = q * 12 + (which * 2 + z) * 3
                frame[z, 12:15, pl.ds(pl.multiple_of(q * QUART + base, HALO), HALO)] = rows[r : r + 3]
        return 0

    lax.fori_loop(0, QUART // HALO, strip, 0)
    east = halo_east[...].astype(F32)
    corner = halo_corner[...].astype(F32)
    for z in range(2):
        r = (which * 2 + z) * 12
        frame[z, 0:12, OWN:FRAME] = east[r : r + 12]
        r = (which * 2 + z) * 3
        frame[z, 12:15, OWN:FRAME] = corner[r : r + 3]


def frame_out(frame, own, ret_lat, ret_east, ret_corner, which):
    def chunk(k, _):
        base = pl.multiple_of(k * HALO, HALO)
        for z in range(2):
            own[z, :, pl.ds(base, HALO)] = frame[z, 0:12, pl.ds(base, HALO)].astype(BF16)
        return 0

    lax.fori_loop(0, OWN // HALO, chunk, 0)


def strips_out(frames, ret_lat, ret_east, ret_corner):
    def strip(k, _):
        base = pl.multiple_of(k * HALO, HALO)
        pieces = []
        for q in range(4):
            for frame in frames:
                for z in range(2):
                    pieces.append(
                        frame[z, 12:15, pl.ds(pl.multiple_of(q * QUART + base, HALO), HALO)]
                    )
        ret_lat[:, pl.ds(base, HALO)] = jnp.concatenate(pieces, axis=0).astype(BF16)
        return 0

    lax.fori_loop(0, QUART // HALO, strip, 0)
    pieces = [frame[z, 0:12, OWN:FRAME] for frame in frames for z in range(2)]
    ret_east[...] = jnp.concatenate(pieces, axis=0).astype(BF16)
    pieces = [frame[z, 12:15, OWN:FRAME] for frame in frames for z in range(2)]
    pieces.append(jnp.zeros((4, HALO), F32))
    ret_corner[...] = jnp.concatenate(pieces, axis=0).astype(BF16)


def windows_in(frame, rows, count, tokens, first):
    def window(w, _):
        base = HALO + w * WLANES
        for z in range(2):
            for m in range(6):
                at = pl.multiple_of(base + m * 2 * C, 128)
                slab = frame[z, rows : rows + 8, pl.ds(at, 2 * C)]
                odd = pltpu.roll(slab[:, 128:384], 192, 1)
                for t in range(2):
                    lanes = slice(t * 128, t * 128 + 128)
                    slots = pl.ds(z * 12 + 2 * m, count, stride=24)
                    tokens[first + w, t, slots, :] = slab[:count, lanes]
                    slots = pl.ds(z * 12 + 2 * m + 1, count, stride=24)
                    tokens[first + w, t, slots, :] = odd[:count, lanes]
        return 0

    lax.fori_loop(0, WPB, window, 0)


def windows_out(frame, rows, count, tokens, first):
    lane = lax.broadcasted_iota(jnp.int32, (8, 128), 1)

    def window(w, _):
        base = HALO + w * WLANES
        for z in range(2):
            for m in range(6):
                at = pl.multiple_of(base + m * 2 * C, 128)
                slots = pl.ds(z * 12 + 2 * m, count, stride=24)
                even = [tokens[first + w, t, slots, :] for t in range(2)]
                slots = pl.ds(z * 12 + 2 * m + 1, count, stride=24)
                odd = [tokens[first + w, t, slots, :] for t in range(2)]
                odd.append(jnp.zeros((8 - count, 256), F32))
                odd = jnp.concatenate([jnp.concatenate(odd[:2], axis=1), odd[2]], axis=0)
                odd = pltpu.roll(odd, 64, 1)
                mid = jnp.where(lane[:count] < 64, even[1], odd[:count, :128])
                frame[z, rows : rows + count, pl.ds(at, 128)] = even[0]
                frame[z, rows : rows + count, pl.ds(at + 128, 128)] = mid
                frame[z, rows : rows + count, pl.ds(at + 256, 128)] = odd[:count, 128:]
        return 0

    lax.fori_loop(0, WPB, window, 0)


def bias_in(table, pick, rows_scratch, shifted, bias):
    for zq in range(2):
        for pq in range(6):
            at = (zq * 6 + pq) * ROWLEN
            part = table[:, at : at + ROWLEN]
            rows_scratch[pq * 2 + zq, 0:12, 0:ROWLEN] = part
    for bh in range(12):
        rows = rows_scratch[:, bh, :]
        rows = jnp.concatenate([rows, jnp.zeros((4, ROWPAD), F32)], axis=0)
        for lq in range(WLON):
            moved = pltpu.roll(rows, (ROWPAD - lq) % ROWPAD, 1) if lq else rows
            for t in range(3):
                shifted[t, pl.ds(lq, 12, stride=12), :] = moved[:12, t * 128 : t * 128 + 128]
        full = jnp.concatenate([shifted[t] for t in range(3)], axis=1)
        high = full.astype(BF16)
        rest = full - high.astype(F32)
        mid = rest.astype(BF16)
        low = (rest - mid.astype(F32)).astype(BF16)
        total = nt(pick, high) + nt(pick, mid) + nt(pick, low)
        bias[bh // HEADS, bh % HEADS] = total * LOG2E


def bias_out(grads, pick, shifted, rows_scratch, out):
    rows_scratch[...] = jnp.zeros_like(rows_scratch)
    for bh in range(12):
        full = grads[bh // HEADS, bh % HEADS].T
        high = full.astype(BF16)
        low = (full - high.astype(F32)).astype(BF16)
        full = nn(high, pick) + nn(low, pick)
        for t in range(3):
            shifted[t] = full[:, t * 128 : t * 128 + 128]
        total = jnp.zeros((16, ROWPAD), F32)
        for lq in range(WLON):
            rows = [shifted[t, pl.ds(lq, 12, stride=12), :] for t in range(3)]
            rows = jnp.concatenate(rows, axis=1)
            rows = jnp.concatenate([rows, jnp.zeros((4, ROWPAD), F32)], axis=0)
            total = total + (pltpu.roll(rows, lq, 1) if lq else rows)
        rows_scratch[:, bh, :] = total[:12]
    parts = [rows_scratch[pq * 2 + zq][:, :ROWLEN] for zq in range(2) for pq in range(6)]
    parts.append(jnp.zeros((16, TABLE - POS), F32))
    out[...] = jnp.concatenate(parts, axis=1)


def attend(n, x_ref, g_ref, at, bias, dbias, band, gain, shift, wqkv, wqkv_t, wproj, wproj_t, eye, raw_q, raw_p):
    x = jnp.concatenate([x_ref[at, 0], x_ref[at, 1]], axis=1)[:, :C]
    g = jnp.concatenate([g_ref[at, 0], g_ref[at, 1]], axis=1)[:, :C]
    gb = g.astype(BF16)
    center = x - jnp.mean(x, axis=1, keepdims=True)
    rstd = lax.rsqrt(jnp.mean(center * center, axis=1, keepdims=True) + EPS)
    xn = center * rstd
    h = (xn * gain + shift).astype(BF16)
    qkv = nn(h, wqkv[...]).astype(BF16)
    kv_t = nt(wqkv_t[C:], h).astype(BF16)
    h_t = nt(eye[...], h).astype(BF16)
    do = nn(gb, wproj_t[...]).astype(BF16)
    o_t, dq_t, dks, dvs = [], [], [], []
    for i in range(HEADS):
        at_h = i * HD
        q = qkv[:, at_h : at_h + HD]
        k = qkv[:, C + at_h : C + at_h + HD]
        v = qkv[:, 2 * C + at_h : 2 * C + at_h + HD]
        k_t = kv_t[at_h : at_h + HD]
        v_t = kv_t[C + at_h : C + at_h + HD]
        do_h = do[:, at_h : at_h + HD]
        s = nt(k, q) * (SCALE * LOG2E) + bias[band, i]
        e = jnp.exp2(s - jnp.max(s, axis=0, keepdims=True))
        p = e * (1.0 / jnp.sum(e, axis=0, keepdims=True))
        pb = p.astype(BF16)
        o_t.append(nn(v_t, pb))
        dp = nt(v, do_h)
        dvs.append(nn(pb, do_h))
        ds = p * (dp - jnp.sum(p * dp, axis=0, keepdims=True))
        dbias[band, i] += ds
        dsb = (ds * SCALE).astype(BF16)
        dks.append(nn(dsb, q))
        dq_t.append(nn(k_t, dsb))
    o_t = jnp.concatenate(o_t, axis=0).astype(BF16)
    dq_t = jnp.concatenate(dq_t, axis=0).astype(BF16)
    o = nt(eye[:n, :n], o_t).astype(BF16)
    dq = nt(eye[:n, :n], dq_t).astype(BF16)
    a = nn(o, wproj[...]).astype(BF16)
    raw_p[...] += nn(o_t, gb)
    dk = jnp.concatenate(dks, axis=1).astype(BF16)
    dv = jnp.concatenate(dvs, axis=1).astype(BF16)
    raw_q[:, 0:C] += nn(h_t, dq)
    raw_q[:, C : 2 * C] += nn(h_t, dk)
    raw_q[:, 2 * C :] += nn(h_t, dv)
    dh = nn(dq, wqkv_t[0:C]) + nn(dk, wqkv_t[C : 2 * C]) + nn(dv, wqkv_t[2 * C :])
    dxn = dh * gain
    m1 = jnp.mean(dxn, axis=1, keepdims=True)
    m2 = jnp.mean(dxn * xn, axis=1, keepdims=True)
    dx = (rstd * (dxn - m1 - xn * m2)).astype(BF16)
    x = x + a.astype(F32)
    g = g + dx.astype(F32)
    x_ref[at, 0] = x[:, :128]
    x_ref[at, 1, :, 0:64] = x[:, 128:]
    g_ref[at, 0] = g[:, :128]
    g_ref[at, 1, :, 0:64] = g[:, 128:]


def window_kernel(
    last,
    lat_ref,
    x_own,
    g_own,
    halo_lat,
    halo_east,
    halo_corner,
    gain_ref,
    shift_ref,
    wqkv,
    wqkv_t,
    wproj,
    wproj_t,
    eye,
    pick,
    table,
    x_out,
    g_out,
    ret_lat,
    ret_east,
    ret_corner,
    raw_q,
    raw_p,
    dtable,
    fx,
    fg,
    xw,
    gw,
    xh,
    gh,
    bias,
    dbias,
    bias_h,
    dbias_h,
    rows_scratch,
    shifted,
):
    lat = lat_ref[0]
    first = lat == 0
    final = lat == last
    frame_in(x_own, halo_lat, halo_east, halo_corner, 0, fx)
    frame_in(g_own, halo_lat, halo_east, halo_corner, 1, fg)
    rows_scratch[...] = jnp.zeros_like(rows_scratch)
    bias_in(table, pick[...], rows_scratch, shifted, bias)
    dbias[...] = jnp.zeros_like(dbias)
    raw_q[...] = jnp.zeros_like(raw_q)
    raw_p[...] = jnp.zeros_like(raw_p)
    for band in range(2):
        windows_in(fx, 3 + 6 * band, 6, xw, band * WPB)
        windows_in(fg, 3 + 6 * band, 6, gw, band * WPB)
    gain = gain_ref[...]
    shift = shift_ref[...]
    rest = (gain, shift, wqkv, wqkv_t, wproj, wproj_t, eye, raw_q, raw_p)

    def full(u, _):
        attend(WIN, xw, gw, u, bias, dbias, u // WPB, *rest)
        return 0

    lax.fori_loop(0, jnp.where(final, WPB, 2 * WPB), full, 0)

    def halves(rows, band, lo):
        windows_in(fx, rows, 3, xh, 0)
        windows_in(fg, rows, 3, gh, 0)
        dbias_h[...] = jnp.zeros_like(dbias_h)
        for i in range(HEADS):
            bias_h[0, i] = bias[band, i][lo : lo + HALF, lo : lo + HALF]

        def half(u, _):
            attend(HALF, xh, gh, u, bias_h, dbias_h, 0, *rest)
            return 0

        lax.fori_loop(0, WPB, half, 0)
        zero = jnp.zeros((HALF, HALF), F32)
        for i in range(HEADS):
            part = dbias_h[0, i]
            part = jnp.concatenate([zero, part] if lo else [part, zero], axis=1)
            dbias[band, i, lo : lo + HALF, :] += part

    for band in range(2):
        windows_out(fx, 3 + 6 * band, 6, xw, band * WPB)
        windows_out(fg, 3 + 6 * band, 6, gw, band * WPB)

    @pl.when(first)
    def _():
        halves(0, 0, HALF)
        windows_out(fx, 0, 3, xh, 0)
        windows_out(fg, 0, 3, gh, 0)

    @pl.when(final)
    def _():
        halves(9, 1, 0)
        windows_out(fx, 9, 3, xh, 0)
        windows_out(fg, 9, 3, gh, 0)

    bias_out(dbias, pick[...], shifted, rows_scratch, dtable)
    frame_out(fx, x_out, ret_lat, ret_east, ret_corner, 0)
    frame_out(fg, g_out, ret_lat, ret_east, ret_corner, 1)
    strips_out((fx, fg), ret_lat, ret_east, ret_corner)


def run_windows(last, lat, x_own, g_own, halos, gain, shift, wqkv, wproj, table):
    vmem = pl.BlockSpec(memory_space=pltpu.VMEM)
    shape = jax.ShapeDtypeStruct
    return pl.pallas_call(
        functools.partial(window_kernel, last),
        in_specs=[pl.BlockSpec(memory_space=pltpu.SMEM)] + [vmem] * 14,
        out_specs=[vmem] * 8,
        out_shape=[
            shape((2, 12, OWN), BF16),
            shape((2, 12, OWN), BF16),
            shape((48, QUART), BF16),
            shape((48, HALO), BF16),
            shape((16, HALO), BF16),
            shape((C, 3 * C), F32),
            shape((C, C), F32),
            shape((16, TABLE), F32),
        ],
        scratch_shapes=[
            pltpu.VMEM((2, FROWS, FRAME), F32),
            pltpu.VMEM((2, FROWS, FRAME), F32),
            pltpu.VMEM((2 * WPB, 2, WIN, 128), F32),
            pltpu.VMEM((2 * WPB, 2, WIN, 128), F32),
            pltpu.VMEM((WPB, 2, HALF, 128), F32),
            pltpu.VMEM((WPB, 2, HALF, 128), F32),
            pltpu.VMEM((2, HEADS, WIN, WIN), F32),
            pltpu.VMEM((2, HEADS, WIN, WIN), F32),
            pltpu.VMEM((1, HEADS, HALF, HALF), F32),
            pltpu.VMEM((1, HEADS, HALF, HALF), F32),
            pltpu.VMEM((12, 16, ROWPAD), F32),
            pltpu.VMEM((3, WIN, 128), F32),
        ],
        compiler_params=pltpu.CompilerParams(vmem_limit_bytes=56 * 2**20),
        name="windows",
    )(
        lat.reshape(1),
        x_own,
        g_own,
        *halos,
        gain.reshape(1, C),
        shift.reshape(1, C),
        wqkv,
        wqkv.T,
        wproj,
        wproj.T,
        jnp.eye(C, dtype=BF16),
        jnp.asarray(pick_matrix(), BF16),
        table.reshape(2 * HEADS, POS),
    )


def copy_to(src, dst, send, recv, lat, lon):
    return pltpu.make_async_remote_copy(
        src_ref=src,
        dst_ref=dst,
        send_sem=send,
        recv_sem=recv,
        device_id=(lat, lon),
        device_id_type=MESH,
    )


def greet(lat, lon):
    barrier = pltpu.get_barrier_semaphore()
    pl.semaphore_signal(barrier, inc=1, device_id=(lat, lon), device_id_type=MESH)


def halo_kernel(
    lats, lons, x, g, halo_lat, halo_east, halo_corner, lat_buf, east_buf, corner_buf, send, recv
):
    lat = lax.axis_index("lat")
    lon = lax.axis_index("lon")
    west = lax.rem(lon + lons - 1, lons)
    east = lax.rem(lon + 1, lons)
    barrier = pltpu.get_barrier_semaphore()
    greet(lat, east)

    @pl.when(lat < lats - 1)
    def _():
        greet(lat + 1, lon)
        greet(lat + 1, east)

    def strip(k, _):
        base = pl.multiple_of(k * HALO, HALO)
        pieces = []
        for q in range(4):
            for ref in (x, g):
                for z in range(2):
                    lanes = pl.ds(pl.multiple_of(q * QUART + base, HALO), HALO)
                    pieces.append(ref[z, :, lanes].astype(F32)[:3])
        lat_buf[:, pl.ds(base, HALO)] = jnp.concatenate(pieces, axis=0).astype(BF16)
        return 0

    lax.fori_loop(0, QUART // HALO, strip, 0)
    sides = [ref[z, :, 0:HALO].astype(F32) for ref in (x, g) for z in range(2)]
    east_buf[...] = jnp.concatenate(sides, axis=0).astype(BF16)
    corners = [side[:3] for side in sides] + [jnp.zeros((4, HALO), F32)]
    corner_buf[...] = jnp.concatenate(corners, axis=0).astype(BF16)

    pl.semaphore_wait(barrier, jnp.where(lat > 0, 3, 1))
    up = copy_to(lat_buf, halo_lat, send.at[0], recv.at[0], lat - 1, lon)
    side = copy_to(east_buf, halo_east, send.at[1], recv.at[1], lat, west)
    diag = copy_to(corner_buf, halo_corner, send.at[2], recv.at[2], lat - 1, west)

    @pl.when(lat > 0)
    def _():
        up.start()
        diag.start()

    side.start()

    @pl.when(lat < lats - 1)
    def _():
        up.wait_recv()
        diag.wait_recv()

    @pl.when(lat == lats - 1)
    def _():
        halo_lat[...] = jnp.zeros_like(halo_lat)
        halo_corner[...] = jnp.zeros_like(halo_corner)

    side.wait_recv()
    side.wait_send()

    @pl.when(lat > 0)
    def _():
        up.wait_send()
        diag.wait_send()


def run_halo(lats, lons, x, g):
    vmem = pl.BlockSpec(memory_space=pltpu.VMEM)
    shapes = ((48, QUART), (48, HALO), (16, HALO))
    return pl.pallas_call(
        functools.partial(halo_kernel, lats, lons),
        in_specs=[vmem] * 2,
        out_specs=[vmem] * 3,
        out_shape=[jax.ShapeDtypeStruct(s, BF16) for s in shapes],
        scratch_shapes=[pltpu.VMEM(s, BF16) for s in shapes]
        + [pltpu.SemaphoreType.DMA((3,)), pltpu.SemaphoreType.DMA((3,))],
        compiler_params=pltpu.CompilerParams(
            collective_id=0, has_side_effects=True, vmem_limit_bytes=32 * 2**20
        ),
        name="halo",
    )(x, g)


def reduce_kernel(
    lats,
    lons,
    ret_lat,
    ret_east,
    ret_corner,
    raw_q,
    raw_p,
    dtable,
    got_lat,
    got_east,
    got_corner,
    summed,
    mine,
    parts,
    parts_in,
    tiles,
    tiles_in,
    joined,
    ret_send,
    ret_recv,
    lon_send,
    lon_recv,
    lat_send,
    lat_recv,
    tile_send,
    tile_recv,
    back_send,
    back_recv,
):
    lat = lax.axis_index("lat")
    lon = lax.axis_index("lon")
    west = lax.rem(lon + lons - 1, lons)
    east = lax.rem(lon + 1, lons)
    barrier = pltpu.get_barrier_semaphore()

    def greet_lon(d, _):
        greet(lat, lax.rem(lon + d, lons))
        return 0

    def greet_lat(d, _):
        greet(lax.rem(lat + d, lats), lon)
        return 0

    lax.fori_loop(1, lons, greet_lon, 0)
    lax.fori_loop(1, lats, greet_lat, 0)

    @pl.when(lat > 0)
    def _():
        greet(lat - 1, west)

    raw = jnp.concatenate([raw_q[...], raw_p[...]], axis=1)
    for j in range(lons):
        row = []
        for t in range(TILES):
            col = j * TILES + t
            r, c = col // 6 * 16, col % 6 * 128
            row.append(raw[r : r + 16, c : c + 128])
        row.append(dtable[:, j * TCHUNK : (j + 1) * TCHUNK])
        chunk = jnp.concatenate(row, axis=1)
        mine[j] = chunk
        parts[j] = chunk.astype(BF16)

    peers = lons - 1 + lats - 1
    pl.semaphore_wait(barrier, jnp.where(lat < lats - 1, peers + 1, peers))

    down = copy_to(ret_lat, got_lat, ret_send.at[0], ret_recv.at[0], lat + 1, lon)
    side = copy_to(ret_east, got_east, ret_send.at[1], ret_recv.at[1], lat, east)
    diag = copy_to(ret_corner, got_corner, ret_send.at[2], ret_recv.at[2], lat + 1, east)

    def to_lon(d):
        to = lax.rem(lon + d, lons)
        return copy_to(parts.at[to], parts_in.at[lon], lon_send.at[to], lon_recv.at[lon], lat, to)

    def from_lon(d):
        at = lax.rem(lon + d, lons)
        return copy_to(parts.at[at], parts_in.at[at], lon_send.at[at], lon_recv.at[at], lat, at)

    def start_lon(d, _):
        to_lon(d).start()
        return 0

    lax.fori_loop(1, lons, start_lon, 0)
    side.start()

    @pl.when(lat < lats - 1)
    def _():
        down.start()
        diag.start()

    def add_lon(d, total):
        from_lon(d).wait_recv()
        return total + parts_in[lax.rem(lon + d, lons)].astype(F32)

    chunk = lax.fori_loop(1, lons, add_lon, mine[lon])
    table = chunk[:, WCHUNK:]
    square = jnp.sum(table * table).reshape(1, 1)
    high = square.astype(BF16).astype(F32)
    low = (square - high).astype(BF16).astype(F32)
    row = lax.broadcasted_iota(jnp.int32, (16, 128), 0)
    pair = jnp.where(row < 8, high, low)
    for t in range(lats):
        piece = chunk[:, t * 128 : t * 128 + 128] if t < TILES else jnp.zeros((16, 128), F32)
        tiles[t] = jnp.concatenate([piece, pair], axis=1).astype(BF16)

    def to_lat(d):
        to = lax.rem(lat + d, lats)
        return copy_to(tiles.at[to], tiles_in.at[lat], lat_send.at[to], lat_recv.at[lat], to, lon)

    def from_lat(d):
        at = lax.rem(lat + d, lats)
        return copy_to(tiles.at[at], tiles_in.at[at], lat_send.at[at], lat_recv.at[at], at, lon)

    def start_lat(d, _):
        to_lat(d).start()
        return 0

    lax.fori_loop(1, lats, start_lat, 0)

    def add_lat(d, total):
        from_lat(d).wait_recv()
        return total + tiles_in[lax.rem(lat + d, lats)].astype(F32)

    total = lax.fori_loop(1, lats, add_lat, tiles[lat].astype(F32))
    square = total[0:1, 128:129] + total[8:9, 128:129]
    high = square.astype(BF16).astype(F32)
    low = (square - high).astype(BF16).astype(F32)
    row = lax.broadcasted_iota(jnp.int32, (16, TCHUNK), 0)
    table = jnp.where(row == 12, high, jnp.where(row == 13, low, table))

    def to_row(d):
        to = lax.rem(lat + d, lats)
        return copy_to(joined.at[lat], joined.at[lat], tile_send.at[to], tile_recv.at[lat], to, lon)

    def from_row(at):
        return copy_to(joined.at[at], joined.at[at], tile_send.at[at], tile_recv.at[at], at, lon)

    def start_row(d, _):
        to_row(d).start()
        return 0

    @pl.when(lat < TILES)
    def _():
        joined[lat] = total[:, :128].astype(BF16)
        lax.fori_loop(1, lats, start_row, 0)

    def wait_row(at, _):
        @pl.when(at != lat)
        def _():
            from_row(at).wait_recv()

        return 0

    lax.fori_loop(0, TILES, wait_row, 0)
    pieces = [joined[t] for t in range(TILES)] + [table.astype(BF16)]
    summed[lon] = jnp.concatenate(pieces, axis=1)

    def to_back(d):
        to = lax.rem(lon + d, lons)
        return copy_to(summed.at[lon], summed.at[lon], back_send.at[to], back_recv.at[lon], lat, to)

    def from_back(d):
        at = lax.rem(lon + d, lons)
        return copy_to(summed.at[at], summed.at[at], back_send.at[at], back_recv.at[at], lat, at)

    def start_back(d, _):
        to_back(d).start()
        return 0

    lax.fori_loop(1, lons, start_back, 0)

    def done_lon(d, _):
        to_lon(d).wait_send()
        from_back(d).wait_recv()
        to_back(d).wait_send()
        return 0

    def done_lat(d, _):
        to_lat(d).wait_send()
        return 0

    def done_row(d, _):
        to_row(d).wait_send()
        return 0

    lax.fori_loop(1, lons, done_lon, 0)
    lax.fori_loop(1, lats, done_lat, 0)

    @pl.when(lat < TILES)
    def _():
        lax.fori_loop(1, lats, done_row, 0)

    side.wait_send()
    side.wait_recv()

    @pl.when(lat < lats - 1)
    def _():
        down.wait_send()
        diag.wait_send()

    @pl.when(lat > 0)
    def _():
        down.wait_recv()
        diag.wait_recv()

    @pl.when(lat == 0)
    def _():
        got_lat[...] = jnp.zeros_like(got_lat)
        got_corner[...] = jnp.zeros_like(got_corner)


def run_reduce(lats, lons, ret_lat, ret_east, ret_corner, raw_q, raw_p, dtable):
    vmem = pl.BlockSpec(memory_space=pltpu.VMEM)
    shapes = ((48, QUART), (48, HALO), (16, HALO), (lons, 16, CHUNK))
    sems = pltpu.SemaphoreType.DMA
    return pl.pallas_call(
        functools.partial(reduce_kernel, lats, lons),
        in_specs=[vmem] * 6,
        out_specs=[vmem] * 4,
        out_shape=[jax.ShapeDtypeStruct(s, BF16) for s in shapes],
        scratch_shapes=[
            pltpu.VMEM((lons, 16, CHUNK), F32),
            pltpu.VMEM((lons, 16, CHUNK), BF16),
            pltpu.VMEM((lons, 16, CHUNK), BF16),
            pltpu.VMEM((lats, 16, 256), BF16),
            pltpu.VMEM((lats, 16, 256), BF16),
            pltpu.VMEM((TILES, 16, 128), BF16),
            sems((3,)),
            sems((3,)),
            sems((lons,)),
            sems((lons,)),
            sems((lats,)),
            sems((lats,)),
            sems((lats,)),
            sems((TILES,)),
            sems((lons,)),
            sems((lons,)),
        ],
        compiler_params=pltpu.CompilerParams(
            collective_id=1, has_side_effects=True, vmem_limit_bytes=32 * 2**20
        ),
        name="reduce",
    )(ret_lat, ret_east, ret_corner, raw_q, raw_p, dtable)


def finish_kernel(
    lats,
    lons,
    lat_ref,
    x_own,
    g_own,
    got_lat,
    got_east,
    got_corner,
    summed,
    x_out,
    g_out,
    grad_q,
    grad_p,
    grad_bias,
):
    first = lat_ref[0] == 0
    east = got_east[...].astype(F32)
    corner = got_corner[...].astype(F32)
    for n, (own, out) in enumerate(((x_own, x_out), (g_own, g_out))):
        for z in range(2):
            at = n * 2 + z
            side = east[at * 12 : at * 12 + 12]
            top = jnp.where(first, side[:3], corner[at * 3 : at * 3 + 3])
            out[z, :, 0:HALO] = jnp.concatenate([top, side[3:]], axis=0).astype(BF16)

    def strip(k, _):
        base = pl.multiple_of(k * HALO, HALO)
        rows = got_lat[:, pl.ds(base, HALO)].astype(F32)
        for q in range(4):
            lanes = pl.ds(pl.multiple_of(q * QUART + base, HALO), HALO)

            @pl.when((k > 0) | (q > 0))
            def _():
                for n, (own, out) in enumerate(((x_own, x_out), (g_own, g_out))):
                    for z in range(2):
                        r = q * 12 + (n * 2 + z) * 3
                        mine = own[z, :, lanes].astype(F32)
                        top = jnp.where(first, mine[:3], rows[r : r + 3])
                        out[z, :, lanes] = jnp.concatenate([top, mine[3:]], axis=0).astype(BF16)

        return 0

    lax.fori_loop(0, QUART // HALO, strip, 0)
    whole = [summed[j].astype(F32) for j in range(lons)]
    squares = jnp.zeros((16, 128), F32)
    table_squares = jnp.zeros((1, 1), F32)
    cols = []
    for j in range(lons):
        for t in range(TILES):
            piece = whole[j][:, t * 128 : t * 128 + 128]
            squares = squares + piece * piece
            cols.append(piece)
        table_squares = table_squares + whole[j][12:13, WCHUNK : WCHUNK + 1]
        table_squares = table_squares + whole[j][13:14, WCHUNK : WCHUNK + 1]
    rms = jnp.sqrt(jnp.sum(squares).reshape(1, 1) / (4 * C * C) + 1e-6)
    for r in range(12):
        row = jnp.concatenate(cols[r * 6 : r * 6 + 6], axis=1) / rms
        grad_q[r * 16 : r * 16 + 16] = row[:, : 3 * C]
        grad_p[r * 16 : r * 16 + 16] = row[:, 3 * C :]
    table = jnp.concatenate([part[:12, WCHUNK:] for part in whole], axis=1)
    table_rms = jnp.sqrt(table_squares / (lats * 2 * HEADS * POS) + 1e-6)
    grad_bias[...] = table[:, :POS] / table_rms


def run_finish(lats, lons, lat, *args):
    vmem = pl.BlockSpec(memory_space=pltpu.VMEM)
    shape = jax.ShapeDtypeStruct
    return pl.pallas_call(
        functools.partial(finish_kernel, lats, lons),
        in_specs=[pl.BlockSpec(memory_space=pltpu.SMEM)] + [vmem] * 6,
        out_specs=[vmem] * 5,
        out_shape=[
            shape((2, 12, OWN), BF16),
            shape((2, 12, OWN), BF16),
            shape((C, 3 * C), F32),
            shape((C, C), F32),
            shape((2 * HEADS, POS), F32),
        ],
        compiler_params=pltpu.CompilerParams(vmem_limit_bytes=32 * 2**20),
        name="finish",
    )(lat.reshape(1), *args)


def on_device(inputs, cotangent, norm_gain, norm_shift, w_qkv, w_proj, bias_table):
    lat = lax.axis_index("lat")
    lats = lax.axis_size("lat")
    lons = lax.axis_size("lon")
    halos = run_halo(lats, lons, inputs, cotangent)
    x_own, g_own, *sent = run_windows(
        lats - 1,
        lat,
        inputs,
        cotangent,
        halos,
        norm_gain,
        norm_shift,
        w_qkv,
        w_proj,
        bias_table,
    )
    got = run_reduce(lats, lons, *sent)
    x_out, g_out, grad_q, grad_p, grad_bias = run_finish(lats, lons, lat, x_own, g_own, *got)
    return x_out, g_out, grad_q, grad_p, grad_bias.reshape(2, HEADS, POS)


def solution(mesh):
    return jax.shard_map(
        on_device,
        mesh=mesh,
        in_specs=(
            P(None, "lat", "lon"),
            P(None, "lat", "lon"),
            P(),
            P(),
            P(),
            P(),
            P("lat", None, None),
        ),
        out_specs=(P(None, "lat", "lon"), P(None, "lat", "lon"), P(), P(), P("lat", None, None)),
        check_vma=False,
    )
```

```python
import functools
import math

import jax
import jax.numpy as jnp
import numpy as np
from jax import lax
from jax.experimental import pallas as pl
from jax.experimental.pallas import tpu as pltpu
from jax.sharding import PartitionSpec as P

C = 192
HEADS = 6
HD = 32
WLON = 12
WIN = 144
HALF = 72
SPAN = 23
ROWLEN = 12 * SPAN
ROWPAD = 384
COLS = 96
HALO = 6 * C
WLANES = WLON * C
OWN = COLS * C
FRAME = OWN + HALO
FROWS = 24
QUART = OWN // 4
WPB = 8
POS = 3312
TABLE = 4096
WCHUNK = 12 * 768 // 8
TCHUNK = TABLE // 8
CHUNK = WCHUNK + TCHUNK
TILES = WCHUNK // 128
MESH = pl.DeviceIdType.MESH
EPS = 1e-5
SCALE = HD**-0.5
LOG2E = math.log2(math.e)
F32 = jnp.float32
BF16 = jnp.bfloat16


def nn(a, b):
    return lax.dot_general(a, b, (((1,), (0,)), ((), ())), preferred_element_type=F32)


def nt(a, b):
    return lax.dot_general(a, b, (((1,), (1,)), ((), ())), preferred_element_type=F32)


def tn(a, b):
    return lax.dot_general(a, b, (((0,), (0,)), ((), ())), preferred_element_type=F32)


def pick_matrix():
    out = np.zeros((WIN, ROWPAD), np.float32)
    for pk in range(6):
        for zk in range(2):
            for lk in range(WLON):
                out[(pk * 2 + zk) * WLON + lk, (zk * 6 + pk) * SPAN + 11 - lk] = 1.0
    return out


def frame_in(own, halo_lat, halo_east, halo_corner, which, frame):
    def chunk(k, _):
        base = pl.multiple_of(k * HALO, HALO)
        for z in range(2):
            frame[z, 0:12, pl.ds(base, HALO)] = own[z, :, pl.ds(base, HALO)].astype(F32)
        return 0

    lax.fori_loop(0, OWN // HALO, chunk, 0)

    def strip(k, _):
        base = pl.multiple_of(k * HALO, HALO)
        rows = halo_lat[:, pl.ds(base, HALO)].astype(F32)
        for q in range(4):
            for z in range(2):
                r = q * 12 + (which * 2 + z) * 3
                frame[z, 12:15, pl.ds(pl.multiple_of(q * QUART + base, HALO), HALO)] = rows[r : r + 3]
        return 0

    lax.fori_loop(0, QUART // HALO, strip, 0)
    east = halo_east[...].astype(F32)
    corner = halo_corner[...].astype(F32)
    for z in range(2):
        r = (which * 2 + z) * 12
        frame[z, 0:12, OWN:FRAME] = east[r : r + 12]
        r = (which * 2 + z) * 3
        frame[z, 12:15, OWN:FRAME] = corner[r : r + 3]


def frame_out(frame, own, ret_lat, ret_east, ret_corner, which):
    def chunk(k, _):
        base = pl.multiple_of(k * HALO, HALO)
        for z in range(2):
            own[z, :, pl.ds(base, HALO)] = frame[z, 0:12, pl.ds(base, HALO)].astype(BF16)
        return 0

    lax.fori_loop(0, OWN // HALO, chunk, 0)


def strips_out(frames, ret_lat, ret_east, ret_corner):
    def strip(k, _):
        base = pl.multiple_of(k * HALO, HALO)
        pieces = []
        for q in range(4):
            for frame in frames:
                for z in range(2):
                    pieces.append(
                        frame[z, 12:15, pl.ds(pl.multiple_of(q * QUART + base, HALO), HALO)]
                    )
        ret_lat[:, pl.ds(base, HALO)] = jnp.concatenate(pieces, axis=0).astype(BF16)
        return 0

    lax.fori_loop(0, QUART // HALO, strip, 0)
    pieces = [frame[z, 0:12, OWN:FRAME] for frame in frames for z in range(2)]
    ret_east[...] = jnp.concatenate(pieces, axis=0).astype(BF16)
    pieces = [frame[z, 12:15, OWN:FRAME] for frame in frames for z in range(2)]
    pieces.append(jnp.zeros((4, HALO), F32))
    ret_corner[...] = jnp.concatenate(pieces, axis=0).astype(BF16)


def windows_in(frame, rows, count, tokens, first):
    def window(w, _):
        base = HALO + w * WLANES
        for z in range(2):
            for m in range(6):
                at = pl.multiple_of(base + m * 2 * C, 128)
                slab = frame[z, rows : rows + 8, pl.ds(at, 2 * C)]
                odd = pltpu.roll(slab[:, 128:384], 192, 1)
                for t in range(2):
                    lanes = slice(t * 128, t * 128 + 128)
                    slots = pl.ds(z * 12 + 2 * m, count, stride=24)
                    tokens[first + w, t, slots, :] = slab[:count, lanes]
                    slots = pl.ds(z * 12 + 2 * m + 1, count, stride=24)
                    tokens[first + w, t, slots, :] = odd[:count, lanes]
        return 0

    lax.fori_loop(0, WPB, window, 0)


def windows_out(frame, rows, count, tokens, first):
    lane = lax.broadcasted_iota(jnp.int32, (8, 128), 1)

    def window(w, _):
        base = HALO + w * WLANES
        for z in range(2):
            for m in range(6):
                at = pl.multiple_of(base + m * 2 * C, 128)
                slots = pl.ds(z * 12 + 2 * m, count, stride=24)
                even = [tokens[first + w, t, slots, :] for t in range(2)]
                slots = pl.ds(z * 12 + 2 * m + 1, count, stride=24)
                odd = [tokens[first + w, t, slots, :] for t in range(2)]
                odd.append(jnp.zeros((8 - count, 256), F32))
                odd = jnp.concatenate([jnp.concatenate(odd[:2], axis=1), odd[2]], axis=0)
                odd = pltpu.roll(odd, 64, 1)
                mid = jnp.where(lane[:count] < 64, even[1], odd[:count, :128])
                frame[z, rows : rows + count, pl.ds(at, 128)] = even[0]
                frame[z, rows : rows + count, pl.ds(at + 128, 128)] = mid
                frame[z, rows : rows + count, pl.ds(at + 256, 128)] = odd[:count, 128:]
        return 0

    lax.fori_loop(0, WPB, window, 0)


def bias_in(table, pick, rows_scratch, shifted, bias):
    for zq in range(2):
        for pq in range(6):
            at = (zq * 6 + pq) * ROWLEN
            part = table[:, at : at + ROWLEN]
            rows_scratch[pq * 2 + zq, 0:12, 0:ROWLEN] = part
    for bh in range(12):
        rows = rows_scratch[:, bh, :]
        rows = jnp.concatenate([rows, jnp.zeros((4, ROWPAD), F32)], axis=0)
        for lq in range(WLON):
            moved = pltpu.roll(rows, (ROWPAD - lq) % ROWPAD, 1) if lq else rows
            for t in range(3):
                shifted[t, pl.ds(lq, 12, stride=12), :] = moved[:12, t * 128 : t * 128 + 128]
        full = jnp.concatenate([shifted[t] for t in range(3)], axis=1)
        high = full.astype(BF16)
        rest = full - high.astype(F32)
        mid = rest.astype(BF16)
        low = (rest - mid.astype(F32)).astype(BF16)
        total = nt(pick, high) + nt(pick, mid) + nt(pick, low)
        bias[bh // HEADS, bh % HEADS] = total * LOG2E


def bias_out(grads, pick, shifted, rows_scratch, out):
    rows_scratch[...] = jnp.zeros_like(rows_scratch)
    for bh in range(12):
        full = grads[bh // HEADS, bh % HEADS].T
        high = full.astype(BF16)
        low = (full - high.astype(F32)).astype(BF16)
        full = nn(high, pick) + nn(low, pick)
        for t in range(3):
            shifted[t] = full[:, t * 128 : t * 128 + 128]
        total = jnp.zeros((16, ROWPAD), F32)
        for lq in range(WLON):
            rows = [shifted[t, pl.ds(lq, 12, stride=12), :] for t in range(3)]
            rows = jnp.concatenate(rows, axis=1)
            rows = jnp.concatenate([rows, jnp.zeros((4, ROWPAD), F32)], axis=0)
            total = total + (pltpu.roll(rows, lq, 1) if lq else rows)
        rows_scratch[:, bh, :] = total[:12]
    parts = [rows_scratch[pq * 2 + zq][:, :ROWLEN] for zq in range(2) for pq in range(6)]
    parts.append(jnp.zeros((16, TABLE - POS), F32))
    out[...] = jnp.concatenate(parts, axis=1)


def attend(n, x_ref, g_ref, us, bias, dbias, band, gain, shift, wqkv, wqkv_t, wproj, wproj_t, eye, raw_q, raw_p):
    ws = range(len(us))
    pairs = [(w, i) for w in ws for i in range(HEADS)]

    def tokens(ref):
        rows = [jnp.concatenate([ref[u, 0], ref[u, 1]], axis=1) for u in us]
        return jnp.concatenate(rows, axis=0)[:, :C]

    def split(a):
        return [a[w * n : (w + 1) * n] for w in ws]

    x = tokens(x_ref)
    g = tokens(g_ref)
    gb = g.astype(BF16)
    center = x - jnp.mean(x, axis=1, keepdims=True)
    rstd = lax.rsqrt(jnp.mean(center * center, axis=1, keepdims=True) + EPS)
    xn = center * rstd
    h = (xn * gain + shift).astype(BF16)
    qkv = split(nn(h, wqkv[...]).astype(BF16))
    kv_t = [nt(wqkv_t[C:], part).astype(BF16) for part in split(h)]
    h_t = nt(eye[...], h).astype(BF16)
    do = split(nn(gb, wproj_t[...]).astype(BF16))

    def cut(a, base):
        return [a[w][:, base + i * HD : base + (i + 1) * HD] for w, i in pairs]

    q, k, v = cut(qkv, 0), cut(qkv, C), cut(qkv, 2 * C)
    k_t = [kv_t[w][i * HD : (i + 1) * HD] for w, i in pairs]
    v_t = [kv_t[w][C + i * HD : C + (i + 1) * HD] for w, i in pairs]
    do_h = cut(do, 0)
    hs = range(len(pairs))
    o_t, dvs, dks, dq_t = {}, {}, {}, {}
    for b0 in range(0, len(pairs), 6):
        grp = range(b0, b0 + 6)
        s = {i: nt(k[i], q[i]) * (SCALE * LOG2E) + bias[band, pairs[i][1]] for i in grp}
        dp = {i: nt(v[i], do_h[i]) for i in grp}
        e = {i: jnp.exp2(s[i] - jnp.max(s[i], axis=0, keepdims=True)) for i in grp}
        p = {i: e[i] * (1.0 / jnp.sum(e[i], axis=0, keepdims=True)) for i in grp}
        pb = {i: p[i].astype(BF16) for i in grp}
        for i in grp:
            o_t[i] = nn(v_t[i], pb[i])
        for i in grp:
            dvs[i] = nn(pb[i], do_h[i])
        ds = {i: p[i] * (dp[i] - jnp.sum(p[i] * dp[i], axis=0, keepdims=True)) for i in grp}
        for i in grp:
            dbias[band, pairs[i][1]] += ds[i]
        dsb = {i: (ds[i] * SCALE).astype(BF16) for i in grp}
        for i in grp:
            dks[i] = nn(dsb[i], q[i])
        for i in grp:
            dq_t[i] = nn(k_t[i], dsb[i])

    def join(parts, axis):
        parts = [[parts[w * HEADS + i] for i in range(HEADS)] for w in ws]
        return [jnp.concatenate(part, axis=axis).astype(BF16) for part in parts]

    o_t, dq_t = join(o_t, 0), join(dq_t, 0)
    dk, dv = (jnp.concatenate(join(part, 1), axis=0) for part in (dks, dvs))
    o = jnp.concatenate([nt(eye[:n, :n], o_t[w]).astype(BF16) for w in ws], axis=0)
    dq = jnp.concatenate([nt(eye[:n, :n], dq_t[w]).astype(BF16) for w in ws], axis=0)
    a = nn(o, wproj[...]).astype(BF16)
    dh = nn(dq, wqkv_t[0:C]) + nn(dk, wqkv_t[C : 2 * C]) + nn(dv, wqkv_t[2 * C :])
    raw_p[...] += sum(nn(o_t[w], gb[w * n : (w + 1) * n]) for w in ws)
    raw_q[:, 0:C] += nn(h_t, dq)
    raw_q[:, C : 2 * C] += nn(h_t, dk)
    raw_q[:, 2 * C :] += nn(h_t, dv)
    dxn = dh * gain
    m1 = jnp.mean(dxn, axis=1, keepdims=True)
    m2 = jnp.mean(dxn * xn, axis=1, keepdims=True)
    dx = (rstd * (dxn - m1 - xn * m2)).astype(BF16)
    x = split(x + a.astype(F32))
    g = split(g + dx.astype(F32))
    for w, u in enumerate(us):
        x_ref[u, 0] = x[w][:, :128]
        x_ref[u, 1, :, 0:64] = x[w][:, 128:]
        g_ref[u, 0] = g[w][:, :128]
        g_ref[u, 1, :, 0:64] = g[w][:, 128:]


def window_kernel(
    last,
    lat_ref,
    x_own,
    g_own,
    halo_lat,
    halo_east,
    halo_corner,
    gain_ref,
    shift_ref,
    wqkv,
    wqkv_t,
    wproj,
    wproj_t,
    eye,
    pick,
    table,
    x_out,
    g_out,
    ret_lat,
    ret_east,
    ret_corner,
    raw_q,
    raw_p,
    dtable,
    fx,
    fg,
    xw,
    gw,
    xh,
    gh,
    bias,
    dbias,
    bias_h,
    dbias_h,
    rows_scratch,
    shifted,
):
    lat = lat_ref[0]
    first = lat == 0
    final = lat == last
    frame_in(x_own, halo_lat, halo_east, halo_corner, 0, fx)
    frame_in(g_own, halo_lat, halo_east, halo_corner, 1, fg)
    rows_scratch[...] = jnp.zeros_like(rows_scratch)
    bias_in(table, pick[...], rows_scratch, shifted, bias)
    dbias[...] = jnp.zeros_like(dbias)
    raw_q[...] = jnp.zeros_like(raw_q)
    raw_p[...] = jnp.zeros_like(raw_p)
    for band in range(2):
        windows_in(fx, 3 + 6 * band, 6, xw, band * WPB)
        windows_in(fg, 3 + 6 * band, 6, gw, band * WPB)
    gain = gain_ref[...]
    shift = shift_ref[...]
    rest = (gain, shift, wqkv, wqkv_t, wproj, wproj_t, eye, raw_q, raw_p)

    def full(u, _):
        attend(WIN, xw, gw, [4 * u + r for r in range(4)], bias, dbias, u // (WPB // 4), *rest)
        return 0

    lax.fori_loop(0, jnp.where(final, WPB // 4, 2 * WPB // 4), full, 0)

    def halves(rows, band, lo):
        windows_in(fx, rows, 3, xh, 0)
        windows_in(fg, rows, 3, gh, 0)
        dbias_h[...] = jnp.zeros_like(dbias_h)
        for i in range(HEADS):
            bias_h[0, i] = bias[band, i][lo : lo + HALF, lo : lo + HALF]

        def half(u, _):
            attend(HALF, xh, gh, [4 * u + r for r in range(4)], bias_h, dbias_h, 0, *rest)
            return 0

        lax.fori_loop(0, WPB // 4, half, 0)
        zero = jnp.zeros((HALF, HALF), F32)
        for i in range(HEADS):
            part = dbias_h[0, i]
            part = jnp.concatenate([zero, part] if lo else [part, zero], axis=1)
            dbias[band, i, lo : lo + HALF, :] += part

    for band in range(2):
        windows_out(fx, 3 + 6 * band, 6, xw, band * WPB)
        windows_out(fg, 3 + 6 * band, 6, gw, band * WPB)

    @pl.when(first)
    def _():
        halves(0, 0, HALF)
        windows_out(fx, 0, 3, xh, 0)
        windows_out(fg, 0, 3, gh, 0)

    @pl.when(final)
    def _():
        halves(9, 1, 0)
        windows_out(fx, 9, 3, xh, 0)
        windows_out(fg, 9, 3, gh, 0)

    bias_out(dbias, pick[...], shifted, rows_scratch, dtable)
    frame_out(fx, x_out, ret_lat, ret_east, ret_corner, 0)
    frame_out(fg, g_out, ret_lat, ret_east, ret_corner, 1)
    strips_out((fx, fg), ret_lat, ret_east, ret_corner)


def run_windows(last, lat, x_own, g_own, halos, gain, shift, wqkv, wproj, table):
    vmem = pl.BlockSpec(memory_space=pltpu.VMEM)
    shape = jax.ShapeDtypeStruct
    return pl.pallas_call(
        functools.partial(window_kernel, last),
        in_specs=[pl.BlockSpec(memory_space=pltpu.SMEM)] + [vmem] * 14,
        out_specs=[vmem] * 8,
        out_shape=[
            shape((2, 12, OWN), BF16),
            shape((2, 12, OWN), BF16),
            shape((48, QUART), BF16),
            shape((48, HALO), BF16),
            shape((16, HALO), BF16),
            shape((C, 3 * C), F32),
            shape((C, C), F32),
            shape((16, TABLE), F32),
        ],
        scratch_shapes=[
            pltpu.VMEM((2, FROWS, FRAME), F32),
            pltpu.VMEM((2, FROWS, FRAME), F32),
            pltpu.VMEM((2 * WPB, 2, WIN, 128), F32),
            pltpu.VMEM((2 * WPB, 2, WIN, 128), F32),
            pltpu.VMEM((WPB, 2, HALF, 128), F32),
            pltpu.VMEM((WPB, 2, HALF, 128), F32),
            pltpu.VMEM((2, HEADS, WIN, WIN), F32),
            pltpu.VMEM((2, HEADS, WIN, WIN), F32),
            pltpu.VMEM((1, HEADS, HALF, HALF), F32),
            pltpu.VMEM((1, HEADS, HALF, HALF), F32),
            pltpu.VMEM((12, 16, ROWPAD), F32),
            pltpu.VMEM((3, WIN, 128), F32),
        ],
        compiler_params=pltpu.CompilerParams(vmem_limit_bytes=56 * 2**20),
        name="windows",
    )(
        lat.reshape(1),
        x_own,
        g_own,
        *halos,
        gain.reshape(1, C),
        shift.reshape(1, C),
        wqkv,
        wqkv.T,
        wproj,
        wproj.T,
        jnp.eye(C, dtype=BF16),
        jnp.asarray(pick_matrix(), BF16),
        table.reshape(2 * HEADS, POS),
    )


def copy_to(src, dst, send, recv, lat, lon):
    return pltpu.make_async_remote_copy(
        src_ref=src,
        dst_ref=dst,
        send_sem=send,
        recv_sem=recv,
        device_id=(lat, lon),
        device_id_type=MESH,
    )


def greet(lat, lon):
    barrier = pltpu.get_barrier_semaphore()
    pl.semaphore_signal(barrier, inc=1, device_id=(lat, lon), device_id_type=MESH)


def halo_kernel(
    lats, lons, x, g, halo_lat, halo_east, halo_corner, lat_buf, east_buf, corner_buf, send, recv
):
    lat = lax.axis_index("lat")
    lon = lax.axis_index("lon")
    west = lax.rem(lon + lons - 1, lons)
    east = lax.rem(lon + 1, lons)
    barrier = pltpu.get_barrier_semaphore()
    greet(lat, east)

    @pl.when(lat < lats - 1)
    def _():
        greet(lat + 1, lon)
        greet(lat + 1, east)

    def strip(k, _):
        base = pl.multiple_of(k * HALO, HALO)
        pieces = []
        for q in range(4):
            for ref in (x, g):
                for z in range(2):
                    lanes = pl.ds(pl.multiple_of(q * QUART + base, HALO), HALO)
                    pieces.append(ref[z, :, lanes].astype(F32)[:3])
        lat_buf[:, pl.ds(base, HALO)] = jnp.concatenate(pieces, axis=0).astype(BF16)
        return 0

    lax.fori_loop(0, QUART // HALO, strip, 0)
    sides = [ref[z, :, 0:HALO].astype(F32) for ref in (x, g) for z in range(2)]
    east_buf[...] = jnp.concatenate(sides, axis=0).astype(BF16)
    corners = [side[:3] for side in sides] + [jnp.zeros((4, HALO), F32)]
    corner_buf[...] = jnp.concatenate(corners, axis=0).astype(BF16)

    pl.semaphore_wait(barrier, jnp.where(lat > 0, 3, 1))
    up = copy_to(lat_buf, halo_lat, send.at[0], recv.at[0], lat - 1, lon)
    side = copy_to(east_buf, halo_east, send.at[1], recv.at[1], lat, west)
    diag = copy_to(corner_buf, halo_corner, send.at[2], recv.at[2], lat - 1, west)

    @pl.when(lat > 0)
    def _():
        up.start()
        diag.start()

    side.start()

    @pl.when(lat < lats - 1)
    def _():
        up.wait_recv()
        diag.wait_recv()

    @pl.when(lat == lats - 1)
    def _():
        halo_lat[...] = jnp.zeros_like(halo_lat)
        halo_corner[...] = jnp.zeros_like(halo_corner)

    side.wait_recv()
    side.wait_send()

    @pl.when(lat > 0)
    def _():
        up.wait_send()
        diag.wait_send()


def run_halo(lats, lons, x, g):
    vmem = pl.BlockSpec(memory_space=pltpu.VMEM)
    shapes = ((48, QUART), (48, HALO), (16, HALO))
    return pl.pallas_call(
        functools.partial(halo_kernel, lats, lons),
        in_specs=[vmem] * 2,
        out_specs=[vmem] * 3,
        out_shape=[jax.ShapeDtypeStruct(s, BF16) for s in shapes],
        scratch_shapes=[pltpu.VMEM(s, BF16) for s in shapes]
        + [pltpu.SemaphoreType.DMA((3,)), pltpu.SemaphoreType.DMA((3,))],
        compiler_params=pltpu.CompilerParams(
            collective_id=0, has_side_effects=True, vmem_limit_bytes=32 * 2**20
        ),
        name="halo",
    )(x, g)


def reduce_kernel(
    lats,
    lons,
    ret_lat,
    ret_east,
    ret_corner,
    raw_q,
    raw_p,
    dtable,
    got_lat,
    got_east,
    got_corner,
    summed,
    mine,
    parts,
    parts_in,
    tiles,
    tiles_in,
    joined,
    ret_send,
    ret_recv,
    lon_send,
    lon_recv,
    lat_send,
    lat_recv,
    tile_send,
    tile_recv,
    back_send,
    back_recv,
):
    lat = lax.axis_index("lat")
    lon = lax.axis_index("lon")
    west = lax.rem(lon + lons - 1, lons)
    east = lax.rem(lon + 1, lons)
    barrier = pltpu.get_barrier_semaphore()

    def greet_lon(d, _):
        greet(lat, lax.rem(lon + d, lons))
        return 0

    def greet_lat(d, _):
        greet(lax.rem(lat + d, lats), lon)
        return 0

    lax.fori_loop(1, lons, greet_lon, 0)
    lax.fori_loop(1, lats, greet_lat, 0)

    @pl.when(lat > 0)
    def _():
        greet(lat - 1, west)

    raw = jnp.concatenate([raw_q[...], raw_p[...]], axis=1)
    for j in range(lons):
        row = []
        for t in range(TILES):
            col = j * TILES + t
            r, c = col // 6 * 16, col % 6 * 128
            row.append(raw[r : r + 16, c : c + 128])
        row.append(dtable[:, j * TCHUNK : (j + 1) * TCHUNK])
        chunk = jnp.concatenate(row, axis=1)
        mine[j] = chunk
        parts[j] = chunk.astype(BF16)

    peers = lons - 1 + lats - 1
    pl.semaphore_wait(barrier, jnp.where(lat < lats - 1, peers + 1, peers))

    down = copy_to(ret_lat, got_lat, ret_send.at[0], ret_recv.at[0], lat + 1, lon)
    side = copy_to(ret_east, got_east, ret_send.at[1], ret_recv.at[1], lat, east)
    diag = copy_to(ret_corner, got_corner, ret_send.at[2], ret_recv.at[2], lat + 1, east)

    def to_lon(d):
        to = lax.rem(lon + d, lons)
        return copy_to(parts.at[to], parts_in.at[lon], lon_send.at[to], lon_recv.at[lon], lat, to)

    def from_lon(d):
        at = lax.rem(lon + d, lons)
        return copy_to(parts.at[at], parts_in.at[at], lon_send.at[at], lon_recv.at[at], lat, at)

    def start_lon(d, _):
        to_lon(d).start()
        return 0

    lax.fori_loop(1, lons, start_lon, 0)
    side.start()

    @pl.when(lat < lats - 1)
    def _():
        down.start()
        diag.start()

    def add_lon(d, total):
        from_lon(d).wait_recv()
        return total + parts_in[lax.rem(lon + d, lons)].astype(F32)

    chunk = lax.fori_loop(1, lons, add_lon, mine[lon])
    table = chunk[:, WCHUNK:]
    square = jnp.sum(table * table).reshape(1, 1)
    high = square.astype(BF16).astype(F32)
    low = (square - high).astype(BF16).astype(F32)
    row = lax.broadcasted_iota(jnp.int32, (16, 128), 0)
    pair = jnp.where(row < 8, high, low)
    for t in range(lats):
        piece = chunk[:, t * 128 : t * 128 + 128] if t < TILES else jnp.zeros((16, 128), F32)
        tiles[t] = jnp.concatenate([piece, pair], axis=1).astype(BF16)

    def to_lat(d):
        to = lax.rem(lat + d, lats)
        return copy_to(tiles.at[to], tiles_in.at[lat], lat_send.at[to], lat_recv.at[lat], to, lon)

    def from_lat(d):
        at = lax.rem(lat + d, lats)
        return copy_to(tiles.at[at], tiles_in.at[at], lat_send.at[at], lat_recv.at[at], at, lon)

    def start_lat(d, _):
        to_lat(d).start()
        return 0

    lax.fori_loop(1, lats, start_lat, 0)

    def add_lat(d, total):
        from_lat(d).wait_recv()
        return total + tiles_in[lax.rem(lat + d, lats)].astype(F32)

    total = lax.fori_loop(1, lats, add_lat, tiles[lat].astype(F32))
    square = total[0:1, 128:129] + total[8:9, 128:129]
    high = square.astype(BF16).astype(F32)
    low = (square - high).astype(BF16).astype(F32)
    row = lax.broadcasted_iota(jnp.int32, (16, TCHUNK), 0)
    table = jnp.where(row == 12, high, jnp.where(row == 13, low, table))

    def to_row(d):
        to = lax.rem(lat + d, lats)
        return copy_to(joined.at[lat], joined.at[lat], tile_send.at[to], tile_recv.at[lat], to, lon)

    def from_row(at):
        return copy_to(joined.at[at], joined.at[at], tile_send.at[at], tile_recv.at[at], at, lon)

    def start_row(d, _):
        to_row(d).start()
        return 0

    @pl.when(lat < TILES)
    def _():
        joined[lat] = total[:, :128].astype(BF16)
        lax.fori_loop(1, lats, start_row, 0)

    def wait_row(at, _):
        @pl.when(at != lat)
        def _():
            from_row(at).wait_recv()

        return 0

    lax.fori_loop(0, TILES, wait_row, 0)
    pieces = [joined[t] for t in range(TILES)] + [table.astype(BF16)]
    summed[lon] = jnp.concatenate(pieces, axis=1)

    def to_back(d):
        to = lax.rem(lon + d, lons)
        return copy_to(summed.at[lon], summed.at[lon], back_send.at[to], back_recv.at[lon], lat, to)

    def from_back(d):
        at = lax.rem(lon + d, lons)
        return copy_to(summed.at[at], summed.at[at], back_send.at[at], back_recv.at[at], lat, at)

    def start_back(d, _):
        to_back(d).start()
        return 0

    lax.fori_loop(1, lons, start_back, 0)

    def done_lon(d, _):
        to_lon(d).wait_send()
        from_back(d).wait_recv()
        to_back(d).wait_send()
        return 0

    def done_lat(d, _):
        to_lat(d).wait_send()
        return 0

    def done_row(d, _):
        to_row(d).wait_send()
        return 0

    lax.fori_loop(1, lons, done_lon, 0)
    lax.fori_loop(1, lats, done_lat, 0)

    @pl.when(lat < TILES)
    def _():
        lax.fori_loop(1, lats, done_row, 0)

    side.wait_send()
    side.wait_recv()

    @pl.when(lat < lats - 1)
    def _():
        down.wait_send()
        diag.wait_send()

    @pl.when(lat > 0)
    def _():
        down.wait_recv()
        diag.wait_recv()

    @pl.when(lat == 0)
    def _():
        got_lat[...] = jnp.zeros_like(got_lat)
        got_corner[...] = jnp.zeros_like(got_corner)


def run_reduce(lats, lons, ret_lat, ret_east, ret_corner, raw_q, raw_p, dtable):
    vmem = pl.BlockSpec(memory_space=pltpu.VMEM)
    shapes = ((48, QUART), (48, HALO), (16, HALO), (lons, 16, CHUNK))
    sems = pltpu.SemaphoreType.DMA
    return pl.pallas_call(
        functools.partial(reduce_kernel, lats, lons),
        in_specs=[vmem] * 6,
        out_specs=[vmem] * 4,
        out_shape=[jax.ShapeDtypeStruct(s, BF16) for s in shapes],
        scratch_shapes=[
            pltpu.VMEM((lons, 16, CHUNK), F32),
            pltpu.VMEM((lons, 16, CHUNK), BF16),
            pltpu.VMEM((lons, 16, CHUNK), BF16),
            pltpu.VMEM((lats, 16, 256), BF16),
            pltpu.VMEM((lats, 16, 256), BF16),
            pltpu.VMEM((TILES, 16, 128), BF16),
            sems((3,)),
            sems((3,)),
            sems((lons,)),
            sems((lons,)),
            sems((lats,)),
            sems((lats,)),
            sems((lats,)),
            sems((TILES,)),
            sems((lons,)),
            sems((lons,)),
        ],
        compiler_params=pltpu.CompilerParams(
            collective_id=1, has_side_effects=True, vmem_limit_bytes=32 * 2**20
        ),
        name="reduce",
    )(ret_lat, ret_east, ret_corner, raw_q, raw_p, dtable)


def finish_kernel(
    lats,
    lons,
    lat_ref,
    x_own,
    g_own,
    got_lat,
    got_east,
    got_corner,
    summed,
    x_out,
    g_out,
    grad_q,
    grad_p,
    grad_bias,
):
    first = lat_ref[0] == 0
    east = got_east[...].astype(F32)
    corner = got_corner[...].astype(F32)
    for n, (own, out) in enumerate(((x_own, x_out), (g_own, g_out))):
        for z in range(2):
            at = n * 2 + z
            side = east[at * 12 : at * 12 + 12]
            top = jnp.where(first, side[:3], corner[at * 3 : at * 3 + 3])
            out[z, :, 0:HALO] = jnp.concatenate([top, side[3:]], axis=0).astype(BF16)

    def strip(k, _):
        base = pl.multiple_of(k * HALO, HALO)
        rows = got_lat[:, pl.ds(base, HALO)].astype(F32)
        for q in range(4):
            lanes = pl.ds(pl.multiple_of(q * QUART + base, HALO), HALO)

            @pl.when((k > 0) | (q > 0))
            def _():
                for n, (own, out) in enumerate(((x_own, x_out), (g_own, g_out))):
                    for z in range(2):
                        r = q * 12 + (n * 2 + z) * 3
                        mine = own[z, :, lanes].astype(F32)
                        top = jnp.where(first, mine[:3], rows[r : r + 3])
                        out[z, :, lanes] = jnp.concatenate([top, mine[3:]], axis=0).astype(BF16)

        return 0

    lax.fori_loop(0, QUART // HALO, strip, 0)
    whole = [summed[j].astype(F32) for j in range(lons)]
    squares = jnp.zeros((16, 128), F32)
    table_squares = jnp.zeros((1, 1), F32)
    cols = []
    for j in range(lons):
        for t in range(TILES):
            piece = whole[j][:, t * 128 : t * 128 + 128]
            squares = squares + piece * piece
            cols.append(piece)
        table_squares = table_squares + whole[j][12:13, WCHUNK : WCHUNK + 1]
        table_squares = table_squares + whole[j][13:14, WCHUNK : WCHUNK + 1]
    rms = jnp.sqrt(jnp.sum(squares).reshape(1, 1) / (4 * C * C) + 1e-6)
    for r in range(12):
        row = jnp.concatenate(cols[r * 6 : r * 6 + 6], axis=1) / rms
        grad_q[r * 16 : r * 16 + 16] = row[:, : 3 * C]
        grad_p[r * 16 : r * 16 + 16] = row[:, 3 * C :]
    table = jnp.concatenate([part[:12, WCHUNK:] for part in whole], axis=1)
    table_rms = jnp.sqrt(table_squares / (lats * 2 * HEADS * POS) + 1e-6)
    grad_bias[...] = table[:, :POS] / table_rms


def run_finish(lats, lons, lat, *args):
    vmem = pl.BlockSpec(memory_space=pltpu.VMEM)
    shape = jax.ShapeDtypeStruct
    return pl.pallas_call(
        functools.partial(finish_kernel, lats, lons),
        in_specs=[pl.BlockSpec(memory_space=pltpu.SMEM)] + [vmem] * 6,
        out_specs=[vmem] * 5,
        out_shape=[
            shape((2, 12, OWN), BF16),
            shape((2, 12, OWN), BF16),
            shape((C, 3 * C), F32),
            shape((C, C), F32),
            shape((2 * HEADS, POS), F32),
        ],
        compiler_params=pltpu.CompilerParams(vmem_limit_bytes=32 * 2**20),
        name="finish",
    )(lat.reshape(1), *args)


def on_device(inputs, cotangent, norm_gain, norm_shift, w_qkv, w_proj, bias_table):
    lat = lax.axis_index("lat")
    lats = lax.axis_size("lat")
    lons = lax.axis_size("lon")
    halos = run_halo(lats, lons, inputs, cotangent)
    x_own, g_own, *sent = run_windows(
        lats - 1,
        lat,
        inputs,
        cotangent,
        halos,
        norm_gain,
        norm_shift,
        w_qkv,
        w_proj,
        bias_table,
    )
    got = run_reduce(lats, lons, *sent)
    x_out, g_out, grad_q, grad_p, grad_bias = run_finish(lats, lons, lat, x_own, g_own, *got)
    return x_out, g_out, grad_q, grad_p, grad_bias.reshape(2, HEADS, POS)


def solution(mesh):
    return jax.shard_map(
        on_device,
        mesh=mesh,
        in_specs=(
            P(None, "lat", "lon"),
            P(None, "lat", "lon"),
            P(),
            P(),
            P(),
            P(),
            P("lat", None, None),
        ),
        out_specs=(P(None, "lat", "lon"), P(None, "lat", "lon"), P(), P(), P("lat", None, None)),
        check_vma=False,
    )
```

```python
import functools
import math

import jax
import jax.numpy as jnp
import numpy as np
from jax import lax
from jax.experimental import pallas as pl
from jax.experimental.pallas import tpu as pltpu
from jax.sharding import PartitionSpec as P

C = 192
HEADS = 6
HD = 32
WLON = 12
WIN = 144
HALF = 72
SPAN = 23
ROWLEN = 12 * SPAN
ROWPAD = 384
COLS = 96
HALO = 6 * C
WLANES = WLON * C
OWN = COLS * C
FRAME = OWN + HALO
FROWS = 15
GROUP = 4
WPB = 8
POS = 3312
TABLE = 4096
WCHUNK = 12 * 768 // 8
TCHUNK = TABLE // 8
TILES = WCHUNK // 128
MESH = pl.DeviceIdType.MESH
EPS = 1e-5
SCALE = HD**-0.5
LOG2E = math.log2(math.e)
F32 = jnp.float32
BF16 = jnp.bfloat16


def nn(a, b):
    return lax.dot_general(a, b, (((1,), (0,)), ((), ())), preferred_element_type=F32)


def nt(a, b):
    return lax.dot_general(a, b, (((1,), (1,)), ((), ())), preferred_element_type=F32)


def tn(a, b):
    return lax.dot_general(a, b, (((0,), (0,)), ((), ())), preferred_element_type=F32)


def pick_matrix():
    row = lax.broadcasted_iota(jnp.int32, (WIN, 1), 0)
    lk = lax.rem(row, WLON)
    block = lax.div(row, WLON)
    kb = lax.rem(block, 2) * 6 + lax.div(block, 2)
    col = lax.broadcasted_iota(jnp.int32, (WIN, ROWPAD), 1)
    return jnp.where(col == kb * SPAN + 11 - lk, 1.0, 0.0).astype(BF16)


def windows_in(frame, row, count, tokens, first, half=0):
    def window(w, _):
        base = HALO + (2 * w + half // HALF if count == 3 else w) * WLANES
        for m in range(6):
            at = pl.multiple_of(base + m * 2 * C, 128)
            slab = frame[row : row + count, :, pl.ds(at, 2 * C)].astype(F32).reshape(2 * count, 2 * C)
            even = slab[:, :C]
            odd = slab[:, C:]
            for n, part in ((2 * m, even), (2 * m + 1, odd)):
                slots = pl.ds(half + n, 2 * count, stride=WLON)
                tokens[first + w, 0, slots, :] = part[:, :128]
                tokens[first + w, 1, slots, :] = jnp.concatenate([part[:, 128:], part[:, 128:]], axis=1)
        return 0

    lax.fori_loop(0, WPB // 2 if count == 3 else WPB, window, 0)


def windows_out(frame, row, count, tokens, first, half=0):
    def window(w, _):
        base = HALO + (2 * w + half // HALF if count == 3 else w) * WLANES
        for m in range(6):
            at = pl.multiple_of(base + m * 2 * C, 128)
            parts = []
            for n in (2 * m, 2 * m + 1):
                slots = pl.ds(half + n, 2 * count, stride=WLON)
                parts.append(tokens[first + w, 0, slots, :])
                parts.append(tokens[first + w, 1, slots, :][:, : C - 128])
            slab = jnp.concatenate(parts, axis=1).reshape(count, 2, 2 * C)
            frame[row : row + count, :, pl.ds(at, 2 * C)] = slab.astype(BF16)
        return 0

    lax.fori_loop(0, WPB // 2 if count == 3 else WPB, window, 0)


def halves(frame, row, tokens, first, out):
    move = windows_out if out else windows_in
    move(frame, row, 3, tokens, first, 0)
    move(frame, row, 3, tokens, first, HALF)


def put_head(ref, slot, i, value):
    ref[slot, :, i * 128 : i * 128 + 128] = value[:, :128]
    ref[slot, :, 768 + i * 16 : 768 + i * 16 + 16] = value[:, 128:]


def get_head(ref, slot, i):
    tail = ref[slot, :, 768 + i * 16 : 768 + i * 16 + 16]
    return jnp.concatenate([ref[slot, :, i * 128 : i * 128 + 128], tail], axis=1)


def bias_in(table, flat, pick, rows_scratch, shifted, bias):
    for i in range(HEADS):
        flat[2 * i : 2 * i + 2, 0:POS] = table[i]
    for zq in range(2):
        for pq in range(6):
            at = (zq * 6 + pq) * ROWLEN
            rows_scratch[pq * 2 + zq, 0:12, 0:ROWLEN] = flat[0:12, at : at + ROWLEN]
    for n in range(12):
        rows = rows_scratch[:, n, :]
        rows = jnp.concatenate([rows, jnp.zeros((4, ROWPAD), F32)], axis=0)
        for lq in range(WLON):
            moved = pltpu.roll(rows, (ROWPAD - lq) % ROWPAD, 1) if lq else rows
            for t in range(3):
                shifted[t, pl.ds(lq, 12, stride=12), :] = moved[:12, t * 128 : t * 128 + 128]
        full = jnp.concatenate([shifted[t] for t in range(3)], axis=1)
        high = full.astype(BF16)
        rest = full - high.astype(F32)
        mid = rest.astype(BF16)
        low = (rest - mid.astype(F32)).astype(BF16)
        total = nt(pick, high) + nt(pick, mid) + nt(pick, low)
        put_head(bias, n % 2, n // 2, total * LOG2E)


def bias_out(grads, pick, shifted, rows_scratch):
    for n in range(12):
        full = nn(get_head(grads, n % 2, n // 2).astype(BF16).T, pick)
        for t in range(3):
            shifted[t] = full[:, t * 128 : t * 128 + 128]
        total = jnp.zeros((16, ROWPAD), F32)
        for lq in range(WLON):
            rows = [shifted[t, pl.ds(lq, 12, stride=12), :] for t in range(3)]
            rows = jnp.concatenate(rows, axis=1)
            rows = jnp.concatenate([rows, jnp.zeros((4, ROWPAD), F32)], axis=0)
            total = total + (pltpu.roll(rows, lq, 1) if lq else rows)
        rows_scratch[:, n, :] = total[:12]
    parts = [rows_scratch[pq * 2 + zq][:, :ROWLEN] for zq in range(2) for pq in range(6)]
    parts.append(jnp.zeros((16, TABLE - POS), F32))
    return jnp.concatenate(parts, axis=1)


def head_rows(a):
    lane = lax.broadcasted_iota(jnp.int32, (1, 128), 1) // HD
    zero = jnp.zeros((), BF16)

    def only(part, i):
        return jnp.where(lane[:, : part.shape[1]] == i % 4, part, zero)

    wide, slim = a[:, :128], a[:, 128:C]
    first = jnp.concatenate([only(wide[:128], i) for i in range(4)], axis=0)
    second = jnp.concatenate([only(slim[:128], i) for i in range(4, HEADS)], axis=0)
    tail = [only(wide[128:], i) for i in range(4)]
    left = jnp.concatenate(tail + [jnp.zeros((64, 128), BF16)], axis=0)
    tail = [only(slim[128:], i) for i in range(4, HEADS)]
    right = jnp.concatenate([jnp.zeros((64, 64), BF16)] + tail + [jnp.zeros((32, 64), BF16)], axis=0)
    return first, second, left, right


def across(a, rows):
    first, second, left, right = rows
    return jnp.concatenate(
        [nt(a[:, :128], first), nt(a[:, 128:C], second), nt(a, jnp.concatenate([left, right], axis=1))],
        axis=1,
    )


def gathered(a, rows):
    first, second, left, right = rows
    tail = nn(a[:, 768:], jnp.concatenate([left, right], axis=1))
    return jnp.concatenate(
        [nn(a[:, :512], first) + tail[:, :128], nn(a[:, 512:768], second) + tail[:, 128:]], axis=1
    )


def by_head(t, a):
    tail = nn(t, a[:, 768:])
    out = []
    for j in range(HEADS // 2):
        pair = nn(t[64 * j : 64 * j + 64], a[:, 256 * j : 256 * j + 256])
        for i in (2 * j, 2 * j + 1):
            r = (i % 2) * HD
            main = pair[r : r + HD, r * 4 : r * 4 + 128]
            out.append(jnp.concatenate([main, tail[i * HD : i * HD + HD, 16 * i : 16 * i + 16]], axis=1))
    return jnp.concatenate(out, axis=0)


def attend(x_ref, g_ref, us, bias, dbias, slot, gain, shift, wqkv, wqkv_t, wproj, wproj_t, raw_q, raw_p):
    n = WIN
    ws = range(len(us))

    def tokens(ref):
        rows = [jnp.concatenate([ref[u, 0], ref[u, 1]], axis=1) for u in us]
        return jnp.concatenate(rows, axis=0)[:, :C]

    def split(a):
        return [a[w * n : (w + 1) * n] for w in ws]

    x = tokens(x_ref)
    g = tokens(g_ref)
    gb = g.astype(BF16)
    center = x - jnp.mean(x, axis=1, keepdims=True)
    rstd = lax.rsqrt(jnp.mean(center * center, axis=1, keepdims=True) + EPS)
    xn = center * rstd
    h = (xn * gain + shift).astype(BF16)
    q = split(nn(h, wqkv[:, :C]).astype(BF16))
    kv = split(nn(h, wqkv[:, C:]).astype(BF16))
    k = [a[:, :C] for a in kv]
    v = [a[:, C:] for a in kv]
    do = split(nn(gb, wproj_t[...]).astype(BF16))
    k_t = [a.T for a in k]
    v_t = [a.T for a in v]
    h_t = h.T
    qr = [head_rows(a) for a in q]
    dor = [head_rows(a) for a in do]
    s = [across(k[w], qr[w]) for w in ws]
    dp = [across(v[w], dor[w]) for w in ws]
    pb, dsb = [], []
    for w in ws:
        ps, dss = [], []
        for b in range(7):
            lanes = slice(b * 128, b * 128 + 128)
            t = s[w][:, lanes] * (SCALE * LOG2E) + bias[slot, :, lanes]
            e = jnp.exp2(t - jnp.max(t, axis=0, keepdims=True))
            p = e * (1.0 / jnp.sum(e, axis=0, keepdims=True))
            d = dp[w][:, lanes]
            ds = p * (d - jnp.sum(p * d, axis=0, keepdims=True))
            dbias[slot, :, lanes] += ds
            ps.append(p.astype(BF16))
            dss.append((ds * SCALE).astype(BF16))
        pb.append(jnp.concatenate(ps, axis=1))
        dsb.append(jnp.concatenate(dss, axis=1))
    o_t = [by_head(v_t[w], pb[w]).astype(BF16) for w in ws]
    dq_t = [by_head(k_t[w], dsb[w]).astype(BF16) for w in ws]
    dv = jnp.concatenate([gathered(pb[w], dor[w]).astype(BF16) for w in ws], axis=0)
    dk = jnp.concatenate([gathered(dsb[w], qr[w]).astype(BF16) for w in ws], axis=0)
    o = jnp.concatenate([o_t[w].T for w in ws], axis=0)
    dq = jnp.concatenate([dq_t[w].T for w in ws], axis=0)
    a = nn(o, wproj[...]).astype(BF16)
    dh = nn(dq, wqkv_t[0:C]) + nn(dk, wqkv_t[C : 2 * C]) + nn(dv, wqkv_t[2 * C :])
    raw_p[...] += sum(nn(o_t[w], gb[w * n : (w + 1) * n]) for w in ws)
    raw_q[:, 0:C] += nn(h_t, dq)
    raw_q[:, C : 2 * C] += nn(h_t, dk)
    raw_q[:, 2 * C :] += nn(h_t, dv)
    dxn = dh * gain
    m1 = jnp.mean(dxn, axis=1, keepdims=True)
    m2 = jnp.mean(dxn * xn, axis=1, keepdims=True)
    dx = (rstd * (dxn - m1 - xn * m2)).astype(BF16)
    x = split(x + a.astype(F32))
    g = split(g + dx.astype(F32))
    for w, u in enumerate(us):
        x_ref[u, 0] = x[w][:, :128]
        x_ref[u, 1, :, 0:64] = x[w][:, 128:]
        g_ref[u, 0] = g[w][:, :128]
        g_ref[u, 1, :, 0:64] = g[w][:, 128:]


def copy_to(src, dst, send, recv, lat, lon):
    return pltpu.make_async_remote_copy(
        src_ref=src,
        dst_ref=dst,
        send_sem=send,
        recv_sem=recv,
        device_id=(lat, lon),
        device_id_type=MESH,
    )


def greet(lat, lon):
    barrier = pltpu.get_barrier_semaphore()
    pl.semaphore_signal(barrier, inc=1, device_id=(lat, lon), device_id_type=MESH)


def each(lo, hi, skip, act):
    def step(i, _):
        @pl.when(i != skip)
        def _():
            act(i)

        return 0

    lax.fori_loop(lo, hi, step, 0)


def kernel(
    lats,
    lons,
    x,
    g,
    gain_ref,
    shift_ref,
    wqkv,
    wproj,
    table,
    x_out,
    g_out,
    grad_q,
    grad_p,
    grad_bias,
    fx,
    fg,
    xw,
    gw,
    bias,
    dbias,
    rows_scratch,
    shifted,
    flat,
    wqkv_t,
    wproj_t,
    raw_q,
    raw_p,
    mine_w,
    part_w,
    part_w_in,
    tiles,
    tiles_in,
    joined,
    sum_w,
    mine_t,
    part_t,
    part_t_in,
    sum_t,
    squares,
    own_sem,
    halo_send,
    halo_recv,
    ret_send,
    ret_recv,
    w_send,
    w_recv,
    t_send,
    t_recv,
    tile_send,
    tile_recv,
    join_send,
    join_recv,
    wb_send,
    wb_recv,
    tb_send,
    tb_recv,
    sq_send,
    sq_recv,
):
    lat = lax.axis_index("lat")
    lon = lax.axis_index("lon")
    west = lax.rem(lon + lons - 1, lons)
    east = lax.rem(lon + 1, lons)
    first = lat == 0
    final = lat == lats - 1
    barrier = pltpu.get_barrier_semaphore()
    each(0, lons, lon, lambda o: greet(lat, o))
    each(0, lats, lat, lambda a: greet(a, lon))

    @pl.when(lat > 0)
    def _():
        greet(lat - 1, west)

    @pl.when(lat < lats - 1)
    def _():
        greet(lat + 1, east)

    pairs = ((x, fx), (g, fg))
    local = []
    for n, (src, frame) in enumerate(pairs):
        local.append(
            pltpu.make_async_copy(
                src.at[3:12, :, HALO:OWN], frame.at[3:12, :, HALO:OWN], own_sem.at[n]
            )
        )
    polar = []
    for n, (src, frame) in enumerate(pairs):
        polar.append(
            pltpu.make_async_copy(
                src.at[0:3, :, HALO:OWN], frame.at[0:3, :, HALO:OWN], own_sem.at[2 + n]
            )
        )
    for copy in local:
        copy.start()

    @pl.when(first)
    def _():
        for copy in polar:
            copy.start()

    wqkv_t[...] = wqkv[...].T
    wproj_t[...] = wproj[...].T

    ups, sides, diags = [], [], []
    for n, (src, frame) in enumerate(pairs):
        ups.append(
            copy_to(
                src.at[0:3, :, HALO:OWN],
                frame.at[12:15, :, HALO:OWN],
                halo_send.at[n],
                halo_recv.at[n],
                lat - 1,
                lon,
            )
        )
        sides.append(
            copy_to(
                src.at[:, :, 0:HALO],
                frame.at[0:12, :, OWN:FRAME],
                halo_send.at[2 + n],
                halo_recv.at[2 + n],
                lat,
                west,
            )
        )
        diags.append(
            copy_to(
                src.at[0:3, :, 0:HALO],
                frame.at[12:15, :, OWN:FRAME],
                halo_send.at[4 + n],
                halo_recv.at[4 + n],
                lat - 1,
                west,
            )
        )
    peers = lons - 1 + lats - 1
    pl.semaphore_wait(barrier, peers + jnp.where(lat > 0, 1, 0) + jnp.where(lat < lats - 1, 1, 0))
    for copy in sides:
        copy.start()

    @pl.when(lat > 0)
    def _():
        for copy in ups + diags:
            copy.start()

    pick = pick_matrix()
    rows_scratch[...] = jnp.zeros_like(rows_scratch)
    bias[:, :, 768:] = jnp.zeros((3, WIN, 128), F32)
    bias_in(table, flat, pick, rows_scratch, shifted, bias)
    dbias[...] = jnp.zeros_like(dbias)
    raw_q[...] = jnp.zeros_like(raw_q)
    raw_p[...] = jnp.zeros_like(raw_p)

    for copy in local:
        copy.wait()
    for copy in sides:
        copy.wait_recv()
    windows_in(fx, 3, 6, xw, 0)
    windows_in(fg, 3, 6, gw, 0)

    def halves_in(row, unit, slot, source, lo):
        halves(fx, row, xw, unit, False)
        halves(fg, row, gw, unit, False)
        for i in range(HEADS):
            part = get_head(bias, source, i)[lo : lo + HALF, lo : lo + HALF]
            away = jnp.full((HALF, HALF), -1e9, F32)
            top = jnp.concatenate([part, away], axis=1)
            low = jnp.concatenate([away, part], axis=1)
            put_head(bias, slot, i, jnp.concatenate([top, low], axis=0))

    def halves_out(row, unit, slot, target, lo):
        halves(fx, row, xw, unit, True)
        halves(fg, row, gw, unit, True)
        zero = jnp.zeros((HALF, HALF), F32)
        for i in range(HEADS):
            both = get_head(dbias, slot, i)
            part = both[:HALF, :HALF] + both[HALF:, HALF:]
            part = jnp.concatenate([zero, part] if lo else [part, zero], axis=1)
            none = jnp.zeros((HALF, WIN), F32)
            part = jnp.concatenate([none, part] if lo else [part, none], axis=0)
            old = get_head(dbias, target, i) if target != slot else 0.0
            put_head(dbias, target, i, old + part)

    @pl.when(first)
    def _():
        for copy in polar:
            copy.wait()
        halves_in(0, 2 * WPB, 2, 0, HALF)

    @pl.when(final)
    def _():
        halves_in(9, WPB, 1, 1, 0)

    rest = (gain_ref[...], shift_ref[...], wqkv, wqkv_t, wproj, wproj_t, raw_q, raw_p)
    full = 2 * WPB // GROUP
    half = WPB // 2 // GROUP

    def group(u, _):
        @pl.when((u == full // 2) & (lat < lats - 1))
        def _():
            for copy in ups + diags:
                copy.wait_recv()
            windows_in(fx, 9, 6, xw, WPB)
            windows_in(fg, 9, 6, gw, WPB)

        slot = jnp.minimum(u // (WPB // GROUP), 2)
        attend(xw, gw, [GROUP * u + r for r in range(GROUP)], bias, dbias, slot, *rest)
        return 0

    lax.fori_loop(0, jnp.where(first, full + half, jnp.where(final, full // 2 + half, full)), group, 0)

    raw = jnp.concatenate([raw_q[...], raw_p[...]], axis=1)
    for j in range(lons):
        row = []
        for t in range(TILES):
            col = j * TILES + t
            r, c = col // 6 * 16, col % 6 * 128
            row.append(raw[r : r + 16, c : c + 128])
        chunk = jnp.concatenate(row, axis=1)
        mine_w[j] = chunk
        part_w[j] = chunk.astype(BF16)

    def w_out(o):
        return copy_to(part_w.at[o], part_w_in.at[lon], w_send.at[o], w_recv.at[lon], lat, o)

    def w_in(o):
        return copy_to(part_w.at[o], part_w_in.at[o], w_send.at[o], w_recv.at[o], lat, o)

    each(0, lons, lon, lambda o: w_out(o).start())

    @pl.when(lat < lats - 1)
    def _():
        windows_out(fx, 9, 6, xw, WPB)
        windows_out(fg, 9, 6, gw, WPB)

    downs, crosses = [], []
    for n, frame in enumerate((fx, fg)):
        downs.append(
            copy_to(
                frame.at[12:15, :, HALO:OWN],
                frame.at[0:3, :, HALO:OWN],
                ret_send.at[n],
                ret_recv.at[n],
                lat + 1,
                lon,
            )
        )
        crosses.append(
            copy_to(
                frame.at[12:15, :, OWN:FRAME],
                frame.at[0:3, :, 0:HALO],
                ret_send.at[4 + n],
                ret_recv.at[4 + n],
                lat + 1,
                east,
            )
        )

    @pl.when(lat < lats - 1)
    def _():
        for copy in downs + crosses:
            copy.start()

    windows_out(fx, 3, 6, xw, 0)
    windows_out(fg, 3, 6, gw, 0)

    @pl.when(first)
    def _():
        halves_out(0, 2 * WPB, 2, 0, HALF)

    @pl.when(final)
    def _():
        halves_out(9, WPB, 1, 1, 0)

    backs, tops = [], []
    for n, frame in enumerate((fx, fg)):
        backs.append(
            copy_to(
                frame.at[3:12, :, OWN:FRAME],
                frame.at[3:12, :, 0:HALO],
                ret_send.at[2 + n],
                ret_recv.at[2 + n],
                lat,
                east,
            )
        )
        tops.append(
            copy_to(
                frame.at[0:3, :, OWN:FRAME],
                frame.at[0:3, :, 0:HALO],
                ret_send.at[6 + n],
                ret_recv.at[6 + n],
                lat,
                east,
            )
        )
    for copy in backs:
        copy.start()

    @pl.when(first)
    def _():
        for copy in tops:
            copy.start()

    grads = bias_out(dbias, pick, shifted, rows_scratch)
    for j in range(lons):
        chunk = grads[:, j * TCHUNK : (j + 1) * TCHUNK]
        mine_t[j] = chunk
        part_t[j] = chunk.astype(BF16)

    def t_out(o):
        return copy_to(part_t.at[o], part_t_in.at[lon], t_send.at[o], t_recv.at[lon], lat, o)

    def t_in(o):
        return copy_to(part_t.at[o], part_t_in.at[o], t_send.at[o], t_recv.at[o], lat, o)

    each(0, lons, lon, lambda o: t_out(o).start())

    def add_w(d, total):
        o = lax.rem(lon + d, lons)
        w_in(o).wait_recv()
        return total + part_w_in[o].astype(F32)

    total = lax.fori_loop(1, lons, add_w, mine_w[lon])
    for t in range(TILES):
        tiles[t] = total[:, t * 128 : t * 128 + 128].astype(BF16)

    def tile_out(a):
        return copy_to(tiles.at[a], tiles_in.at[lat], tile_send.at[a], tile_recv.at[lat], a, lon)

    def tile_in(a):
        return copy_to(tiles.at[0], tiles_in.at[a], tile_send.at[0], tile_recv.at[a], a, lon)

    each(0, TILES, lat, lambda a: tile_out(a).start())

    def add_t(d, total):
        o = lax.rem(lon + d, lons)
        t_in(o).wait_recv()
        return total + part_t_in[o].astype(F32)

    sum_t[lon] = lax.fori_loop(1, lons, add_t, mine_t[lon]).astype(BF16)

    def tb_out(o):
        return copy_to(sum_t.at[lon], sum_t.at[lon], tb_send.at[o], tb_recv.at[lon], lat, o)

    def tb_in(o):
        return copy_to(sum_t.at[o], sum_t.at[o], tb_send.at[o], tb_recv.at[o], lat, o)

    each(0, lons, lon, lambda o: tb_out(o).start())

    def join_out(a):
        return copy_to(joined.at[lat], joined.at[lat], join_send.at[a], join_recv.at[lat], a, lon)

    def join_in(a):
        return copy_to(joined.at[a], joined.at[a], join_send.at[a], join_recv.at[a], a, lon)

    @pl.when(lat < TILES)
    def _():
        def add_tile(d, total):
            a = lax.rem(lat + d, lats)
            tile_in(a).wait_recv()
            return total + tiles_in[a].astype(F32)

        total = lax.fori_loop(1, lats, add_tile, tiles[lat].astype(F32))
        joined[lat] = total.astype(BF16)
        each(0, lats, lat, lambda a: join_out(a).start())

    each(0, lons, lon, lambda o: tb_in(o).wait_recv())
    whole = jnp.concatenate([sum_t[j].astype(F32) for j in range(lons)], axis=1)
    square = jnp.sum(whole * whole).reshape(1, 1)
    squares[lat] = jnp.broadcast_to(square, (8, 128))

    def sq_out(a):
        return copy_to(squares.at[lat], squares.at[lat], sq_send.at[a], sq_recv.at[lat], a, lon)

    def sq_in(a):
        return copy_to(squares.at[a], squares.at[a], sq_send.at[a], sq_recv.at[a], a, lon)

    each(0, lats, lat, lambda a: sq_out(a).start())

    each(0, TILES, lat, lambda a: join_in(a).wait_recv())
    sum_w[lon] = jnp.concatenate([joined[t] for t in range(TILES)], axis=1)

    def wb_out(o):
        return copy_to(sum_w.at[lon], sum_w.at[lon], wb_send.at[o], wb_recv.at[lon], lat, o)

    def wb_in(o):
        return copy_to(sum_w.at[o], sum_w.at[o], wb_send.at[o], wb_recv.at[o], lat, o)

    each(0, lons, lon, lambda o: wb_out(o).start())

    for copy in backs:
        copy.wait()

    @pl.when(lat > 0)
    def _():
        for copy in downs + crosses:
            copy.wait_recv()

    @pl.when(lat < lats - 1)
    def _():
        for copy in downs + crosses:
            copy.wait_send()

    @pl.when(first)
    def _():
        for copy in tops:
            copy.wait()

    leave = [
        pltpu.make_async_copy(frame.at[0:12, :, 0:OWN], out, own_sem.at[n])
        for n, (frame, out) in enumerate(((fx, x_out), (fg, g_out)))
    ]
    for copy in leave:
        copy.start()

    each(0, lats, lat, lambda a: sq_in(a).wait_recv())
    table_squares = jnp.zeros((1, 1), F32)
    for a in range(lats):
        table_squares = table_squares + squares[a][0:1, 0:1]
    table_rms = jnp.sqrt(table_squares / (lats * 2 * HEADS * POS) + 1e-6)
    whole = whole[:, :POS] / table_rms
    for i in range(HEADS):
        grad_bias[i] = whole[2 * i : 2 * i + 2]

    each(0, lons, lon, lambda o: wb_in(o).wait_recv())
    cols = []
    square = jnp.zeros((16, 128), F32)
    for j in range(lons):
        for t in range(TILES):
            piece = sum_w[j, :, t * 128 : t * 128 + 128].astype(F32)
            square = square + piece * piece
            cols.append(piece)
    rms = jnp.sqrt(jnp.sum(square).reshape(1, 1) / (4 * C * C) + 1e-6)
    inverse = 1.0 / rms
    for r in range(12):
        row = jnp.concatenate(cols[r * 6 : r * 6 + 6], axis=1) * inverse
        grad_q[r * 16 : r * 16 + 16] = row[:, : 3 * C]
        grad_p[r * 16 : r * 16 + 16] = row[:, 3 * C :]

    def sent(o):
        w_out(o).wait_send()
        t_out(o).wait_send()
        tb_out(o).wait_send()
        wb_out(o).wait_send()

    each(0, lons, lon, sent)
    each(0, TILES, lat, lambda a: tile_out(a).wait_send())
    each(0, lats, lat, lambda a: sq_out(a).wait_send())

    @pl.when(lat < TILES)
    def _():
        each(0, lats, lat, lambda a: join_out(a).wait_send())

    for copy in sides:
        copy.wait_send()

    @pl.when(lat > 0)
    def _():
        for copy in ups + diags:
            copy.wait_send()

    for copy in leave:
        copy.wait()


def on_device(inputs, cotangent, norm_gain, norm_shift, w_qkv, w_proj, bias_table):
    lats = lax.axis_size("lat")
    lons = lax.axis_size("lon")
    vmem = pl.BlockSpec(memory_space=pltpu.VMEM)
    hbm = pl.BlockSpec(memory_space=pl.ANY)
    shape = jax.ShapeDtypeStruct
    units = 2 * WPB + WPB // 2
    sems = pltpu.SemaphoreType.DMA
    counts = [4, 6, 6, 8, 8] + [lons] * 4 + [lats] * 4 + [lons] * 4 + [lats] * 2
    x_out, g_out, grad_q, grad_p, grad_bias = pl.pallas_call(
        functools.partial(kernel, lats, lons),
        in_specs=[hbm, hbm] + [vmem] * 5,
        out_specs=[hbm, hbm] + [vmem] * 3,
        out_shape=[
            shape((12, 2, OWN), BF16),
            shape((12, 2, OWN), BF16),
            shape((C, 3 * C), F32),
            shape((C, C), F32),
            shape((HEADS, 2, POS), F32),
        ],
        scratch_shapes=[
            pltpu.VMEM((FROWS, 2, FRAME), BF16),
            pltpu.VMEM((FROWS, 2, FRAME), BF16),
            pltpu.VMEM((units, 2, WIN, 128), F32),
            pltpu.VMEM((units, 2, WIN, 128), F32),
            pltpu.VMEM((3, WIN, 896), F32),
            pltpu.VMEM((3, WIN, 896), F32),
            pltpu.VMEM((12, 16, ROWPAD), F32),
            pltpu.VMEM((3, WIN, 128), F32),
            pltpu.VMEM((16, 3328), F32),
            pltpu.VMEM((3 * C, C), BF16),
            pltpu.VMEM((C, C), BF16),
            pltpu.VMEM((C, 3 * C), F32),
            pltpu.VMEM((C, C), F32),
            pltpu.VMEM((lons, 16, WCHUNK), F32),
            pltpu.VMEM((lons, 16, WCHUNK), BF16),
            pltpu.VMEM((lons, 16, WCHUNK), BF16),
            pltpu.VMEM((TILES, 16, 128), BF16),
            pltpu.VMEM((lats, 16, 128), BF16),
            pltpu.VMEM((TILES, 16, 128), BF16),
            pltpu.VMEM((lons, 16, WCHUNK), BF16),
            pltpu.VMEM((lons, 16, TCHUNK), F32),
            pltpu.VMEM((lons, 16, TCHUNK), BF16),
            pltpu.VMEM((lons, 16, TCHUNK), BF16),
            pltpu.VMEM((lons, 16, TCHUNK), BF16),
            pltpu.VMEM((lats, 8, 128), F32),
        ]
        + [sems((n,)) for n in counts],
        compiler_params=pltpu.CompilerParams(
            collective_id=0, has_side_effects=True, vmem_limit_bytes=56 * 2**20
        ),
        name="windows",
    )(
        inputs.transpose(1, 0, 2),
        cotangent.transpose(1, 0, 2),
        norm_gain.reshape(1, C),
        norm_shift.reshape(1, C),
        w_qkv,
        w_proj,
        bias_table.transpose(1, 0, 2),
    )
    x_out, g_out, grad_bias = (a.transpose(1, 0, 2) for a in (x_out, g_out, grad_bias))
    return x_out, g_out, grad_q, grad_p, grad_bias


def solution(mesh):
    return jax.shard_map(
        on_device,
        mesh=mesh,
        in_specs=(
            P(None, "lat", "lon"),
            P(None, "lat", "lon"),
            P(),
            P(),
            P(),
            P(),
            P("lat", None, None),
        ),
        out_specs=(P(None, "lat", "lon"), P(None, "lat", "lon"), P(), P(), P("lat", None, None)),
        check_vma=False,
    )
```

```python
import functools
import math

import jax
import jax.numpy as jnp
import numpy as np
from jax import lax
from jax.experimental import pallas as pl
from jax.experimental.pallas import tpu as pltpu
from jax.sharding import PartitionSpec as P

C = 192
HEADS = 6
HD = 32
WLON = 12
WIN = 144
HALF = 72
SPAN = 23
ROWLEN = 12 * SPAN
ROWPAD = 384
COLS = 96
HALO = 6 * C
WLANES = WLON * C
OWN = COLS * C
FRAME = OWN + HALO
FROWS = 15
GROUP = 4
WPB = 8
POS = 3312
TABLE = 4096
WCHUNK = 12 * 768 // 8
TCHUNK = TABLE // 8
TILES = WCHUNK // 128
MESH = pl.DeviceIdType.MESH
EPS = 1e-5
SCALE = HD**-0.5
LOG2E = math.log2(math.e)
F32 = jnp.float32
BF16 = jnp.bfloat16


def nn(a, b):
    return lax.dot_general(a, b, (((1,), (0,)), ((), ())), preferred_element_type=F32)


def nt(a, b):
    return lax.dot_general(a, b, (((1,), (1,)), ((), ())), preferred_element_type=F32)


def tn(a, b):
    return lax.dot_general(a, b, (((0,), (0,)), ((), ())), preferred_element_type=F32)


def pick_matrix():
    row = lax.broadcasted_iota(jnp.int32, (WIN, 1), 0)
    lk = lax.rem(row, WLON)
    block = lax.div(row, WLON)
    kb = lax.rem(block, 2) * 6 + lax.div(block, 2)
    col = lax.broadcasted_iota(jnp.int32, (WIN, ROWPAD), 1)
    return jnp.where(col == kb * SPAN + 11 - lk, 1.0, 0.0).astype(BF16)


def windows_in(frame, row, count, tokens, first, half=0, lo=0, hi=WPB):
    def window(w, _):
        base = HALO + (2 * w + half // HALF if count == 3 else w) * WLANES
        for m in range(6):
            at = pl.multiple_of(base + m * 2 * C, 128)
            slab = frame[row : row + count, :, pl.ds(at, 2 * C)].astype(F32).reshape(2 * count, 2 * C)
            even = slab[:, :C]
            odd = slab[:, C:]
            for n, part in ((2 * m, even), (2 * m + 1, odd)):
                slots = pl.ds(half + n, 2 * count, stride=WLON)
                tokens[first + w, 0, slots, :] = part[:, :128]
                tokens[first + w, 1, slots, :] = jnp.concatenate([part[:, 128:], part[:, 128:]], axis=1)
        return 0

    lax.fori_loop(lo, WPB // 2 if count == 3 else hi, window, 0)


def windows_out(frame, row, count, tokens, first, half=0):
    def window(w, _):
        base = HALO + (2 * w + half // HALF if count == 3 else w) * WLANES
        for p in range(count):
            for m in range(6):
                at = pl.multiple_of(base + m * 2 * C, 128)
                parts = []
                for n in (2 * m, 2 * m + 1):
                    slots = pl.ds(half + p * 24 + n, 2, stride=WLON)
                    parts.append(tokens[first + w, 0, slots, :])
                    parts.append(tokens[first + w, 1, slots, :][:, : C - 128])
                frame[row + p, :, pl.ds(at, 2 * C)] = jnp.concatenate(parts, axis=1).astype(BF16)
        return 0

    lax.fori_loop(0, WPB // 2 if count == 3 else WPB, window, 0)


def halves(frame, row, tokens, first, out):
    move = windows_out if out else windows_in
    move(frame, row, 3, tokens, first, 0)
    move(frame, row, 3, tokens, first, HALF)


def put_head(ref, slot, i, value):
    ref[slot, :, i * 128 : i * 128 + 128] = value[:, :128]
    ref[slot, :, 768 + i * 16 : 768 + i * 16 + 16] = value[:, 128:]


def get_head(ref, slot, i):
    tail = ref[slot, :, 768 + i * 16 : 768 + i * 16 + 16]
    return jnp.concatenate([ref[slot, :, i * 128 : i * 128 + 128], tail], axis=1)


def bias_rows(table, flat, rows_scratch):
    rows_scratch[...] = jnp.zeros_like(rows_scratch)
    for i in range(HEADS):
        flat[2 * i : 2 * i + 2, 0:POS] = table[i]
    for zq in range(2):
        for pq in range(6):
            at = (zq * 6 + pq) * ROWLEN
            rows_scratch[pq * 2 + zq, 0:12, 0:ROWLEN] = flat[0:12, at : at + ROWLEN]


def bias_in(lo, hi, pick, rows_scratch, shifted, bias):
    for n in range(lo, hi):
        rows = rows_scratch[:, n, :]
        rows = jnp.concatenate([rows, jnp.zeros((4, ROWPAD), F32)], axis=0)
        for lq in range(WLON):
            moved = pltpu.roll(rows, (ROWPAD - lq) % ROWPAD, 1) if lq else rows
            for t in range(3):
                shifted[t, pl.ds(lq, 12, stride=12), :] = moved[:12, t * 128 : t * 128 + 128]
        full = jnp.concatenate([shifted[t] for t in range(3)], axis=1)
        high = full.astype(BF16)
        low = (full - high.astype(F32)).astype(BF16)
        total = nt(pick, high) + nt(pick, low)
        put_head(bias, n % 2, n // 2, total * LOG2E)


def bias_out(grads, pick, shifted, rows_scratch):
    for n in range(12):
        full = nn(get_head(grads, n % 2, n // 2).astype(BF16).T, pick)
        for t in range(3):
            shifted[t] = full[:, t * 128 : t * 128 + 128]
        total = jnp.zeros((16, ROWPAD), F32)
        for lq in range(WLON):
            rows = [shifted[t, pl.ds(lq, 12, stride=12), :] for t in range(3)]
            rows = jnp.concatenate(rows, axis=1)
            rows = jnp.concatenate([rows, jnp.zeros((4, ROWPAD), F32)], axis=0)
            total = total + (pltpu.roll(rows, lq, 1) if lq else rows)
        rows_scratch[:, n, :] = total[:12]
    parts = [rows_scratch[pq * 2 + zq][:, :ROWLEN] for zq in range(2) for pq in range(6)]
    parts.append(jnp.zeros((16, TABLE - POS), F32))
    return jnp.concatenate(parts, axis=1)


def head_rows(a):
    lane = lax.broadcasted_iota(jnp.int32, (1, 128), 1) // HD
    zero = jnp.zeros((), BF16)

    def only(part, i):
        return jnp.where(lane[:, : part.shape[1]] == i % 4, part, zero)

    wide, slim = a[:, :128], a[:, 128:C]
    first = jnp.concatenate([only(wide[:128], i) for i in range(4)], axis=0)
    second = jnp.concatenate([only(slim[:128], i) for i in range(4, HEADS)], axis=0)
    tail = [only(wide[128:], i) for i in range(4)]
    left = jnp.concatenate(tail + [jnp.zeros((64, 128), BF16)], axis=0)
    tail = [only(slim[128:], i) for i in range(4, HEADS)]
    right = jnp.concatenate([jnp.zeros((64, 64), BF16)] + tail + [jnp.zeros((32, 64), BF16)], axis=0)
    return first, second, left, right


def across(a, rows):
    first, second, left, right = rows
    return jnp.concatenate(
        [nt(a[:, :128], first), nt(a[:, 128:C], second), nt(a, jnp.concatenate([left, right], axis=1))],
        axis=1,
    )


def gathered(a, rows):
    first, second, left, right = rows
    tail = nn(a[:, 768:], jnp.concatenate([left, right], axis=1))
    return jnp.concatenate(
        [nn(a[:, :512], first) + tail[:, :128], nn(a[:, 512:768], second) + tail[:, 128:]], axis=1
    )


def by_head(t, a):
    tail = nn(t, a[:, 768:])
    out = []
    for j in range(HEADS // 2):
        pair = nn(t[64 * j : 64 * j + 64], a[:, 256 * j : 256 * j + 256])
        for i in (2 * j, 2 * j + 1):
            r = (i % 2) * HD
            main = pair[r : r + HD, r * 4 : r * 4 + 128]
            out.append(jnp.concatenate([main, tail[i * HD : i * HD + HD, 16 * i : 16 * i + 16]], axis=1))
    return jnp.concatenate(out, axis=0)


def attend(x_ref, g_ref, us, bias, dbias, slot, gain, shift, wqkv, wqkv_t, wproj, wproj_t, raw_q, raw_p):
    n = WIN
    ws = range(len(us))

    def tokens(ref):
        rows = [jnp.concatenate([ref[u, 0], ref[u, 1]], axis=1) for u in us]
        return jnp.concatenate(rows, axis=0)[:, :C]

    def split(a):
        return [a[w * n : (w + 1) * n] for w in ws]

    x = tokens(x_ref)
    g = tokens(g_ref)
    gb = g.astype(BF16)
    center = x - jnp.mean(x, axis=1, keepdims=True)
    rstd = lax.rsqrt(jnp.mean(center * center, axis=1, keepdims=True) + EPS)
    xn = center * rstd
    h = (xn * gain + shift).astype(BF16)
    q = split(nn(h, wqkv[:, :C]).astype(BF16))
    kv = split(nn(h, wqkv[:, C:]).astype(BF16))
    k = [a[:, :C] for a in kv]
    v = [a[:, C:] for a in kv]
    do = split(nn(gb, wproj_t[...]).astype(BF16))
    k_t = [a.T for a in k]
    v_t = [a.T for a in v]
    h_t = h.T
    qr = [head_rows(a) for a in q]
    dor = [head_rows(a) for a in do]
    s = [across(k[w], qr[w]) for w in ws]
    dp = [across(v[w], dor[w]) for w in ws]
    pb, dsb = [], []
    for w in ws:
        ps, dss = [], []
        for b in range(7):
            lanes = slice(b * 128, b * 128 + 128)
            t = s[w][:, lanes] * (SCALE * LOG2E) + bias[slot, :, lanes]
            e = jnp.exp2(t - jnp.max(t, axis=0, keepdims=True))
            p = e * (1.0 / jnp.sum(e, axis=0, keepdims=True))
            d = dp[w][:, lanes]
            ds = p * (d - jnp.sum(p * d, axis=0, keepdims=True))
            dbias[slot, :, lanes] += ds
            ps.append(p.astype(BF16))
            dss.append((ds * SCALE).astype(BF16))
        pb.append(jnp.concatenate(ps, axis=1))
        dsb.append(jnp.concatenate(dss, axis=1))
    o_t = [by_head(v_t[w], pb[w]).astype(BF16) for w in ws]
    dq_t = [by_head(k_t[w], dsb[w]).astype(BF16) for w in ws]
    dv = jnp.concatenate([gathered(pb[w], dor[w]).astype(BF16) for w in ws], axis=0)
    dk = jnp.concatenate([gathered(dsb[w], qr[w]).astype(BF16) for w in ws], axis=0)
    o = jnp.concatenate([o_t[w].T for w in ws], axis=0)
    dq = jnp.concatenate([dq_t[w].T for w in ws], axis=0)
    a = nn(o, wproj[...]).astype(BF16)
    dh = nn(dq, wqkv_t[0:C]) + nn(dk, wqkv_t[C : 2 * C]) + nn(dv, wqkv_t[2 * C :])
    raw_p[...] += sum(nn(o_t[w], gb[w * n : (w + 1) * n]) for w in ws)
    raw_q[:, 0:C] += nn(h_t, dq)
    raw_q[:, C : 2 * C] += nn(h_t, dk)
    raw_q[:, 2 * C :] += nn(h_t, dv)
    dxn = dh * gain
    m1 = jnp.mean(dxn, axis=1, keepdims=True)
    m2 = jnp.mean(dxn * xn, axis=1, keepdims=True)
    dx = (rstd * (dxn - m1 - xn * m2)).astype(BF16)
    x = split(x + a.astype(F32))
    g = split(g + dx.astype(F32))
    for w, u in enumerate(us):
        x_ref[u, 0] = x[w][:, :128]
        x_ref[u, 1, :, 0:64] = x[w][:, 128:]
        g_ref[u, 0] = g[w][:, :128]
        g_ref[u, 1, :, 0:64] = g[w][:, 128:]


def copy_to(src, dst, send, recv, lat, lon):
    return pltpu.make_async_remote_copy(
        src_ref=src,
        dst_ref=dst,
        send_sem=send,
        recv_sem=recv,
        device_id=(lat, lon),
        device_id_type=MESH,
    )


def greet(lat, lon):
    barrier = pltpu.get_barrier_semaphore()
    pl.semaphore_signal(barrier, inc=1, device_id=(lat, lon), device_id_type=MESH)


def each(lo, hi, skip, act):
    def step(i, _):
        @pl.when(i != skip)
        def _():
            act(i)

        return 0

    lax.fori_loop(lo, hi, step, 0)


def kernel(
    lats,
    lons,
    x,
    g,
    gain_ref,
    shift_ref,
    wqkv,
    wproj,
    table,
    x_out,
    g_out,
    grad_q,
    grad_p,
    grad_bias,
    fx,
    fg,
    xw,
    gw,
    bias,
    dbias,
    rows_scratch,
    shifted,
    flat,
    wqkv_t,
    wproj_t,
    raw_q,
    raw_p,
    mine_w,
    part_w,
    part_w_in,
    tiles,
    tiles_in,
    joined,
    sum_w,
    mine_t,
    part_t,
    part_t_in,
    sum_t,
    squares,
    own_sem,
    halo_send,
    halo_recv,
    ret_send,
    ret_recv,
    w_send,
    w_recv,
    t_send,
    t_recv,
    tile_send,
    tile_recv,
    join_send,
    join_recv,
    wb_send,
    wb_recv,
    tb_send,
    tb_recv,
    sq_send,
    sq_recv,
):
    lat = lax.axis_index("lat")
    lon = lax.axis_index("lon")
    west = lax.rem(lon + lons - 1, lons)
    east = lax.rem(lon + 1, lons)
    first = lat == 0
    final = lat == lats - 1
    barrier = pltpu.get_barrier_semaphore()
    each(0, lons, lon, lambda o: greet(lat, o))
    each(0, lats, lat, lambda a: greet(a, lon))

    @pl.when(lat > 0)
    def _():
        greet(lat - 1, west)

    @pl.when(lat < lats - 1)
    def _():
        greet(lat + 1, east)

    pairs = ((x, fx), (g, fg))
    local = []
    for n, (src, frame) in enumerate(pairs):
        local.append(
            pltpu.make_async_copy(
                src.at[3:12, :, HALO:OWN], frame.at[3:12, :, HALO:OWN], own_sem.at[n]
            )
        )
    polar = []
    for n, (src, frame) in enumerate(pairs):
        polar.append(
            pltpu.make_async_copy(
                src.at[0:3, :, HALO:OWN], frame.at[0:3, :, HALO:OWN], own_sem.at[2 + n]
            )
        )
    for copy in local:
        copy.start()

    @pl.when(first)
    def _():
        for copy in polar:
            copy.start()

    wqkv_t[...] = wqkv[...].T
    wproj_t[...] = wproj[...].T

    ups, sides, diags = [], [], []
    for n, (src, frame) in enumerate(pairs):
        ups.append(
            copy_to(
                src.at[0:3, :, HALO:OWN],
                frame.at[12:15, :, HALO:OWN],
                halo_send.at[n],
                halo_recv.at[n],
                lat - 1,
                lon,
            )
        )
        sides.append(
            copy_to(
                src.at[:, :, 0:HALO],
                frame.at[0:12, :, OWN:FRAME],
                halo_send.at[2 + n],
                halo_recv.at[2 + n],
                lat,
                west,
            )
        )
        diags.append(
            copy_to(
                src.at[0:3, :, 0:HALO],
                frame.at[12:15, :, OWN:FRAME],
                halo_send.at[4 + n],
                halo_recv.at[4 + n],
                lat - 1,
                west,
            )
        )
    pick = pick_matrix()
    bias[:, :, 768:] = jnp.zeros((3, WIN, 128), F32)
    bias_rows(table, flat, rows_scratch)
    bias_in(0, 6, pick, rows_scratch, shifted, bias)
    peers = lons - 1 + lats - 1
    pl.semaphore_wait(barrier, peers + jnp.where(lat > 0, 1, 0) + jnp.where(lat < lats - 1, 1, 0))
    for copy in sides:
        copy.start()

    @pl.when(lat > 0)
    def _():
        for copy in ups + diags:
            copy.start()

    bias_in(6, 12, pick, rows_scratch, shifted, bias)
    dbias[...] = jnp.zeros_like(dbias)
    raw_q[...] = jnp.zeros_like(raw_q)
    raw_p[...] = jnp.zeros_like(raw_p)

    for copy in local:
        copy.wait()
    windows_in(fx, 3, 6, xw, 0, 0, 0, WPB - 1)
    windows_in(fg, 3, 6, gw, 0, 0, 0, WPB - 1)
    for copy in sides:
        copy.wait_recv()
    windows_in(fx, 3, 6, xw, 0, 0, WPB - 1)
    windows_in(fg, 3, 6, gw, 0, 0, WPB - 1)

    def halves_in(row, unit, slot, source, lo):
        halves(fx, row, xw, unit, False)
        halves(fg, row, gw, unit, False)
        for i in range(HEADS):
            part = get_head(bias, source, i)[lo : lo + HALF, lo : lo + HALF]
            away = jnp.full((HALF, HALF), -1e9, F32)
            top = jnp.concatenate([part, away], axis=1)
            low = jnp.concatenate([away, part], axis=1)
            put_head(bias, slot, i, jnp.concatenate([top, low], axis=0))

    def halves_grad(slot, target, lo):
        zero = jnp.zeros((HALF, HALF), F32)
        for i in range(HEADS):
            both = get_head(dbias, slot, i)
            part = both[:HALF, :HALF] + both[HALF:, HALF:]
            part = jnp.concatenate([zero, part] if lo else [part, zero], axis=1)
            none = jnp.zeros((HALF, WIN), F32)
            part = jnp.concatenate([none, part] if lo else [part, none], axis=0)
            old = get_head(dbias, target, i) if target != slot else 0.0
            put_head(dbias, target, i, old + part)

    @pl.when(first)
    def _():
        for copy in polar:
            copy.wait()
        halves_in(0, 2 * WPB, 2, 0, HALF)

    @pl.when(final)
    def _():
        halves_in(9, WPB, 1, 1, 0)

    rest = (gain_ref[...], shift_ref[...], wqkv, wqkv_t, wproj, wproj_t, raw_q, raw_p)
    full = 2 * WPB // GROUP
    half = WPB // 2 // GROUP

    def group(u, _):
        @pl.when((u == full // 2) & (lat < lats - 1))
        def _():
            for copy in ups + diags:
                copy.wait_recv()
            windows_in(fx, 9, 6, xw, WPB)
            windows_in(fg, 9, 6, gw, WPB)

        slot = jnp.minimum(u // (WPB // GROUP), 2)
        attend(xw, gw, [GROUP * u + r for r in range(GROUP)], bias, dbias, slot, *rest)
        return 0

    lax.fori_loop(0, jnp.where(first, full + half, jnp.where(final, full // 2 + half, full)), group, 0)

    raw = jnp.concatenate([raw_q[...], raw_p[...]], axis=1)
    for j in range(lons):
        row = []
        for t in range(TILES):
            col = j * TILES + t
            r, c = col // 6 * 16, col % 6 * 128
            row.append(raw[r : r + 16, c : c + 128])
        chunk = jnp.concatenate(row, axis=1)
        mine_w[j] = chunk
        part_w[j] = chunk.astype(BF16)

    def w_out(o):
        return copy_to(part_w.at[o], part_w_in.at[lon], w_send.at[o], w_recv.at[lon], lat, o)

    def w_in(o):
        return copy_to(part_w.at[o], part_w_in.at[o], w_send.at[o], w_recv.at[o], lat, o)

    each(0, lons, lon, lambda o: w_out(o).start())

    @pl.when(first)
    def _():
        halves_grad(2, 0, HALF)

    @pl.when(final)
    def _():
        halves_grad(1, 1, 0)

    grads = bias_out(dbias, pick, shifted, rows_scratch)
    for j in range(lons):
        chunk = grads[:, j * TCHUNK : (j + 1) * TCHUNK]
        mine_t[j] = chunk
        part_t[j] = chunk.astype(BF16)

    def t_out(o):
        return copy_to(part_t.at[o], part_t_in.at[lon], t_send.at[o], t_recv.at[lon], lat, o)

    def t_in(o):
        return copy_to(part_t.at[o], part_t_in.at[o], t_send.at[o], t_recv.at[o], lat, o)

    each(0, lons, lon, lambda o: t_out(o).start())

    downs, crosses, backs, tops = [], [], [], []
    for n, frame in enumerate((fx, fg)):
        rows = frame.at[0:3, :, HALO:OWN]
        side = frame.at[3:12, :, 0:HALO]
        corner = frame.at[0:3, :, 0:HALO]
        sems = [(ret_send.at[2 * r + n], ret_recv.at[2 * r + n]) for r in range(4)]
        downs.append(copy_to(frame.at[12:15, :, HALO:OWN], rows, *sems[0], lat + 1, lon))
        crosses.append(copy_to(frame.at[12:15, :, OWN:FRAME], corner, *sems[1], lat + 1, east))
        backs.append(copy_to(frame.at[3:12, :, OWN:FRAME], side, *sems[2], lat, east))
        tops.append(copy_to(frame.at[0:3, :, OWN:FRAME], corner, *sems[3], lat, east))

    @pl.when(lat < lats - 1)
    def _():
        windows_out(fx, 9, 6, xw, WPB)
        windows_out(fg, 9, 6, gw, WPB)
        for copy in downs + crosses:
            copy.start()

    def add_w(d, total):
        o = lax.rem(lon + d, lons)
        w_in(o).wait_recv()
        return total + part_w_in[o].astype(F32)

    total = lax.fori_loop(1, lons, add_w, mine_w[lon])
    for t in range(TILES):
        tiles[t] = total[:, t * 128 : t * 128 + 128].astype(BF16)

    def tile_out(a):
        return copy_to(tiles.at[a], tiles_in.at[lat], tile_send.at[a], tile_recv.at[lat], a, lon)

    def tile_in(a):
        return copy_to(tiles.at[0], tiles_in.at[a], tile_send.at[0], tile_recv.at[a], a, lon)

    each(0, TILES, lat, lambda a: tile_out(a).start())

    windows_out(fx, 3, 6, xw, 0)
    windows_out(fg, 3, 6, gw, 0)

    @pl.when(first)
    def _():
        halves(fx, 0, xw, 2 * WPB, True)
        halves(fg, 0, gw, 2 * WPB, True)
        for copy in tops:
            copy.start()

    @pl.when(final)
    def _():
        halves(fx, 9, xw, WPB, True)
        halves(fg, 9, gw, WPB, True)

    for copy in backs:
        copy.start()

    def add_t(d, total):
        o = lax.rem(lon + d, lons)
        t_in(o).wait_recv()
        return total + part_t_in[o].astype(F32)

    sum_t[lon] = lax.fori_loop(1, lons, add_t, mine_t[lon]).astype(BF16)

    def tb_out(o):
        return copy_to(sum_t.at[lon], sum_t.at[lon], tb_send.at[o], tb_recv.at[lon], lat, o)

    def tb_in(o):
        return copy_to(sum_t.at[o], sum_t.at[o], tb_send.at[o], tb_recv.at[o], lat, o)

    each(0, lons, lon, lambda o: tb_out(o).start())

    def join_out(a):
        return copy_to(joined.at[lat], joined.at[lat], join_send.at[a], join_recv.at[lat], a, lon)

    def join_in(a):
        return copy_to(joined.at[a], joined.at[a], join_send.at[a], join_recv.at[a], a, lon)

    @pl.when(lat < TILES)
    def _():
        def add_tile(d, total):
            a = lax.rem(lat + d, lats)
            tile_in(a).wait_recv()
            return total + tiles_in[a].astype(F32)

        total = lax.fori_loop(1, lats, add_tile, tiles[lat].astype(F32))
        joined[lat] = total.astype(BF16)
        each(0, lats, lat, lambda a: join_out(a).start())

    each(0, TILES, lat, lambda a: join_in(a).wait_recv())
    sum_w[lon] = jnp.concatenate([joined[t] for t in range(TILES)], axis=1)

    def wb_out(o):
        return copy_to(sum_w.at[lon], sum_w.at[lon], wb_send.at[o], wb_recv.at[lon], lat, o)

    def wb_in(o):
        return copy_to(sum_w.at[o], sum_w.at[o], wb_send.at[o], wb_recv.at[o], lat, o)

    each(0, lons, lon, lambda o: wb_out(o).start())

    each(0, lons, lon, lambda o: tb_in(o).wait_recv())
    whole = jnp.concatenate([sum_t[j].astype(F32) for j in range(lons)], axis=1)
    square = jnp.sum(whole * whole).reshape(1, 1)
    squares[lat] = jnp.broadcast_to(square, (8, 128))

    def sq_out(a):
        return copy_to(squares.at[lat], squares.at[lat], sq_send.at[a], sq_recv.at[lat], a, lon)

    def sq_in(a):
        return copy_to(squares.at[a], squares.at[a], sq_send.at[a], sq_recv.at[a], a, lon)

    each(0, lats, lat, lambda a: sq_out(a).start())

    for copy in backs:
        copy.wait()

    @pl.when(lat > 0)
    def _():
        for copy in downs + crosses:
            copy.wait_recv()

    @pl.when(lat < lats - 1)
    def _():
        for copy in downs + crosses:
            copy.wait_send()

    @pl.when(first)
    def _():
        for copy in tops:
            copy.wait()

    leave = [
        pltpu.make_async_copy(frame.at[0:12, :, 0:OWN], out, own_sem.at[n])
        for n, (frame, out) in enumerate(((fx, x_out), (fg, g_out)))
    ]
    for copy in leave:
        copy.start()

    each(0, lats, lat, lambda a: sq_in(a).wait_recv())
    table_squares = jnp.zeros((1, 1), F32)
    for a in range(lats):
        table_squares = table_squares + squares[a][0:1, 0:1]
    table_rms = jnp.sqrt(table_squares / (lats * 2 * HEADS * POS) + 1e-6)
    whole = whole[:, :POS] / table_rms
    for i in range(HEADS):
        grad_bias[i] = whole[2 * i : 2 * i + 2]

    each(0, lons, lon, lambda o: wb_in(o).wait_recv())
    cols = []
    square = jnp.zeros((16, 128), F32)
    for j in range(lons):
        for t in range(TILES):
            piece = sum_w[j, :, t * 128 : t * 128 + 128].astype(F32)
            square = square + piece * piece
            cols.append(piece)
    rms = jnp.sqrt(jnp.sum(square).reshape(1, 1) / (4 * C * C) + 1e-6)
    inverse = 1.0 / rms
    for r in range(12):
        row = jnp.concatenate(cols[r * 6 : r * 6 + 6], axis=1) * inverse
        grad_q[r * 16 : r * 16 + 16] = row[:, : 3 * C]
        grad_p[r * 16 : r * 16 + 16] = row[:, 3 * C :]

    def sent(o):
        w_out(o).wait_send()
        t_out(o).wait_send()
        tb_out(o).wait_send()
        wb_out(o).wait_send()

    each(0, lons, lon, sent)
    each(0, TILES, lat, lambda a: tile_out(a).wait_send())
    each(0, lats, lat, lambda a: sq_out(a).wait_send())

    @pl.when(lat < TILES)
    def _():
        each(0, lats, lat, lambda a: join_out(a).wait_send())

    for copy in sides:
        copy.wait_send()

    @pl.when(lat > 0)
    def _():
        for copy in ups + diags:
            copy.wait_send()

    for copy in leave:
        copy.wait()


def finish_kernel(x, g, q, p, b, x_out, g_out, q_out, p_out, b_out, sems):
    copies = []
    for src, dst in ((x, x_out), (g, g_out)):
        for r in range(0, 12, 3):
            copies.append((src.at[r : r + 3], dst.at[r : r + 3]))
    copies += [(q, q_out), (p, p_out), (b, b_out)]
    copies = [pltpu.make_async_copy(*pair, sems.at[n]) for n, pair in enumerate(copies)]
    for copy in copies:
        copy.start()
    for copy in copies:
        copy.wait()


def finish(*results):
    hbm = pl.BlockSpec(memory_space=pl.ANY)
    return pl.pallas_call(
        finish_kernel,
        in_specs=[hbm] * 5,
        out_specs=[hbm] * 5,
        out_shape=[jax.ShapeDtypeStruct(a.shape, a.dtype) for a in results],
        scratch_shapes=[pltpu.SemaphoreType.DMA((11,))],
        compiler_params=pltpu.CompilerParams(vmem_limit_bytes=56 * 2**20),
        name="finish",
    )(*results)


def on_device(inputs, cotangent, norm_gain, norm_shift, w_qkv, w_proj, bias_table):
    lats = lax.axis_size("lat")
    lons = lax.axis_size("lon")
    vmem = pl.BlockSpec(memory_space=pltpu.VMEM)
    hbm = pl.BlockSpec(memory_space=pl.ANY)
    shape = jax.ShapeDtypeStruct
    units = 2 * WPB + WPB // 2
    sems = pltpu.SemaphoreType.DMA
    counts = [4, 6, 6, 8, 8] + [lons] * 4 + [lats] * 4 + [lons] * 4 + [lats] * 2
    results = pl.pallas_call(
        functools.partial(kernel, lats, lons),
        in_specs=[hbm, hbm] + [vmem] * 5,
        out_specs=[hbm, hbm] + [vmem] * 3,
        out_shape=[
            shape((12, 2, OWN), BF16),
            shape((12, 2, OWN), BF16),
            shape((C, 3 * C), F32),
            shape((C, C), F32),
            shape((HEADS, 2, POS), F32),
        ],
        scratch_shapes=[
            pltpu.VMEM((FROWS, 2, FRAME), BF16),
            pltpu.VMEM((FROWS, 2, FRAME), BF16),
            pltpu.VMEM((units, 2, WIN, 128), F32),
            pltpu.VMEM((units, 2, WIN, 128), F32),
            pltpu.VMEM((3, WIN, 896), F32),
            pltpu.VMEM((3, WIN, 896), F32),
            pltpu.VMEM((12, 16, ROWPAD), F32),
            pltpu.VMEM((3, WIN, 128), F32),
            pltpu.VMEM((16, 3328), F32),
            pltpu.VMEM((3 * C, C), BF16),
            pltpu.VMEM((C, C), BF16),
            pltpu.VMEM((C, 3 * C), F32),
            pltpu.VMEM((C, C), F32),
            pltpu.VMEM((lons, 16, WCHUNK), F32),
            pltpu.VMEM((lons, 16, WCHUNK), BF16),
            pltpu.VMEM((lons, 16, WCHUNK), BF16),
            pltpu.VMEM((TILES, 16, 128), BF16),
            pltpu.VMEM((lats, 16, 128), BF16),
            pltpu.VMEM((TILES, 16, 128), BF16),
            pltpu.VMEM((lons, 16, WCHUNK), BF16),
            pltpu.VMEM((lons, 16, TCHUNK), F32),
            pltpu.VMEM((lons, 16, TCHUNK), BF16),
            pltpu.VMEM((lons, 16, TCHUNK), BF16),
            pltpu.VMEM((lons, 16, TCHUNK), BF16),
            pltpu.VMEM((lats, 8, 128), F32),
        ]
        + [sems((n,)) for n in counts],
        compiler_params=pltpu.CompilerParams(
            collective_id=0, has_side_effects=True, vmem_limit_bytes=56 * 2**20
        ),
        name="windows",
    )(
        inputs.transpose(1, 0, 2),
        cotangent.transpose(1, 0, 2),
        norm_gain.reshape(1, C),
        norm_shift.reshape(1, C),
        w_qkv,
        w_proj,
        bias_table.transpose(1, 0, 2),
    )
    x_out, g_out, grad_q, grad_p, grad_bias = finish(*results)
    x_out, g_out, grad_bias = (a.transpose(1, 0, 2) for a in (x_out, g_out, grad_bias))
    return x_out, g_out, grad_q, grad_p, grad_bias


def solution(mesh):
    return jax.shard_map(
        on_device,
        mesh=mesh,
        in_specs=(
            P(None, "lat", "lon"),
            P(None, "lat", "lon"),
            P(),
            P(),
            P(),
            P(),
            P("lat", None, None),
        ),
        out_specs=(P(None, "lat", "lon"), P(None, "lat", "lon"), P(), P(), P("lat", None, None)),
        check_vma=False,
    )
```

```python
import functools
import math

import jax
import jax.numpy as jnp
import numpy as np
from jax import lax
from jax.experimental import pallas as pl
from jax.experimental.pallas import tpu as pltpu
from jax.sharding import PartitionSpec as P

C = 192
HEADS = 6
HD = 32
WLON = 12
WIN = 144
HALF = 72
SPAN = 23
ROWLEN = 12 * SPAN
ROWPAD = 384
COLS = 96
HALO = 6 * C
WLANES = WLON * C
OWN = COLS * C
FRAME = OWN + HALO
FROWS = 15
GROUP = 4
WPB = 8
POS = 3312
TABLE = 4096
WCHUNK = 12 * 768 // 8
TCHUNK = TABLE // 8
TILES = WCHUNK // 128
MESH = pl.DeviceIdType.MESH
EPS = 1e-5
SCALE = HD**-0.5
LOG2E = math.log2(math.e)
F32 = jnp.float32
BF16 = jnp.bfloat16


def nn(a, b):
    return lax.dot_general(a, b, (((1,), (0,)), ((), ())), preferred_element_type=F32)


def nt(a, b):
    return lax.dot_general(a, b, (((1,), (1,)), ((), ())), preferred_element_type=F32)


def tn(a, b):
    return lax.dot_general(a, b, (((0,), (0,)), ((), ())), preferred_element_type=F32)


def pick_matrix():
    row = lax.broadcasted_iota(jnp.int32, (WIN, 1), 0)
    lk = lax.rem(row, WLON)
    block = lax.div(row, WLON)
    kb = lax.rem(block, 2) * 6 + lax.div(block, 2)
    col = lax.broadcasted_iota(jnp.int32, (WIN, ROWPAD), 1)
    return jnp.where(col == kb * SPAN + 11 - lk, 1.0, 0.0).astype(BF16)


def pieces_in(frame, tokens, place, unit, count=GROUP):
    def piece(r, side, m):
        row, base = place(r, side)
        slab = frame[pl.ds(row, 3), :, pl.ds(pl.multiple_of(base + m * 2 * C, 128), 2 * C)]
        slab = slab.astype(F32).reshape(6, 2 * C)
        for n, part in ((2 * m, slab[:, :C]), (2 * m + 1, slab[:, C:])):
            slots = pl.ds(side * HALF + n, 6, stride=WLON)
            tokens[unit + r, 0, slots, :] = part[:, :128]
            tokens[unit + r, 1, slots, :] = jnp.concatenate([part[:, 128:], part[:, 128:]], axis=1)

    return [
        functools.partial(piece, r, side, m) for r in range(count) for side in range(2) for m in range(6)
    ]


def pieces_out(frame, tokens, place, unit, count=GROUP):
    def piece(r, side, m):
        row, base = place(r, side)
        for p in range(3):
            parts = []
            for n in (2 * m, 2 * m + 1):
                slots = pl.ds(side * HALF + p * 24 + n, 2, stride=WLON)
                parts.append(tokens[unit + r, 0, slots, :])
                parts.append(tokens[unit + r, 1, slots, :][:, : C - 128])
            lanes = pl.ds(pl.multiple_of(base + m * 2 * C, 128), 2 * C)
            frame[row + p, :, lanes] = jnp.concatenate(parts, axis=1).astype(BF16)

    return [
        functools.partial(piece, r, side, m) for r in range(count) for side in range(2) for m in range(6)
    ]


def put_head(ref, slot, i, value):
    ref[slot, :, i * 128 : i * 128 + 128] = value[:, :128]
    ref[slot, :, 768 + i * 16 : 768 + i * 16 + 16] = value[:, 128:]


def get_head(ref, slot, i):
    tail = ref[slot, :, 768 + i * 16 : 768 + i * 16 + 16]
    return jnp.concatenate([ref[slot, :, i * 128 : i * 128 + 128], tail], axis=1)


def bias_rows(table, flat, rows_scratch):
    rows_scratch[...] = jnp.zeros_like(rows_scratch)
    for i in range(HEADS):
        flat[2 * i : 2 * i + 2, 0:POS] = table[i]
    for zq in range(2):
        for pq in range(6):
            at = (zq * 6 + pq) * ROWLEN
            rows_scratch[pq * 2 + zq, 0:12, 0:ROWLEN] = flat[0:12, at : at + ROWLEN]


def bias_in(lo, hi, pick, rows_scratch, shifted, bias):
    for n in range(lo, hi):
        rows = rows_scratch[:, n, :]
        rows = jnp.concatenate([rows, jnp.zeros((4, ROWPAD), F32)], axis=0)
        for lq in range(WLON):
            moved = pltpu.roll(rows, (ROWPAD - lq) % ROWPAD, 1) if lq else rows
            for t in range(3):
                shifted[t, pl.ds(lq, 12, stride=12), :] = moved[:12, t * 128 : t * 128 + 128]
        full = jnp.concatenate([shifted[t] for t in range(3)], axis=1)
        high = full.astype(BF16)
        low = (full - high.astype(F32)).astype(BF16)
        total = nt(pick, high) + nt(pick, low)
        put_head(bias, n % 2, n // 2, total * LOG2E)


def bias_out(grads, pick, shifted, rows_scratch):
    for n in range(12):
        full = nn(get_head(grads, n % 2, n // 2).astype(BF16).T, pick)
        for t in range(3):
            shifted[t] = full[:, t * 128 : t * 128 + 128]
        total = jnp.zeros((16, ROWPAD), F32)
        for lq in range(WLON):
            rows = [shifted[t, pl.ds(lq, 12, stride=12), :] for t in range(3)]
            rows = jnp.concatenate(rows, axis=1)
            rows = jnp.concatenate([rows, jnp.zeros((4, ROWPAD), F32)], axis=0)
            total = total + (pltpu.roll(rows, lq, 1) if lq else rows)
        rows_scratch[:, n, :] = total[:12]
    parts = [rows_scratch[pq * 2 + zq][:, :ROWLEN] for zq in range(2) for pq in range(6)]
    parts.append(jnp.zeros((16, TABLE - POS), F32))
    return jnp.concatenate(parts, axis=1)


def head_rows(a):
    lane = lax.broadcasted_iota(jnp.int32, (1, 128), 1) // HD
    zero = jnp.zeros((), BF16)

    def only(part, i):
        return jnp.where(lane[:, : part.shape[1]] == i % 4, part, zero)

    wide, slim = a[:, :128], a[:, 128:C]
    first = jnp.concatenate([only(wide[:128], i) for i in range(4)], axis=0)
    second = jnp.concatenate([only(slim[:128], i) for i in range(4, HEADS)], axis=0)
    tail = [only(wide[128:], i) for i in range(4)]
    left = jnp.concatenate(tail + [jnp.zeros((64, 128), BF16)], axis=0)
    tail = [only(slim[128:], i) for i in range(4, HEADS)]
    right = jnp.concatenate([jnp.zeros((64, 64), BF16)] + tail + [jnp.zeros((32, 64), BF16)], axis=0)
    return first, second, left, right


def across(a, rows):
    first, second, left, right = rows
    return jnp.concatenate(
        [nt(a[:, :128], first), nt(a[:, 128:C], second), nt(a, jnp.concatenate([left, right], axis=1))],
        axis=1,
    )


def gathered(a, rows):
    first, second, left, right = rows
    tail = nn(a[:, 768:], jnp.concatenate([left, right], axis=1))
    return jnp.concatenate(
        [nn(a[:, :512], first) + tail[:, :128], nn(a[:, 512:768], second) + tail[:, 128:]], axis=1
    )


def by_head(t, a):
    tail = nn(t, a[:, 768:])
    out = []
    for j in range(HEADS // 2):
        pair = nn(t[64 * j : 64 * j + 64], a[:, 256 * j : 256 * j + 256])
        for i in (2 * j, 2 * j + 1):
            r = (i % 2) * HD
            main = pair[r : r + HD, r * 4 : r * 4 + 128]
            out.append(jnp.concatenate([main, tail[i * HD : i * HD + HD, 16 * i : 16 * i + 16]], axis=1))
    return jnp.concatenate(out, axis=0)


def weight_sums(raw_q, h_t, dqkv):
    for j in range(3):
        raw_q[:, j * C : j * C + C] += nn(h_t, dqkv[:, j * C : j * C + C])


def attend(
    x_ref, g_ref, us, bias, dbias, slot, gain, shift, wqkv, wqkv_t, wproj, wproj_t, raw_q, raw_p, held_h, held_d, early, late
):
    n = WIN
    ws = range(len(us))
    early, late = iter(early), iter(late)

    def emit(queue, count):
        for _ in range(count):
            step = next(queue, None)
            if step is not None:
                step()

    def tokens(ref):
        rows = [jnp.concatenate([ref[u, 0], ref[u, 1]], axis=1) for u in us]
        return jnp.concatenate(rows, axis=0)[:, :C]

    def split(a):
        return [a[w * n : (w + 1) * n] for w in ws]

    x = tokens(x_ref)
    g = tokens(g_ref)
    gb = g.astype(BF16)
    do = split(nn(gb, wproj_t[...]).astype(BF16))
    weight_sums(raw_q, held_h[...], held_d[...])
    center = x - jnp.mean(x, axis=1, keepdims=True)
    rstd = lax.rsqrt(jnp.mean(center * center, axis=1, keepdims=True) + EPS)
    xn = center * rstd
    h = (xn * gain + shift).astype(BF16)
    held_h[...] = h.T
    qkv = split(nn(h, wqkv[...]).astype(BF16))
    q = [a[:, :C] for a in qkv]
    k = [a[:, C : 2 * C] for a in qkv]
    v = [a[:, 2 * C :] for a in qkv]
    k_t = [a.T for a in k]
    v_t = [a.T for a in v]
    qr = [head_rows(a) for a in q]
    dor = [head_rows(a) for a in do]
    s, dp, pb, dsb, o_t, dq_t, dv, dk = {}, {}, {}, {}, {}, {}, {}, {}

    def scores(w):
        def one(out, a, rows):
            out[w] = across(a[w], rows[w])

        return [functools.partial(one, s, k, qr), functools.partial(one, dp, v, dor)]

    def products(w):
        def one(out, act, *args):
            out[w] = act(*args).astype(BF16)

        return [
            functools.partial(one, dq_t, by_head, k_t[w], dsb[w]),
            functools.partial(one, dk, gathered, dsb[w], qr[w]),
            functools.partial(one, dv, gathered, pb[w], dor[w]),
            functools.partial(one, o_t, by_head, v_t[w], pb[w]),
        ]

    for step in scores(0):
        step()
    for w in ws:
        ready = scores(w + 1) if w + 1 < len(us) else []
        done = products(w - 1) if w else []
        ready = done + ready
        ps, dss = [], []
        for b in range(7):
            lanes = slice(b * 128, b * 128 + 128)
            t = s[w][:, lanes] * (SCALE * LOG2E) + bias[slot, :, lanes]
            e = jnp.exp2(t - jnp.max(t, axis=0, keepdims=True))
            p = e * (1.0 / jnp.sum(e, axis=0, keepdims=True))
            d = dp[w][:, lanes]
            ds = p * (d - jnp.sum(p * d, axis=0, keepdims=True))
            dbias[slot, :, lanes] += ds
            ps.append(p.astype(BF16))
            dss.append((ds * SCALE).astype(BF16))
            if ready:
                ready.pop(0)()
            emit(early, 0)
            emit(late, 0)
        for step in ready:
            step()
        pb[w] = jnp.concatenate(ps, axis=1)
        dsb[w] = jnp.concatenate(dss, axis=1)
    for step in products(len(us) - 1):
        step()
    dk = [dk[w] for w in ws]
    dv = [dv[w] for w in ws]
    dk = jnp.concatenate(dk, axis=0)
    dv = jnp.concatenate(dv, axis=0)
    dq = jnp.concatenate([dq_t[w].T for w in ws], axis=0)
    dqkv = jnp.concatenate([dq, dk, dv], axis=1)
    held_d[...] = dqkv
    dh = nn(dqkv, wqkv_t[...])
    emit(late, 0)
    o = jnp.concatenate([o_t[w].T for w in ws], axis=0)
    dxn = dh * gain
    m1 = jnp.mean(dxn, axis=1, keepdims=True)
    m2 = jnp.mean(dxn * xn, axis=1, keepdims=True)
    dx = (rstd * (dxn - m1 - xn * m2)).astype(BF16)
    g = split(g + dx.astype(F32))
    a = nn(o, wproj[...]).astype(BF16)
    raw_p[...] += sum(nn(o_t[w], gb[w * n : (w + 1) * n]) for w in ws)
    x = split(x + a.astype(F32))
    emit(early, 10**6)
    emit(late, 10**6)
    for w, u in enumerate(us):
        x_ref[u, 0] = x[w][:, :128]
        x_ref[u, 1, :, 0:64] = x[w][:, 128:]
        g_ref[u, 0] = g[w][:, :128]
        g_ref[u, 1, :, 0:64] = g[w][:, 128:]


def copy_to(src, dst, send, recv, lat, lon):
    return pltpu.make_async_remote_copy(
        src_ref=src,
        dst_ref=dst,
        send_sem=send,
        recv_sem=recv,
        device_id=(lat, lon),
        device_id_type=MESH,
    )


def greet(lat, lon):
    barrier = pltpu.get_barrier_semaphore()
    pl.semaphore_signal(barrier, inc=1, device_id=(lat, lon), device_id_type=MESH)


def each(lo, hi, skip, act):
    def step(i, _):
        @pl.when(i != skip)
        def _():
            act(i)

        return 0

    lax.fori_loop(lo, hi, step, 0)


def kernel(
    lats,
    lons,
    x,
    g,
    gain_ref,
    shift_ref,
    wqkv,
    wproj,
    table,
    x_out,
    g_out,
    grad_q,
    grad_p,
    grad_bias,
    fx,
    fg,
    xw,
    gw,
    bias,
    dbias,
    rows_scratch,
    shifted,
    flat,
    wqkv_t,
    wproj_t,
    raw_q,
    raw_p,
    held_h,
    held_d,
    mine_w,
    part_w,
    part_w_in,
    tiles,
    tiles_in,
    joined,
    sum_w,
    mine_t,
    part_t,
    part_t_in,
    sum_t,
    squares,
    own_sem,
    halo_send,
    halo_recv,
    ret_send,
    ret_recv,
    w_send,
    w_recv,
    t_send,
    t_recv,
    tile_send,
    tile_recv,
    join_send,
    join_recv,
    wb_send,
    wb_recv,
    tb_send,
    tb_recv,
    sq_send,
    sq_recv,
):
    lat = lax.axis_index("lat")
    lon = lax.axis_index("lon")
    west = lax.rem(lon + lons - 1, lons)
    east = lax.rem(lon + 1, lons)
    first = lat == 0
    final = lat == lats - 1
    barrier = pltpu.get_barrier_semaphore()
    each(0, lons, lon, lambda o: greet(lat, o))
    each(0, lats, lat, lambda a: greet(a, lon))

    @pl.when(lat > 0)
    def _():
        greet(lat - 1, west)

    @pl.when(lat < lats - 1)
    def _():
        greet(lat + 1, east)

    pairs = ((x, fx), (g, fg))
    local = []
    for n, (src, frame) in enumerate(pairs):
        local.append(
            pltpu.make_async_copy(
                src.at[3:12, :, HALO:OWN], frame.at[3:12, :, HALO:OWN], own_sem.at[n]
            )
        )
    polar = []
    for n, (src, frame) in enumerate(pairs):
        polar.append(
            pltpu.make_async_copy(
                src.at[0:3, :, HALO:OWN], frame.at[0:3, :, HALO:OWN], own_sem.at[2 + n]
            )
        )
    for copy in local:
        copy.start()

    @pl.when(first)
    def _():
        for copy in polar:
            copy.start()

    wqkv_t[...] = wqkv[...].T
    wproj_t[...] = wproj[...].T

    ups, sides, diags = [], [], []
    for n, (src, frame) in enumerate(pairs):
        ups.append(
            copy_to(
                src.at[0:3, :, HALO:OWN],
                frame.at[12:15, :, HALO:OWN],
                halo_send.at[n],
                halo_recv.at[n],
                lat - 1,
                lon,
            )
        )
        sides.append(
            copy_to(
                src.at[:, :, 0:HALO],
                frame.at[0:12, :, OWN:FRAME],
                halo_send.at[2 + n],
                halo_recv.at[2 + n],
                lat,
                west,
            )
        )
        diags.append(
            copy_to(
                src.at[0:3, :, 0:HALO],
                frame.at[12:15, :, OWN:FRAME],
                halo_send.at[4 + n],
                halo_recv.at[4 + n],
                lat - 1,
                west,
            )
        )
    pick = pick_matrix()
    bias[:, :, 768:] = jnp.zeros((3, WIN, 128), F32)
    bias_rows(table, flat, rows_scratch)
    bias_in(0, 6, pick, rows_scratch, shifted, bias)
    peers = lons - 1 + lats - 1
    pl.semaphore_wait(barrier, peers + jnp.where(lat > 0, 1, 0) + jnp.where(lat < lats - 1, 1, 0))
    for copy in sides:
        copy.start()

    @pl.when(lat > 0)
    def _():
        for copy in ups + diags:
            copy.start()

    bias_in(6, 12, pick, rows_scratch, shifted, bias)
    dbias[...] = jnp.zeros_like(dbias)
    raw_q[...] = jnp.zeros_like(raw_q)
    raw_p[...] = jnp.zeros_like(raw_p)

    for copy in local:
        copy.wait()
    def halves_in(slot, source, lo):
        for i in range(HEADS):
            part = get_head(bias, source, i)[lo : lo + HALF, lo : lo + HALF]
            away = jnp.full((HALF, HALF), -1e9, F32)
            top = jnp.concatenate([part, away], axis=1)
            low = jnp.concatenate([away, part], axis=1)
            put_head(bias, slot, i, jnp.concatenate([top, low], axis=0))

    def halves_grad(slot, target, lo):
        zero = jnp.zeros((HALF, HALF), F32)
        for i in range(HEADS):
            both = get_head(dbias, slot, i)
            part = both[:HALF, :HALF] + both[HALF:, HALF:]
            part = jnp.concatenate([zero, part] if lo else [part, zero], axis=1)
            none = jnp.zeros((HALF, WIN), F32)
            part = jnp.concatenate([none, part] if lo else [part, none], axis=0)
            old = get_head(dbias, target, i) if target != slot else 0.0
            put_head(dbias, target, i, old + part)

    @pl.when(first)
    def _():
        for copy in polar:
            copy.wait()
        halves_in(2, 0, HALF)

    @pl.when(final)
    def _():
        halves_in(1, 1, 0)

    rest = (gain_ref[...], shift_ref[...], wqkv, wqkv_t, wproj, wproj_t, raw_q, raw_p, held_h, held_d)
    full = 2 * WPB // GROUP
    half = WPB // 2 // GROUP
    steps = jnp.where(first, full + half, jnp.where(final, full // 2 + half, full))

    def place(v, r, side, spare):
        halved = (first & (v == full)) | (final & (v == full // 2))
        row = jnp.where(halved, jnp.where(first, 0, 9), 3 + 6 * (v // (full // 2)) + 3 * side)
        window = jnp.where(halved, 2 * r + side, lax.rem(v, full // 2) * GROUP + r)
        return jnp.where(spare, FROWS + 3 * side, row), HALO + window * WLANES

    def laying(v, unit, out, spare=False):
        move = pieces_out if out else pieces_in
        at = functools.partial(lambda r, side: place(v, r, side, spare))
        both = zip(move(fx, xw, at, unit), move(fg, gw, at, unit))
        return [step for pair in both for step in pair]

    held_h[...] = jnp.zeros_like(held_h)
    held_d[...] = jnp.zeros_like(held_d)

    def start(r, _):
        for frame, tokens in ((fx, xw), (fg, gw)):
            for step in pieces_in(frame, tokens, lambda _, side: place(0, r, side, False), r, 1):
                step()
        return 0

    lax.fori_loop(0, GROUP, start, 0)
    for copy in sides:
        copy.wait_recv()

    def group(u, _):
        @pl.when((u == full // 2 - 1) & (lat < lats - 1))
        def _():
            for copy in ups + diags:
                copy.wait_recv()

        slot = jnp.minimum(u // (WPB // GROUP), 2)
        us = [GROUP * u + r for r in range(GROUP)]
        behind = jnp.maximum(u - 1, 0)
        early = laying(behind, GROUP * behind, True, u == 0)
        late = laying(jnp.minimum(u + 1, steps - 1), GROUP * (u + 1), False)
        attend(xw, gw, us, bias, dbias, slot, *rest, early, late)
        return 0

    lax.fori_loop(0, steps, group, 0)
    weight_sums(raw_q, held_h[...], held_d[...])

    raw = jnp.concatenate([raw_q[...], raw_p[...]], axis=1)
    for j in range(lons):
        row = []
        for t in range(TILES):
            col = j * TILES + t
            r, c = col // 6 * 16, col % 6 * 128
            row.append(raw[r : r + 16, c : c + 128])
        chunk = jnp.concatenate(row, axis=1)
        mine_w[j] = chunk
        part_w[j] = chunk.astype(BF16)

    def w_out(o):
        return copy_to(part_w.at[o], part_w_in.at[lon], w_send.at[o], w_recv.at[lon], lat, o)

    def w_in(o):
        return copy_to(part_w.at[o], part_w_in.at[o], w_send.at[o], w_recv.at[o], lat, o)

    each(0, lons, lon, lambda o: w_out(o).start())

    @pl.when(first)
    def _():
        halves_grad(2, 0, HALF)

    @pl.when(final)
    def _():
        halves_grad(1, 1, 0)

    grads = bias_out(dbias, pick, shifted, rows_scratch)
    for j in range(lons):
        chunk = grads[:, j * TCHUNK : (j + 1) * TCHUNK]
        mine_t[j] = chunk
        part_t[j] = chunk.astype(BF16)

    def t_out(o):
        return copy_to(part_t.at[o], part_t_in.at[lon], t_send.at[o], t_recv.at[lon], lat, o)

    def t_in(o):
        return copy_to(part_t.at[o], part_t_in.at[o], t_send.at[o], t_recv.at[o], lat, o)

    each(0, lons, lon, lambda o: t_out(o).start())

    downs, crosses, backs, tops = [], [], [], []
    for n, frame in enumerate((fx, fg)):
        rows = frame.at[0:3, :, HALO:OWN]
        side = frame.at[3:12, :, 0:HALO]
        corner = frame.at[0:3, :, 0:HALO]
        sems = [(ret_send.at[2 * r + n], ret_recv.at[2 * r + n]) for r in range(4)]
        downs.append(copy_to(frame.at[12:15, :, HALO:OWN], rows, *sems[0], lat + 1, lon))
        crosses.append(copy_to(frame.at[12:15, :, OWN:FRAME], corner, *sems[1], lat + 1, east))
        backs.append(copy_to(frame.at[3:12, :, OWN:FRAME], side, *sems[2], lat, east))
        tops.append(copy_to(frame.at[0:3, :, OWN:FRAME], corner, *sems[3], lat, east))

    def finish_out(r, _):
        for frame, tokens in ((fx, xw), (fg, gw)):
            at = lambda _, side: place(steps - 1, r, side, False)
            for step in pieces_out(frame, tokens, at, GROUP * (steps - 1) + r, 1):
                step()
        return 0

    lax.fori_loop(0, GROUP, finish_out, 0)

    @pl.when(lat < lats - 1)
    def _():
        for copy in downs + crosses:
            copy.start()

    @pl.when(first)
    def _():
        for copy in tops:
            copy.start()

    for copy in backs:
        copy.start()

    def add_w(d, total):
        o = lax.rem(lon + d, lons)
        w_in(o).wait_recv()
        return total + part_w_in[o].astype(F32)

    total = lax.fori_loop(1, lons, add_w, mine_w[lon])
    for t in range(TILES):
        tiles[t] = total[:, t * 128 : t * 128 + 128].astype(BF16)

    def tile_out(a):
        return copy_to(tiles.at[a], tiles_in.at[lat], tile_send.at[a], tile_recv.at[lat], a, lon)

    def tile_in(a):
        return copy_to(tiles.at[0], tiles_in.at[a], tile_send.at[0], tile_recv.at[a], a, lon)

    each(0, TILES, lat, lambda a: tile_out(a).start())

    def add_t(d, total):
        o = lax.rem(lon + d, lons)
        t_in(o).wait_recv()
        return total + part_t_in[o].astype(F32)

    sum_t[lon] = lax.fori_loop(1, lons, add_t, mine_t[lon]).astype(BF16)

    def tb_out(o):
        return copy_to(sum_t.at[lon], sum_t.at[lon], tb_send.at[o], tb_recv.at[lon], lat, o)

    def tb_in(o):
        return copy_to(sum_t.at[o], sum_t.at[o], tb_send.at[o], tb_recv.at[o], lat, o)

    each(0, lons, lon, lambda o: tb_out(o).start())

    def join_out(a):
        return copy_to(joined.at[lat], joined.at[lat], join_send.at[a], join_recv.at[lat], a, lon)

    def join_in(a):
        return copy_to(joined.at[a], joined.at[a], join_send.at[a], join_recv.at[a], a, lon)

    @pl.when(lat < TILES)
    def _():
        def add_tile(d, total):
            a = lax.rem(lat + d, lats)
            tile_in(a).wait_recv()
            return total + tiles_in[a].astype(F32)

        total = lax.fori_loop(1, lats, add_tile, tiles[lat].astype(F32))
        joined[lat] = total.astype(BF16)
        each(0, lats, lat, lambda a: join_out(a).start())

    each(0, TILES, lat, lambda a: join_in(a).wait_recv())
    sum_w[lon] = jnp.concatenate([joined[t] for t in range(TILES)], axis=1)

    def wb_out(o):
        return copy_to(sum_w.at[lon], sum_w.at[lon], wb_send.at[o], wb_recv.at[lon], lat, o)

    def wb_in(o):
        return copy_to(sum_w.at[o], sum_w.at[o], wb_send.at[o], wb_recv.at[o], lat, o)

    each(0, lons, lon, lambda o: wb_out(o).start())

    each(0, lons, lon, lambda o: tb_in(o).wait_recv())
    whole = jnp.concatenate([sum_t[j].astype(F32) for j in range(lons)], axis=1)
    square = jnp.sum(whole * whole).reshape(1, 1)
    squares[lat] = jnp.broadcast_to(square, (8, 128))

    def sq_out(a):
        return copy_to(squares.at[lat], squares.at[lat], sq_send.at[a], sq_recv.at[lat], a, lon)

    def sq_in(a):
        return copy_to(squares.at[a], squares.at[a], sq_send.at[a], sq_recv.at[a], a, lon)

    each(0, lats, lat, lambda a: sq_out(a).start())

    for copy in backs:
        copy.wait()

    @pl.when(lat > 0)
    def _():
        for copy in downs + crosses:
            copy.wait_recv()

    @pl.when(lat < lats - 1)
    def _():
        for copy in downs + crosses:
            copy.wait_send()

    @pl.when(first)
    def _():
        for copy in tops:
            copy.wait()

    leave = [
        pltpu.make_async_copy(frame.at[0:12, :, 0:OWN], out, own_sem.at[n])
        for n, (frame, out) in enumerate(((fx, x_out), (fg, g_out)))
    ]
    for copy in leave:
        copy.start()

    each(0, lats, lat, lambda a: sq_in(a).wait_recv())
    table_squares = jnp.zeros((1, 1), F32)
    for a in range(lats):
        table_squares = table_squares + squares[a][0:1, 0:1]
    table_rms = jnp.sqrt(table_squares / (lats * 2 * HEADS * POS) + 1e-6)
    whole = whole[:, :POS] / table_rms
    for i in range(HEADS):
        grad_bias[i] = whole[2 * i : 2 * i + 2]

    each(0, lons, lon, lambda o: wb_in(o).wait_recv())
    cols = []
    square = jnp.zeros((16, 128), F32)
    for j in range(lons):
        for t in range(TILES):
            piece = sum_w[j, :, t * 128 : t * 128 + 128].astype(F32)
            square = square + piece * piece
            cols.append(piece)
    rms = jnp.sqrt(jnp.sum(square).reshape(1, 1) / (4 * C * C) + 1e-6)
    inverse = 1.0 / rms
    for r in range(12):
        row = jnp.concatenate(cols[r * 6 : r * 6 + 6], axis=1) * inverse
        grad_q[r * 16 : r * 16 + 16] = row[:, : 3 * C]
        grad_p[r * 16 : r * 16 + 16] = row[:, 3 * C :]

    def sent(o):
        w_out(o).wait_send()
        t_out(o).wait_send()
        tb_out(o).wait_send()
        wb_out(o).wait_send()

    each(0, lons, lon, sent)
    each(0, TILES, lat, lambda a: tile_out(a).wait_send())
    each(0, lats, lat, lambda a: sq_out(a).wait_send())

    @pl.when(lat < TILES)
    def _():
        each(0, lats, lat, lambda a: join_out(a).wait_send())

    for copy in sides:
        copy.wait_send()

    @pl.when(lat > 0)
    def _():
        for copy in ups + diags:
            copy.wait_send()

    for copy in leave:
        copy.wait()


def finish_kernel(x, g, q, p, b, x_out, g_out, q_out, p_out, b_out, xs, gs, qs, ps, bs, sems):
    moves = []
    for src, mid, dst in ((x, xs, x_out), (g, gs, g_out)):
        for r in range(0, 12, 3):
            part = slice(r, r + 3)
            moves.append((src.at[part], mid.at[part], dst.at[part]))
    moves += [(q, qs, q_out), (p, ps, p_out), (b, bs, b_out)]
    into = [pltpu.make_async_copy(m[0], m[1], sems.at[n]) for n, m in enumerate(moves)]
    away = [pltpu.make_async_copy(m[1], m[2], sems.at[len(moves) + n]) for n, m in enumerate(moves)]
    for copy in into:
        copy.start()
    for first, second in zip(into, away):
        first.wait()
        second.start()
    for copy in away:
        copy.wait()


def finish(*results):
    hbm = pl.BlockSpec(memory_space=pl.ANY)
    return pl.pallas_call(
        finish_kernel,
        in_specs=[hbm] * 5,
        out_specs=[hbm] * 5,
        out_shape=[jax.ShapeDtypeStruct(a.shape, a.dtype) for a in results],
        scratch_shapes=[pltpu.VMEM(a.shape, a.dtype) for a in results]
        + [pltpu.SemaphoreType.DMA((22,))],
        compiler_params=pltpu.CompilerParams(vmem_limit_bytes=56 * 2**20),
        name="finish",
    )(*results)


def on_device(inputs, cotangent, norm_gain, norm_shift, w_qkv, w_proj, bias_table):
    lats = lax.axis_size("lat")
    lons = lax.axis_size("lon")
    vmem = pl.BlockSpec(memory_space=pltpu.VMEM)
    hbm = pl.BlockSpec(memory_space=pl.ANY)
    shape = jax.ShapeDtypeStruct
    units = 2 * WPB + WPB // 2 + GROUP
    sems = pltpu.SemaphoreType.DMA
    counts = [4, 6, 6, 8, 8] + [lons] * 4 + [lats] * 4 + [lons] * 4 + [lats] * 2
    results = pl.pallas_call(
        functools.partial(kernel, lats, lons),
        in_specs=[hbm, hbm] + [vmem] * 5,
        out_specs=[hbm, hbm] + [vmem] * 3,
        out_shape=[
            shape((12, 2, OWN), BF16),
            shape((12, 2, OWN), BF16),
            shape((C, 3 * C), F32),
            shape((C, C), F32),
            shape((HEADS, 2, POS), F32),
        ],
        scratch_shapes=[
            pltpu.VMEM((FROWS + 6, 2, FRAME), BF16),
            pltpu.VMEM((FROWS + 6, 2, FRAME), BF16),
            pltpu.VMEM((units, 2, WIN, 128), F32),
            pltpu.VMEM((units, 2, WIN, 128), F32),
            pltpu.VMEM((3, WIN, 896), F32),
            pltpu.VMEM((3, WIN, 896), F32),
            pltpu.VMEM((12, 16, ROWPAD), F32),
            pltpu.VMEM((3, WIN, 128), F32),
            pltpu.VMEM((16, 3328), F32),
            pltpu.VMEM((3 * C, C), BF16),
            pltpu.VMEM((C, C), BF16),
            pltpu.VMEM((C, 3 * C), F32),
            pltpu.VMEM((C, C), F32),
            pltpu.VMEM((C, GROUP * WIN), BF16),
            pltpu.VMEM((GROUP * WIN, 3 * C), BF16),
            pltpu.VMEM((lons, 16, WCHUNK), F32),
            pltpu.VMEM((lons, 16, WCHUNK), BF16),
            pltpu.VMEM((lons, 16, WCHUNK), BF16),
            pltpu.VMEM((TILES, 16, 128), BF16),
            pltpu.VMEM((lats, 16, 128), BF16),
            pltpu.VMEM((TILES, 16, 128), BF16),
            pltpu.VMEM((lons, 16, WCHUNK), BF16),
            pltpu.VMEM((lons, 16, TCHUNK), F32),
            pltpu.VMEM((lons, 16, TCHUNK), BF16),
            pltpu.VMEM((lons, 16, TCHUNK), BF16),
            pltpu.VMEM((lons, 16, TCHUNK), BF16),
            pltpu.VMEM((lats, 8, 128), F32),
        ]
        + [sems((n,)) for n in counts],
        compiler_params=pltpu.CompilerParams(
            collective_id=0, has_side_effects=True, vmem_limit_bytes=56 * 2**20
        ),
        name="windows",
    )(
        inputs.transpose(1, 0, 2),
        cotangent.transpose(1, 0, 2),
        norm_gain.reshape(1, C),
        norm_shift.reshape(1, C),
        w_qkv,
        w_proj,
        bias_table.transpose(1, 0, 2),
    )
    x_out, g_out, grad_q, grad_p, grad_bias = finish(*results)
    x_out, g_out, grad_bias = (a.transpose(1, 0, 2) for a in (x_out, g_out, grad_bias))
    return x_out, g_out, grad_q, grad_p, grad_bias


def solution(mesh):
    return jax.shard_map(
        on_device,
        mesh=mesh,
        in_specs=(
            P(None, "lat", "lon"),
            P(None, "lat", "lon"),
            P(),
            P(),
            P(),
            P(),
            P("lat", None, None),
        ),
        out_specs=(P(None, "lat", "lon"), P(None, "lat", "lon"), P(), P(), P("lat", None, None)),
        check_vma=False,
    )
```

```python
import functools
import math

import jax
import jax.numpy as jnp
import numpy as np
from jax import lax
from jax.experimental import pallas as pl
from jax.experimental.pallas import tpu as pltpu
from jax.sharding import PartitionSpec as P

C = 192
HEADS = 6
HD = 32
WLON = 12
WIN = 144
HALF = 72
SPAN = 23
ROWLEN = 12 * SPAN
ROWPAD = 384
COLS = 96
HALO = 6 * C
WLANES = WLON * C
OWN = COLS * C
FRAME = OWN + HALO
FROWS = 15
GROUP = 4
WPB = 8
POS = 3312
TABLE = 4096
WTILES = 72
PARTS = 16
PTILES = 5
TCHUNK = TABLE // 8
MESH = pl.DeviceIdType.MESH
EPS = 1e-5
SCALE = HD**-0.5
LOG2E = math.log2(math.e)
F32 = jnp.float32
BF16 = jnp.bfloat16


def nn(a, b):
    return lax.dot_general(a, b, (((1,), (0,)), ((), ())), preferred_element_type=F32)


def nt(a, b):
    return lax.dot_general(a, b, (((1,), (1,)), ((), ())), preferred_element_type=F32)


def tn(a, b):
    return lax.dot_general(a, b, (((0,), (0,)), ((), ())), preferred_element_type=F32)


def pick_matrix():
    row = lax.broadcasted_iota(jnp.int32, (WIN, 1), 0)
    lk = lax.rem(row, WLON)
    block = lax.div(row, WLON)
    kb = lax.rem(block, 2) * 6 + lax.div(block, 2)
    col = lax.broadcasted_iota(jnp.int32, (WIN, ROWPAD), 1)
    return jnp.where(col == kb * SPAN + 11 - lk, 1.0, 0.0).astype(BF16)


def pieces_in(frame, tokens, place, unit, count=GROUP):
    def piece(r, side, m):
        row, base = place(r, side)
        slab = frame[pl.ds(row, 3), :, pl.ds(pl.multiple_of(base + m * 2 * C, 128), 2 * C)]
        slab = slab.astype(F32).reshape(6, 2 * C)
        for n, part in ((2 * m, slab[:, :C]), (2 * m + 1, slab[:, C:])):
            slots = pl.ds(side * HALF + n, 6, stride=WLON)
            tokens[unit + r, 0, slots, :] = part[:, :128]
            tokens[unit + r, 1, slots, :] = jnp.concatenate([part[:, 128:], part[:, 128:]], axis=1)

    return [
        functools.partial(piece, r, side, m) for r in range(count) for side in range(2) for m in range(6)
    ]


def pieces_out(frame, tokens, place, unit, count=GROUP):
    def piece(r, side, m):
        row, base = place(r, side)
        for p in range(3):
            parts = []
            for n in (2 * m, 2 * m + 1):
                slots = pl.ds(side * HALF + p * 24 + n, 2, stride=WLON)
                parts.append(tokens[unit + r, 0, slots, :])
                parts.append(tokens[unit + r, 1, slots, :][:, : C - 128])
            lanes = pl.ds(pl.multiple_of(base + m * 2 * C, 128), 2 * C)
            frame[row + p, :, lanes] = jnp.concatenate(parts, axis=1).astype(BF16)

    return [
        functools.partial(piece, r, side, m) for r in range(count) for side in range(2) for m in range(6)
    ]


def put_head(ref, slot, i, value):
    ref[slot, :, i * 128 : i * 128 + 128] = value[:, :128]
    ref[slot, :, 768 + i * 16 : 768 + i * 16 + 16] = value[:, 128:]


def get_head(ref, slot, i):
    tail = ref[slot, :, 768 + i * 16 : 768 + i * 16 + 16]
    return jnp.concatenate([ref[slot, :, i * 128 : i * 128 + 128], tail], axis=1)


def bias_rows(table, flat, rows_scratch):
    rows_scratch[...] = jnp.zeros_like(rows_scratch)
    for i in range(HEADS):
        flat[2 * i : 2 * i + 2, 0:POS] = table[i]
    for zq in range(2):
        for pq in range(6):
            at = (zq * 6 + pq) * ROWLEN
            rows_scratch[pq * 2 + zq, 0:12, 0:ROWLEN] = flat[0:12, at : at + ROWLEN]


def bias_in(lo, hi, pick, rows_scratch, shifted, bias):
    for n in range(lo, hi):
        rows = rows_scratch[:, n, :]
        rows = jnp.concatenate([rows, jnp.zeros((4, ROWPAD), F32)], axis=0)
        for lq in range(WLON):
            moved = pltpu.roll(rows, (ROWPAD - lq) % ROWPAD, 1) if lq else rows
            for t in range(3):
                shifted[t, pl.ds(lq, 12, stride=12), :] = moved[:12, t * 128 : t * 128 + 128]
        full = jnp.concatenate([shifted[t] for t in range(3)], axis=1)
        high = full.astype(BF16)
        low = (full - high.astype(F32)).astype(BF16)
        total = nt(pick, high) + nt(pick, low)
        put_head(bias, n % 2, n // 2, total * LOG2E)


def bias_out(grads, pick, shifted, rows_scratch):
    for n in range(12):
        full = nn(get_head(grads, n % 2, n // 2).astype(BF16).T, pick)
        for t in range(3):
            shifted[t] = full[:, t * 128 : t * 128 + 128]
        total = jnp.zeros((16, ROWPAD), F32)
        for lq in range(WLON):
            rows = [shifted[t, pl.ds(lq, 12, stride=12), :] for t in range(3)]
            rows = jnp.concatenate(rows, axis=1)
            rows = jnp.concatenate([rows, jnp.zeros((4, ROWPAD), F32)], axis=0)
            total = total + (pltpu.roll(rows, lq, 1) if lq else rows)
        rows_scratch[:, n, :] = total[:12]
    parts = [rows_scratch[pq * 2 + zq][:, :ROWLEN] for zq in range(2) for pq in range(6)]
    parts.append(jnp.zeros((16, TABLE - POS), F32))
    return jnp.concatenate(parts, axis=1)


def head_rows(a):
    lane = lax.broadcasted_iota(jnp.int32, (1, 128), 1) // HD
    zero = jnp.zeros((), BF16)

    def only(part, i):
        return jnp.where(lane[:, : part.shape[1]] == i % 4, part, zero)

    wide, slim = a[:, :128], a[:, 128:C]
    first = jnp.concatenate([only(wide[:128], i) for i in range(4)], axis=0)
    second = jnp.concatenate([only(slim[:128], i) for i in range(4, HEADS)], axis=0)
    tail = [only(wide[128:], i) for i in range(4)]
    left = jnp.concatenate(tail + [jnp.zeros((64, 128), BF16)], axis=0)
    tail = [only(slim[128:], i) for i in range(4, HEADS)]
    right = jnp.concatenate([jnp.zeros((64, 64), BF16)] + tail + [jnp.zeros((32, 64), BF16)], axis=0)
    return first, second, left, right


def across(a, rows):
    first, second, left, right = rows
    return jnp.concatenate(
        [nt(a[:, :128], first), nt(a[:, 128:C], second), nt(a, jnp.concatenate([left, right], axis=1))],
        axis=1,
    )


def gathered(a, rows):
    first, second, left, right = rows
    tail = nn(a[:, 768:], jnp.concatenate([left, right], axis=1))
    return jnp.concatenate(
        [nn(a[:, :512], first) + tail[:, :128], nn(a[:, 512:768], second) + tail[:, 128:]], axis=1
    )


def by_head(t, a):
    tail = nn(t, a[:, 768:])
    out = []
    for j in range(HEADS // 2):
        pair = nn(t[64 * j : 64 * j + 64], a[:, 256 * j : 256 * j + 256])
        for i in (2 * j, 2 * j + 1):
            r = (i % 2) * HD
            main = pair[r : r + HD, r * 4 : r * 4 + 128]
            out.append(jnp.concatenate([main, tail[i * HD : i * HD + HD, 16 * i : 16 * i + 16]], axis=1))
    return jnp.concatenate(out, axis=0)


def weight_sums(raw_q, h_t, dqkv):
    for j in range(3):
        raw_q[:, j * C : j * C + C] += nn(h_t, dqkv[:, j * C : j * C + C])


def attend(
    x_ref, g_ref, us, bias, dbias, slot, gain, shift, wqkv, wqkv_t, wproj, wproj_t, raw_q, raw_p, held_h, held_d, early, late
):
    n = WIN
    ws = range(len(us))
    early, late = iter(early), iter(late)

    def emit(queue, count):
        for _ in range(count):
            step = next(queue, None)
            if step is not None:
                step()

    def tokens(ref):
        rows = [jnp.concatenate([ref[u, 0], ref[u, 1]], axis=1) for u in us]
        return jnp.concatenate(rows, axis=0)[:, :C]

    def split(a):
        return [a[w * n : (w + 1) * n] for w in ws]

    x = tokens(x_ref)
    g = tokens(g_ref)
    gb = g.astype(BF16)
    do = split(nn(gb, wproj_t[...]).astype(BF16))
    weight_sums(raw_q, held_h[...], held_d[...])
    center = x - jnp.mean(x, axis=1, keepdims=True)
    rstd = lax.rsqrt(jnp.mean(center * center, axis=1, keepdims=True) + EPS)
    xn = center * rstd
    h = (xn * gain + shift).astype(BF16)
    held_h[...] = h.T
    qkv = split(nn(h, wqkv[...]).astype(BF16))
    q = [a[:, :C] for a in qkv]
    k = [a[:, C : 2 * C] for a in qkv]
    v = [a[:, 2 * C :] for a in qkv]
    k_t = [a.T for a in k]
    v_t = [a.T for a in v]
    qr = [head_rows(a) for a in q]
    dor = [head_rows(a) for a in do]
    s, dp, pb, dsb, o_t, dq_t, dv, dk = {}, {}, {}, {}, {}, {}, {}, {}

    def scores(w):
        def one(out, a, rows):
            out[w] = across(a[w], rows[w])

        return [functools.partial(one, s, k, qr), functools.partial(one, dp, v, dor)]

    def products(w):
        def one(out, act, *args):
            out[w] = act(*args).astype(BF16)

        return [
            functools.partial(one, dq_t, by_head, k_t[w], dsb[w]),
            functools.partial(one, dk, gathered, dsb[w], qr[w]),
            functools.partial(one, dv, gathered, pb[w], dor[w]),
            functools.partial(one, o_t, by_head, v_t[w], pb[w]),
        ]

    halves = [ws[n : n + 2] for n in range(0, len(us), 2)]
    for w in halves[0]:
        for step in scores(w):
            step()
    for at, duo in enumerate(halves):
        ready = [step for w in halves[at - 1] for step in products(w)] if at else []
        if at + 1 < len(halves):
            ready += [step for w in halves[at + 1] for step in scores(w)]
        ps, dss = {w: [] for w in duo}, {w: [] for w in duo}
        for b in range(7):
            lanes = slice(b * 128, b * 128 + 128)
            add = bias[slot, :, lanes]
            change = 0.0
            for w in duo:
                t = s[w][:, lanes] * (SCALE * LOG2E) + add
                e = jnp.exp2(t - jnp.max(t, axis=0, keepdims=True))
                p = e * (1.0 / jnp.sum(e, axis=0, keepdims=True))
                d = dp[w][:, lanes]
                ds = p * (d - jnp.sum(p * d, axis=0, keepdims=True))
                change = change + ds
                ps[w].append(p.astype(BF16))
                dss[w].append((ds * SCALE).astype(BF16))
                if ready:
                    ready.pop(0)()
            dbias[slot, :, lanes] += change
        for step in ready:
            step()
        for w in duo:
            pb[w] = jnp.concatenate(ps[w], axis=1)
            dsb[w] = jnp.concatenate(dss[w], axis=1)
    for w in halves[-1]:
        for step in products(w):
            step()
    dk = [dk[w] for w in ws]
    dv = [dv[w] for w in ws]
    dk = jnp.concatenate(dk, axis=0)
    dv = jnp.concatenate(dv, axis=0)
    dq = jnp.concatenate([dq_t[w].T for w in ws], axis=0)
    dqkv = jnp.concatenate([dq, dk, dv], axis=1)
    held_d[...] = dqkv
    dh = nn(dqkv, wqkv_t[...])
    emit(late, 0)
    o = jnp.concatenate([o_t[w].T for w in ws], axis=0)
    dxn = dh * gain
    m1 = jnp.mean(dxn, axis=1, keepdims=True)
    m2 = jnp.mean(dxn * xn, axis=1, keepdims=True)
    dx = (rstd * (dxn - m1 - xn * m2)).astype(BF16)
    g = split(g + dx.astype(F32))
    a = nn(o, wproj[...]).astype(BF16)
    raw_p[...] += sum(nn(o_t[w], gb[w * n : (w + 1) * n]) for w in ws)
    x = split(x + a.astype(F32))
    emit(early, 10**6)
    emit(late, 10**6)
    for w, u in enumerate(us):
        x_ref[u, 0] = x[w][:, :128]
        x_ref[u, 1, :, 0:64] = x[w][:, 128:]
        g_ref[u, 0] = g[w][:, :128]
        g_ref[u, 1, :, 0:64] = g[w][:, 128:]


def copy_to(src, dst, send, recv, lat, lon):
    return pltpu.make_async_remote_copy(
        src_ref=src,
        dst_ref=dst,
        send_sem=send,
        recv_sem=recv,
        device_id=(lat, lon),
        device_id_type=MESH,
    )


def greet(lat, lon):
    barrier = pltpu.get_barrier_semaphore()
    pl.semaphore_signal(barrier, inc=1, device_id=(lat, lon), device_id_type=MESH)


def each(lo, hi, skip, act):
    def step(i, _):
        @pl.when(i != skip)
        def _():
            act(i)

        return 0

    lax.fori_loop(lo, hi, step, 0)


def kernel(
    lats,
    lons,
    x,
    g,
    gain_ref,
    shift_ref,
    wqkv,
    wproj,
    table,
    x_out,
    g_out,
    sum_w,
    sum_t,
    squares,
    fx,
    fg,
    xw,
    gw,
    bias,
    dbias,
    rows_scratch,
    shifted,
    flat,
    wqkv_t,
    wproj_t,
    raw_q,
    raw_p,
    held_h,
    held_d,
    mine_w,
    part_w,
    part_w_in,
    cross,
    mine_t,
    part_t,
    part_t_in,
    own_sem,
    halo_send,
    halo_recv,
    ret_send,
    ret_recv,
    w_send,
    w_recv,
    t_send,
    t_recv,
    tile_send,
    tile_recv,
    wb_send,
    wb_recv,
    tb_send,
    tb_recv,
    sq_send,
    sq_recv,
):
    lat = lax.axis_index("lat")
    lon = lax.axis_index("lon")
    west = lax.rem(lon + lons - 1, lons)
    east = lax.rem(lon + 1, lons)
    first = lat == 0
    final = lat == lats - 1
    barrier = pltpu.get_barrier_semaphore()
    core = lax.rem(lat, 2)
    base = lat - core
    own = 2 * lon + core
    each(0, PARTS, own, lambda m: greet(base + lax.rem(m, 2), m // 2))
    each(0, lats // 2, lat // 2, lambda a: greet(2 * a, lon))
    each(0, lats // 2, lat // 2, lambda a: greet(2 * a + 1, lon))

    @pl.when(lat > 0)
    def _():
        greet(lat - 1, west)

    @pl.when(lat < lats - 1)
    def _():
        greet(lat + 1, east)

    pairs = ((x, fx), (g, fg))
    local = []
    for n, (src, frame) in enumerate(pairs):
        local.append(
            pltpu.make_async_copy(
                src.at[3:12, :, HALO:OWN], frame.at[3:12, :, HALO:OWN], own_sem.at[n]
            )
        )
    polar = []
    for n, (src, frame) in enumerate(pairs):
        polar.append(
            pltpu.make_async_copy(
                src.at[0:3, :, HALO:OWN], frame.at[0:3, :, HALO:OWN], own_sem.at[2 + n]
            )
        )
    for copy in local:
        copy.start()

    @pl.when(first)
    def _():
        for copy in polar:
            copy.start()

    wqkv_t[...] = wqkv[...].T
    wproj_t[...] = wproj[...].T

    ups, sides, diags = [], [], []
    for n, (src, frame) in enumerate(pairs):
        ups.append(
            copy_to(
                src.at[0:3, :, HALO:OWN],
                frame.at[12:15, :, HALO:OWN],
                halo_send.at[n],
                halo_recv.at[n],
                lat - 1,
                lon,
            )
        )
        sides.append(
            copy_to(
                src.at[:, :, 0:HALO],
                frame.at[0:12, :, OWN:FRAME],
                halo_send.at[2 + n],
                halo_recv.at[2 + n],
                lat,
                west,
            )
        )
        diags.append(
            copy_to(
                src.at[0:3, :, 0:HALO],
                frame.at[12:15, :, OWN:FRAME],
                halo_send.at[4 + n],
                halo_recv.at[4 + n],
                lat - 1,
                west,
            )
        )
    pick = pick_matrix()
    bias[:, :, 768:] = jnp.zeros((3, WIN, 128), F32)
    bias_rows(table, flat, rows_scratch)
    bias_in(0, 6, pick, rows_scratch, shifted, bias)
    peers = PARTS - 1 + lats - 2
    pl.semaphore_wait(barrier, peers + jnp.where(lat > 0, 1, 0) + jnp.where(lat < lats - 1, 1, 0))
    for copy in sides:
        copy.start()

    @pl.when(lat > 0)
    def _():
        for copy in ups + diags:
            copy.start()

    bias_in(6, 12, pick, rows_scratch, shifted, bias)
    dbias[...] = jnp.zeros_like(dbias)
    raw_q[...] = jnp.zeros_like(raw_q)
    raw_p[...] = jnp.zeros_like(raw_p)

    for copy in local:
        copy.wait()
    def halves_in(slot, source, lo):
        for i in range(HEADS):
            part = get_head(bias, source, i)[lo : lo + HALF, lo : lo + HALF]
            away = jnp.full((HALF, HALF), -1e9, F32)
            top = jnp.concatenate([part, away], axis=1)
            low = jnp.concatenate([away, part], axis=1)
            put_head(bias, slot, i, jnp.concatenate([top, low], axis=0))

    def halves_grad(slot, target, lo):
        zero = jnp.zeros((HALF, HALF), F32)
        for i in range(HEADS):
            both = get_head(dbias, slot, i)
            part = both[:HALF, :HALF] + both[HALF:, HALF:]
            part = jnp.concatenate([zero, part] if lo else [part, zero], axis=1)
            none = jnp.zeros((HALF, WIN), F32)
            part = jnp.concatenate([none, part] if lo else [part, none], axis=0)
            old = get_head(dbias, target, i) if target != slot else 0.0
            put_head(dbias, target, i, old + part)

    @pl.when(first)
    def _():
        for copy in polar:
            copy.wait()
        halves_in(2, 0, HALF)

    @pl.when(final)
    def _():
        halves_in(1, 1, 0)

    rest = (gain_ref[...], shift_ref[...], wqkv, wqkv_t, wproj, wproj_t, raw_q, raw_p, held_h, held_d)
    full = 2 * WPB // GROUP
    half = WPB // 2 // GROUP
    steps = jnp.where(first, full + half, jnp.where(final, full // 2 + half, full))

    def place(v, r, side, spare):
        halved = (first & (v == full)) | (final & (v == full // 2))
        row = jnp.where(halved, jnp.where(first, 0, 9), 3 + 6 * (v // (full // 2)) + 3 * side)
        window = jnp.where(halved, 2 * r + side, lax.rem(v, full // 2) * GROUP + r)
        return jnp.where(spare, FROWS + 3 * side, row), HALO + window * WLANES

    def laying(v, unit, out, spare=False):
        move = pieces_out if out else pieces_in
        at = functools.partial(lambda r, side: place(v, r, side, spare))
        both = zip(move(fx, xw, at, unit), move(fg, gw, at, unit))
        return [step for pair in both for step in pair]

    held_h[...] = jnp.zeros_like(held_h)
    held_d[...] = jnp.zeros_like(held_d)

    def start(r, _):
        for frame, tokens in ((fx, xw), (fg, gw)):
            for step in pieces_in(frame, tokens, lambda _, side: place(0, r, side, False), r, 1):
                step()
        return 0

    lax.fori_loop(0, GROUP, start, 0)
    for copy in sides:
        copy.wait_recv()

    def group(u, _):
        @pl.when((u == full // 2 - 1) & (lat < lats - 1))
        def _():
            for copy in ups + diags:
                copy.wait_recv()

        slot = jnp.minimum(u // (WPB // GROUP), 2)
        us = [GROUP * u + r for r in range(GROUP)]
        behind = jnp.maximum(u - 1, 0)
        early = laying(behind, GROUP * behind, True, u == 0)
        late = laying(jnp.minimum(u + 1, steps - 1), GROUP * (u + 1), False)
        attend(xw, gw, us, bias, dbias, slot, *rest, early, late)
        return 0

    lax.fori_loop(0, steps, group, 0)
    weight_sums(raw_q, held_h[...], held_d[...])

    raw = jnp.concatenate([raw_q[...], raw_p[...]], axis=1)
    for m in range(PARTS):
        row = []
        for col in range(m * PTILES, m * PTILES + PTILES):
            r, c = col // 6 * 16, col % 6 * 128
            row.append(raw[r : r + 16, c : c + 128] if col < WTILES else jnp.zeros((16, 128), F32))
        chunk = jnp.concatenate(row, axis=1)
        mine_w[m] = chunk
        part_w[m] = chunk.astype(BF16)

    def member(m):
        return base + lax.rem(m, 2), m // 2

    def w_out(m):
        return copy_to(part_w.at[m], part_w_in.at[own], w_send.at[m], w_recv.at[own], *member(m))

    def w_in(m):
        return copy_to(part_w.at[m], part_w_in.at[m], w_send.at[m], w_recv.at[m], *member(m))

    each(0, PARTS, own, lambda m: w_out(m).start())

    downs, crosses, backs, tops = [], [], [], []
    for n, frame in enumerate((fx, fg)):
        rows = frame.at[0:3, :, HALO:OWN]
        side = frame.at[3:12, :, 0:HALO]
        corner = frame.at[0:3, :, 0:HALO]
        sems = [(ret_send.at[2 * r + n], ret_recv.at[2 * r + n]) for r in range(4)]
        downs.append(copy_to(frame.at[12:15, :, HALO:OWN], rows, *sems[0], lat + 1, lon))
        crosses.append(copy_to(frame.at[12:15, :, OWN:FRAME], corner, *sems[1], lat + 1, east))
        backs.append(copy_to(frame.at[3:12, :, OWN:FRAME], side, *sems[2], lat, east))
        tops.append(copy_to(frame.at[0:3, :, OWN:FRAME], corner, *sems[3], lat, east))

    def finish_out(r, _):
        for frame, tokens in ((fx, xw), (fg, gw)):
            at = lambda _, side: place(steps - 1, r, side, False)
            for step in pieces_out(frame, tokens, at, GROUP * (steps - 1) + r, 1):
                step()
        return 0

    lax.fori_loop(0, GROUP, finish_out, 0)

    @pl.when(lat < lats - 1)
    def _():
        for copy in downs + crosses:
            copy.start()

    @pl.when(first)
    def _():
        for copy in tops:
            copy.start()

    for copy in backs:
        copy.start()

    @pl.when(first)
    def _():
        halves_grad(2, 0, HALF)

    @pl.when(final)
    def _():
        halves_grad(1, 1, 0)

    grads = bias_out(dbias, pick, shifted, rows_scratch)
    for j in range(lons):
        chunk = grads[:, j * TCHUNK : (j + 1) * TCHUNK]
        mine_t[j] = chunk
        part_t[j] = chunk.astype(BF16)

    def t_out(o):
        return copy_to(part_t.at[o], part_t_in.at[lon], t_send.at[o], t_recv.at[lon], lat, o)

    def t_in(o):
        return copy_to(part_t.at[o], part_t_in.at[o], t_send.at[o], t_recv.at[o], lat, o)

    each(0, lons, lon, lambda o: t_out(o).start())

    def add_w(d, total):
        m = lax.rem(own + d, PARTS)
        w_in(m).wait_recv()
        return total + part_w_in[m].astype(F32)

    chip = lat // 2
    cross[chip] = lax.fori_loop(1, PARTS, add_w, mine_w[own]).astype(BF16)

    def cross_out(a):
        at = cross.at[chip]
        return copy_to(at, at, tile_send.at[a], tile_recv.at[chip], 2 * a + core, lon)

    def cross_in(a):
        at = cross.at[a]
        return copy_to(at, at, tile_send.at[a], tile_recv.at[a], 2 * a + core, lon)

    each(0, lats // 2, chip, lambda a: cross_out(a).start())

    def add_t(d, total):
        o = lax.rem(lon + d, lons)
        t_in(o).wait_recv()
        return total + part_t_in[o].astype(F32)

    sum_t[lon] = lax.fori_loop(1, lons, add_t, mine_t[lon]).astype(BF16)

    def tb_out(o):
        return copy_to(sum_t.at[lon], sum_t.at[lon], tb_send.at[o], tb_recv.at[lon], lat, o)

    def tb_in(o):
        return copy_to(sum_t.at[o], sum_t.at[o], tb_send.at[o], tb_recv.at[o], lat, o)

    each(0, lons, lon, lambda o: tb_out(o).start())

    each(0, lats // 2, chip, lambda a: cross_in(a).wait_recv())
    total = cross[0].astype(F32)
    for a in range(1, lats // 2):
        total = total + cross[a].astype(F32)
    sum_w[own] = total.astype(BF16)

    def wb_out(m):
        return copy_to(sum_w.at[own], sum_w.at[own], wb_send.at[m], wb_recv.at[own], *member(m))

    def wb_in(m):
        return copy_to(sum_w.at[m], sum_w.at[m], wb_send.at[m], wb_recv.at[m], *member(m))

    each(0, PARTS, own, lambda m: wb_out(m).start())

    each(0, lons, lon, lambda o: tb_in(o).wait_recv())
    whole = jnp.concatenate([sum_t[j].astype(F32) for j in range(lons)], axis=1)
    square = jnp.sum(whole * whole).reshape(1, 1)
    squares[lat] = jnp.broadcast_to(square, (8, 128))

    def sq_out(a):
        return copy_to(squares.at[lat], squares.at[lat], sq_send.at[a], sq_recv.at[lat], a, lon)

    def sq_in(a):
        return copy_to(squares.at[a], squares.at[a], sq_send.at[a], sq_recv.at[a], a, lon)

    each(0, lats, lat, lambda a: sq_out(a).start())

    for copy in backs:
        copy.wait()

    @pl.when(lat > 0)
    def _():
        for copy in downs + crosses:
            copy.wait_recv()

    @pl.when(lat < lats - 1)
    def _():
        for copy in downs + crosses:
            copy.wait_send()

    @pl.when(first)
    def _():
        for copy in tops:
            copy.wait()

    leave = [
        pltpu.make_async_copy(frame.at[0:12, :, 0:OWN], out, own_sem.at[n])
        for n, (frame, out) in enumerate(((fx, x_out), (fg, g_out)))
    ]
    for copy in leave:
        copy.start()

    each(0, lats, lat, lambda a: sq_in(a).wait_recv())
    each(0, PARTS, own, lambda m: wb_in(m).wait_recv())

    def sent_w(m):
        w_out(m).wait_send()
        wb_out(m).wait_send()

    def sent_t(o):
        t_out(o).wait_send()
        tb_out(o).wait_send()

    each(0, PARTS, own, sent_w)
    each(0, lons, lon, sent_t)
    each(0, lats // 2, chip, lambda a: cross_out(a).wait_send())
    each(0, lats, lat, lambda a: sq_out(a).wait_send())

    for copy in sides:
        copy.wait_send()

    @pl.when(lat > 0)
    def _():
        for copy in ups + diags:
            copy.wait_send()

    for copy in leave:
        copy.wait()


def finish_kernel(lats, lons, x, g, sum_w, sum_t, squares, x_out, g_out, q_out, p_out, b_out, xs, gs, ws, ts, ss, grad_q, grad_p, grad_bias, sems):
    small = [(sum_w, ws), (sum_t, ts), (squares, ss)]
    moves = []
    for src, mid, dst in ((x, xs, x_out), (g, gs, g_out)):
        for r in range(0, 12, 3):
            part = slice(r, r + 3)
            moves.append((src.at[part], mid.at[part], dst.at[part]))
    into = [pltpu.make_async_copy(m[0], m[1], sems.at[n]) for n, m in enumerate(moves)]
    away = [pltpu.make_async_copy(m[1], m[2], sems.at[8 + n]) for n, m in enumerate(moves)]
    small = [pltpu.make_async_copy(*pair, sems.at[16 + n]) for n, pair in enumerate(small)]
    ends = ((grad_q, q_out), (grad_p, p_out), (grad_bias, b_out))
    ends = [pltpu.make_async_copy(*pair, sems.at[19 + n]) for n, pair in enumerate(ends)]
    for copy in small + into:
        copy.start()
    for copy in small:
        copy.wait()
    cols = []
    square = jnp.zeros((16, 128), F32)
    for col in range(WTILES):
        m, t = col // PTILES, col % PTILES
        piece = ws[m, :, t * 128 : t * 128 + 128].astype(F32)
        square = square + piece * piece
        cols.append(piece)
    rms = jnp.sqrt(jnp.sum(square).reshape(1, 1) / (4 * C * C) + 1e-6)
    inverse = 1.0 / rms
    for r in range(12):
        row = jnp.concatenate(cols[r * 6 : r * 6 + 6], axis=1) * inverse
        grad_q[r * 16 : r * 16 + 16] = row[:, : 3 * C]
        grad_p[r * 16 : r * 16 + 16] = row[:, 3 * C :]
    ends[0].start()
    ends[1].start()
    for first, second in zip(into, away):
        first.wait()
        second.start()
    table_squares = jnp.zeros((1, 1), F32)
    for a in range(lats):
        table_squares = table_squares + ss[a][0:1, 0:1]
    table_rms = jnp.sqrt(table_squares / (lats * 2 * HEADS * POS) + 1e-6)
    whole = jnp.concatenate([ts[j].astype(F32) for j in range(lons)], axis=1)
    whole = whole[:, :POS] * (1.0 / table_rms)
    for i in range(HEADS):
        grad_bias[i] = whole[2 * i : 2 * i + 2]
    ends[2].start()
    for copy in away + ends:
        copy.wait()


def finish(lats, lons, *results):
    hbm = pl.BlockSpec(memory_space=pl.ANY)
    shapes = [
        jax.ShapeDtypeStruct((12, 2, OWN), BF16),
        jax.ShapeDtypeStruct((12, 2, OWN), BF16),
        jax.ShapeDtypeStruct((C, 3 * C), F32),
        jax.ShapeDtypeStruct((C, C), F32),
        jax.ShapeDtypeStruct((HEADS, 2, POS), F32),
    ]
    return pl.pallas_call(
        functools.partial(finish_kernel, lats, lons),
        in_specs=[hbm] * 5,
        out_specs=[hbm] * 5,
        out_shape=shapes,
        scratch_shapes=[pltpu.VMEM(a.shape, a.dtype) for a in list(results) + shapes[2:]]
        + [pltpu.SemaphoreType.DMA((22,))],
        compiler_params=pltpu.CompilerParams(vmem_limit_bytes=56 * 2**20),
        name="finish",
    )(*results)


def on_device(inputs, cotangent, norm_gain, norm_shift, w_qkv, w_proj, bias_table):
    lats = lax.axis_size("lat")
    lons = lax.axis_size("lon")
    vmem = pl.BlockSpec(memory_space=pltpu.VMEM)
    hbm = pl.BlockSpec(memory_space=pl.ANY)
    shape = jax.ShapeDtypeStruct
    units = 2 * WPB + WPB // 2 + GROUP
    sems = pltpu.SemaphoreType.DMA
    counts = [4, 6, 6, 8, 8] + [PARTS] * 2 + [lons] * 2 + [lats // 2] * 2 + [PARTS] * 2 + [lons] * 2 + [lats] * 2
    results = pl.pallas_call(
        functools.partial(kernel, lats, lons),
        in_specs=[hbm, hbm] + [vmem] * 5,
        out_specs=[hbm, hbm] + [vmem] * 3,
        out_shape=[
            shape((12, 2, OWN), BF16),
            shape((12, 2, OWN), BF16),
            shape((PARTS, 16, PTILES * 128), BF16),
            shape((lons, 16, TCHUNK), BF16),
            shape((lats, 8, 128), F32),
        ],
        scratch_shapes=[
            pltpu.VMEM((FROWS + 6, 2, FRAME), BF16),
            pltpu.VMEM((FROWS + 6, 2, FRAME), BF16),
            pltpu.VMEM((units, 2, WIN, 128), F32),
            pltpu.VMEM((units, 2, WIN, 128), F32),
            pltpu.VMEM((3, WIN, 896), F32),
            pltpu.VMEM((3, WIN, 896), F32),
            pltpu.VMEM((12, 16, ROWPAD), F32),
            pltpu.VMEM((3, WIN, 128), F32),
            pltpu.VMEM((16, 3328), F32),
            pltpu.VMEM((3 * C, C), BF16),
            pltpu.VMEM((C, C), BF16),
            pltpu.VMEM((C, 3 * C), F32),
            pltpu.VMEM((C, C), F32),
            pltpu.VMEM((C, GROUP * WIN), BF16),
            pltpu.VMEM((GROUP * WIN, 3 * C), BF16),
            pltpu.VMEM((PARTS, 16, PTILES * 128), F32),
            pltpu.VMEM((PARTS, 16, PTILES * 128), BF16),
            pltpu.VMEM((PARTS, 16, PTILES * 128), BF16),
            pltpu.VMEM((lats // 2, 16, PTILES * 128), BF16),
            pltpu.VMEM((lons, 16, TCHUNK), F32),
            pltpu.VMEM((lons, 16, TCHUNK), BF16),
            pltpu.VMEM((lons, 16, TCHUNK), BF16),
        ]
        + [sems((n,)) for n in counts],
        compiler_params=pltpu.CompilerParams(
            collective_id=0, has_side_effects=True, vmem_limit_bytes=56 * 2**20
        ),
        name="windows",
    )(
        inputs.transpose(1, 0, 2),
        cotangent.transpose(1, 0, 2),
        norm_gain.reshape(1, C),
        norm_shift.reshape(1, C),
        w_qkv,
        w_proj,
        bias_table.transpose(1, 0, 2),
    )
    x_out, g_out, grad_q, grad_p, grad_bias = finish(lats, lons, *results)
    x_out, g_out, grad_bias = (a.transpose(1, 0, 2) for a in (x_out, g_out, grad_bias))
    return x_out, g_out, grad_q, grad_p, grad_bias


def solution(mesh):
    return jax.shard_map(
        on_device,
        mesh=mesh,
        in_specs=(
            P(None, "lat", "lon"),
            P(None, "lat", "lon"),
            P(),
            P(),
            P(),
            P(),
            P("lat", None, None),
        ),
        out_specs=(P(None, "lat", "lon"), P(None, "lat", "lon"), P(), P(), P("lat", None, None)),
        check_vma=False,
    )
```

```python
import functools
import math

import jax
import jax.numpy as jnp
import numpy as np
from jax import lax
from jax.experimental import pallas as pl
from jax.experimental.pallas import tpu as pltpu
from jax.sharding import PartitionSpec as P

C = 192
HEADS = 6
HD = 32
WLON = 12
WIN = 144
HALF = 72
SPAN = 23
ROWLEN = 12 * SPAN
ROWPAD = 384
COLS = 96
HALO = 6 * C
WLANES = WLON * C
OWN = COLS * C
FRAME = OWN + HALO
FROWS = 15
GROUP = 4
WPB = 8
POS = 3312
TABLE = 4096
WTILES = 72
PARTS = 16
PTILES = 5
TCHUNK = TABLE // 8
MESH = pl.DeviceIdType.MESH
EPS = 1e-5
SCALE = HD**-0.5
LOG2E = math.log2(math.e)
F32 = jnp.float32
BF16 = jnp.bfloat16


def nn(a, b):
    return lax.dot_general(a, b, (((1,), (0,)), ((), ())), preferred_element_type=F32)


def nt(a, b):
    return lax.dot_general(a, b, (((1,), (1,)), ((), ())), preferred_element_type=F32)


def tn(a, b):
    return lax.dot_general(a, b, (((0,), (0,)), ((), ())), preferred_element_type=F32)


def pick_matrix(lq):
    row = lax.broadcasted_iota(jnp.int32, (WIN, 1), 0)
    lk = lax.rem(row, WLON)
    block = lax.div(row, WLON)
    kb = lax.rem(block, 2) * 6 + lax.div(block, 2)
    col = lax.broadcasted_iota(jnp.int32, (WIN, ROWPAD), 1)
    return jnp.where(col == kb * SPAN + 11 + lq - lk, 1.0, 0.0).astype(BF16)


def pieces_in(frame, tokens, place, unit, count=GROUP):
    def piece(r, side, m):
        row, base = place(r, side)
        slab = frame[pl.ds(row, 3), :, pl.ds(pl.multiple_of(base + m * 2 * C, 128), 2 * C)]
        slab = slab.astype(F32).reshape(6, 2 * C)
        for n, part in ((2 * m, slab[:, :C]), (2 * m + 1, slab[:, C:])):
            slots = pl.ds(side * HALF + n, 6, stride=WLON)
            tokens[unit + r, 0, slots, :] = part[:, :128]
            tokens[unit + r, 1, slots, :] = jnp.concatenate([part[:, 128:], part[:, 128:]], axis=1)

    return [
        functools.partial(piece, r, side, m) for r in range(count) for side in range(2) for m in range(6)
    ]


def pieces_out(frame, tokens, place, unit, count=GROUP):
    def piece(r, side, m):
        row, base = place(r, side)
        for p in range(3):
            parts = []
            for n in (2 * m, 2 * m + 1):
                slots = pl.ds(side * HALF + p * 24 + n, 2, stride=WLON)
                parts.append(tokens[unit + r, 0, slots, :])
                parts.append(tokens[unit + r, 1, slots, :][:, : C - 128])
            lanes = pl.ds(pl.multiple_of(base + m * 2 * C, 128), 2 * C)
            frame[row + p, :, lanes] = jnp.concatenate(parts, axis=1).astype(BF16)

    return [
        functools.partial(piece, r, side, m) for r in range(count) for side in range(2) for m in range(6)
    ]


def put_head(ref, slot, i, value):
    ref[slot, :, i * 128 : i * 128 + 128] = value[:, :128]
    ref[slot, :, 768 + i * 16 : 768 + i * 16 + 16] = value[:, 128:]


def get_head(ref, slot, i):
    tail = ref[slot, :, 768 + i * 16 : 768 + i * 16 + 16]
    return jnp.concatenate([ref[slot, :, i * 128 : i * 128 + 128], tail], axis=1)


def bias_rows(table, flat, rows_scratch):
    rows_scratch[...] = jnp.zeros_like(rows_scratch)
    for i in range(HEADS):
        flat[2 * i : 2 * i + 2, 0:POS] = table[i]
    for zq in range(2):
        for pq in range(6):
            at = (zq * 6 + pq) * ROWLEN
            rows_scratch[pq * 2 + zq, 0:12, 0:ROWLEN] = flat[0:12, at : at + ROWLEN]


def bias_in(lo, hi, pick, rows_scratch, shifted, bias):
    for n in range(lo, hi):
        rows = rows_scratch[:, n, :]
        rows = jnp.concatenate([rows, jnp.zeros((4, ROWPAD), F32)], axis=0)
        for lq in range(WLON):
            moved = pltpu.roll(rows, (ROWPAD - lq) % ROWPAD, 1) if lq else rows
            for t in range(3):
                shifted[t, pl.ds(lq, 12, stride=12), :] = moved[:12, t * 128 : t * 128 + 128]
        full = jnp.concatenate([shifted[t] for t in range(3)], axis=1)
        high = full.astype(BF16)
        low = (full - high.astype(F32)).astype(BF16)
        total = nt(pick, high) + nt(pick, low)
        put_head(bias, n % 2, n // 2, total * LOG2E)


def bias_out(grads, natural):
    for n in range(12):
        full = get_head(grads, n % 2, n // 2).astype(BF16).T.astype(F32)
        block = slice(n * WIN, n * WIN + WIN)
        natural[0, block, :] = full[:, :128]
        natural[1, block, 0 : WIN - 128] = full[:, 128:]
    total = jnp.zeros((WIN, ROWPAD), F32)
    for lq in range(WLON):
        rows = [natural[0, pl.ds(lq, WIN, stride=WLON), :]]
        rows.append(natural[1, pl.ds(lq, WIN, stride=WLON), :][:, : WIN - 128])
        total = total + nn(jnp.concatenate(rows, axis=1).astype(BF16), pick_matrix(lq))
    for t in range(3):
        natural[2, t * WIN : t * WIN + WIN, :] = total[:, t * 128 : t * 128 + 128]
    parts = []
    for zq in range(2):
        for pq in range(6):
            part = [natural[2, pl.ds(t * WIN + pq * 2 + zq, 12, stride=12), :] for t in range(3)]
            parts.append(jnp.concatenate(part, axis=1)[:, :ROWLEN])
    parts.append(jnp.zeros((12, TABLE - POS), F32))
    return jnp.concatenate([jnp.concatenate(parts, axis=1), jnp.zeros((4, TABLE), F32)], axis=0)


def head_rows(a):
    lane = lax.broadcasted_iota(jnp.int32, (1, 128), 1) // HD
    zero = jnp.zeros((), BF16)

    def only(part, i):
        return jnp.where(lane[:, : part.shape[1]] == i % 4, part, zero)

    wide, slim = a[:, :128], a[:, 128:C]
    first = jnp.concatenate([only(wide[:128], i) for i in range(4)], axis=0)
    second = jnp.concatenate([only(slim[:128], i) for i in range(4, HEADS)], axis=0)
    tail = [only(wide[128:], i) for i in range(4)]
    left = jnp.concatenate(tail + [jnp.zeros((64, 128), BF16)], axis=0)
    tail = [only(slim[128:], i) for i in range(4, HEADS)]
    right = jnp.concatenate([jnp.zeros((64, 64), BF16)] + tail + [jnp.zeros((32, 64), BF16)], axis=0)
    return first, second, left, right


def across(a, rows):
    first, second, left, right = rows
    return jnp.concatenate(
        [nt(a[:, :128], first), nt(a[:, 128:C], second), nt(a, jnp.concatenate([left, right], axis=1))],
        axis=1,
    )


def gathered(a, rows):
    first, second, left, right = rows
    tail = nn(a[:, 768:], jnp.concatenate([left, right], axis=1))
    return jnp.concatenate(
        [nn(a[:, :512], first) + tail[:, :128], nn(a[:, 512:768], second) + tail[:, 128:]], axis=1
    )


def by_head(t, a):
    tail = nn(t, a[:, 768:])
    out = []
    for j in range(HEADS // 2):
        pair = nn(t[64 * j : 64 * j + 64], a[:, 256 * j : 256 * j + 256])
        for i in (2 * j, 2 * j + 1):
            r = (i % 2) * HD
            main = pair[r : r + HD, r * 4 : r * 4 + 128]
            out.append(jnp.concatenate([main, tail[i * HD : i * HD + HD, 16 * i : 16 * i + 16]], axis=1))
    return jnp.concatenate(out, axis=0)


def weight_sums(raw_q, h_t, dqkv):
    for j in range(3):
        raw_q[:, j * C : j * C + C] += nn(h_t, dqkv[:, j * C : j * C + C])


def attend(
    x_ref, g_ref, us, bias, dbias, slot, gain, shift, wqkv, wqkv_t, wproj, wproj_t, raw_q, raw_p, held_h, held_d, early, late
):
    n = WIN
    ws = range(len(us))
    early, late = iter(early), iter(late)

    def emit(queue, count):
        for _ in range(count):
            step = next(queue, None)
            if step is not None:
                step()

    def tokens(ref):
        rows = [jnp.concatenate([ref[u, 0], ref[u, 1]], axis=1) for u in us]
        return jnp.concatenate(rows, axis=0)[:, :C]

    def split(a):
        return [a[w * n : (w + 1) * n] for w in ws]

    x = tokens(x_ref)
    g = tokens(g_ref)
    gb = g.astype(BF16)
    do = split(nn(gb, wproj_t[...]).astype(BF16))
    weight_sums(raw_q, held_h[...], held_d[...])
    center = x - jnp.mean(x, axis=1, keepdims=True)
    rstd = lax.rsqrt(jnp.mean(center * center, axis=1, keepdims=True) + EPS)
    xn = center * rstd
    h = (xn * gain + shift).astype(BF16)
    held_h[...] = h.T
    qkv = split(nn(h, wqkv[...]).astype(BF16))
    q = [a[:, :C] for a in qkv]
    k = [a[:, C : 2 * C] for a in qkv]
    v = [a[:, 2 * C :] for a in qkv]
    k_t = [a.T for a in k]
    v_t = [a.T for a in v]
    qr = [head_rows(a) for a in q]
    dor = [head_rows(a) for a in do]
    s, dp, pb, dsb, o_t, dq_t, dv, dk = {}, {}, {}, {}, {}, {}, {}, {}

    def scores(w):
        def one(out, a, rows):
            out[w] = across(a[w], rows[w])

        return [functools.partial(one, s, k, qr), functools.partial(one, dp, v, dor)]

    def products(w):
        def one(out, act, *args):
            out[w] = act(*args).astype(BF16)

        return [
            functools.partial(one, dq_t, by_head, k_t[w], dsb[w]),
            functools.partial(one, dk, gathered, dsb[w], qr[w]),
            functools.partial(one, dv, gathered, pb[w], dor[w]),
            functools.partial(one, o_t, by_head, v_t[w], pb[w]),
        ]

    halves = [ws[n : n + 2] for n in range(0, len(us), 2)]
    for w in halves[0]:
        for step in scores(w):
            step()
    for at, duo in enumerate(halves):
        ready = [step for w in halves[at - 1] for step in products(w)] if at else []
        if at + 1 < len(halves):
            ready += [step for w in halves[at + 1] for step in scores(w)]
        ps, dss = {w: [] for w in duo}, {w: [] for w in duo}
        for b in range(7):
            lanes = slice(b * 128, b * 128 + 128)
            add = bias[slot, :, lanes]
            change = 0.0
            for w in duo:
                t = s[w][:, lanes] * (SCALE * LOG2E) + add
                e = jnp.exp2(t - jnp.max(t, axis=0, keepdims=True))
                p = e * (1.0 / jnp.sum(e, axis=0, keepdims=True))
                d = dp[w][:, lanes]
                ds = p * (d - jnp.sum(p * d, axis=0, keepdims=True))
                change = change + ds
                ps[w].append(p.astype(BF16))
                dss[w].append((ds * SCALE).astype(BF16))
                if ready:
                    ready.pop(0)()
            dbias[slot, :, lanes] += change
        for step in ready:
            step()
        for w in duo:
            pb[w] = jnp.concatenate(ps[w], axis=1)
            dsb[w] = jnp.concatenate(dss[w], axis=1)
    for w in halves[-1]:
        for step in products(w):
            step()
    dk = [dk[w] for w in ws]
    dv = [dv[w] for w in ws]
    dk = jnp.concatenate(dk, axis=0)
    dv = jnp.concatenate(dv, axis=0)
    dq = jnp.concatenate([dq_t[w].T for w in ws], axis=0)
    dqkv = jnp.concatenate([dq, dk, dv], axis=1)
    held_d[...] = dqkv
    dh = nn(dqkv, wqkv_t[...])
    emit(late, 0)
    o = jnp.concatenate([o_t[w].T for w in ws], axis=0)
    dxn = dh * gain
    m1 = jnp.mean(dxn, axis=1, keepdims=True)
    m2 = jnp.mean(dxn * xn, axis=1, keepdims=True)
    dx = (rstd * (dxn - m1 - xn * m2)).astype(BF16)
    g = split(g + dx.astype(F32))
    a = nn(o, wproj[...]).astype(BF16)
    raw_p[...] += sum(nn(o_t[w], gb[w * n : (w + 1) * n]) for w in ws)
    x = split(x + a.astype(F32))
    emit(early, 10**6)
    emit(late, 10**6)
    for w, u in enumerate(us):
        x_ref[u, 0] = x[w][:, :128]
        x_ref[u, 1, :, 0:64] = x[w][:, 128:]
        g_ref[u, 0] = g[w][:, :128]
        g_ref[u, 1, :, 0:64] = g[w][:, 128:]


def copy_to(src, dst, send, recv, lat, lon):
    return pltpu.make_async_remote_copy(
        src_ref=src,
        dst_ref=dst,
        send_sem=send,
        recv_sem=recv,
        device_id=(lat, lon),
        device_id_type=MESH,
    )


def greet(lat, lon):
    barrier = pltpu.get_barrier_semaphore()
    pl.semaphore_signal(barrier, inc=1, device_id=(lat, lon), device_id_type=MESH)


def each(lo, hi, skip, act):
    def step(i, _):
        @pl.when(i != skip)
        def _():
            act(i)

        return 0

    lax.fori_loop(lo, hi, step, 0)


def kernel(
    lats,
    lons,
    x,
    g,
    gain_ref,
    shift_ref,
    wqkv,
    wproj,
    table,
    x_out,
    g_out,
    sum_w,
    sum_t,
    squares,
    fx,
    fg,
    xw,
    gw,
    bias,
    dbias,
    rows_scratch,
    shifted,
    natural,
    flat,
    wqkv_t,
    wproj_t,
    raw_q,
    raw_p,
    held_h,
    held_d,
    mine_w,
    part_w,
    part_w_in,
    cross,
    mine_t,
    part_t,
    part_t_in,
    own_sem,
    halo_send,
    halo_recv,
    ret_send,
    ret_recv,
    w_send,
    w_recv,
    t_send,
    t_recv,
    tile_send,
    tile_recv,
    wb_send,
    wb_recv,
    tb_send,
    tb_recv,
    sq_send,
    sq_recv,
):
    lat = lax.axis_index("lat")
    lon = lax.axis_index("lon")
    west = lax.rem(lon + lons - 1, lons)
    east = lax.rem(lon + 1, lons)
    first = lat == 0
    final = lat == lats - 1
    barrier = pltpu.get_barrier_semaphore()
    core = lax.rem(lat, 2)
    base = lat - core
    own = 2 * lon + core
    each(0, PARTS, own, lambda m: greet(base + lax.rem(m, 2), m // 2))
    each(0, lats // 2, lat // 2, lambda a: greet(2 * a, lon))
    each(0, lats // 2, lat // 2, lambda a: greet(2 * a + 1, lon))

    @pl.when(lat > 0)
    def _():
        greet(lat - 1, west)

    @pl.when(lat < lats - 1)
    def _():
        greet(lat + 1, east)

    pairs = ((x, fx), (g, fg))
    local = []
    for n, (src, frame) in enumerate(pairs):
        local.append(
            pltpu.make_async_copy(
                src.at[3:12, :, HALO:OWN], frame.at[3:12, :, HALO:OWN], own_sem.at[n]
            )
        )
    polar = []
    for n, (src, frame) in enumerate(pairs):
        polar.append(
            pltpu.make_async_copy(
                src.at[0:3, :, HALO:OWN], frame.at[0:3, :, HALO:OWN], own_sem.at[2 + n]
            )
        )
    for copy in local:
        copy.start()

    @pl.when(first)
    def _():
        for copy in polar:
            copy.start()

    wqkv_t[...] = wqkv[...].T
    wproj_t[...] = wproj[...].T

    ups, sides, diags = [], [], []
    for n, (src, frame) in enumerate(pairs):
        ups.append(
            copy_to(
                src.at[0:3, :, HALO:OWN],
                frame.at[12:15, :, HALO:OWN],
                halo_send.at[n],
                halo_recv.at[n],
                lat - 1,
                lon,
            )
        )
        sides.append(
            copy_to(
                src.at[:, :, 0:HALO],
                frame.at[0:12, :, OWN:FRAME],
                halo_send.at[2 + n],
                halo_recv.at[2 + n],
                lat,
                west,
            )
        )
        diags.append(
            copy_to(
                src.at[0:3, :, 0:HALO],
                frame.at[12:15, :, OWN:FRAME],
                halo_send.at[4 + n],
                halo_recv.at[4 + n],
                lat - 1,
                west,
            )
        )
    pick = pick_matrix(0)
    bias[:, :, 768:] = jnp.zeros((3, WIN, 128), F32)
    bias_rows(table, flat, rows_scratch)
    bias_in(0, 6, pick, rows_scratch, shifted, bias)
    peers = PARTS - 1 + lats - 2
    pl.semaphore_wait(barrier, peers + jnp.where(lat > 0, 1, 0) + jnp.where(lat < lats - 1, 1, 0))
    for copy in sides:
        copy.start()

    @pl.when(lat > 0)
    def _():
        for copy in ups + diags:
            copy.start()

    bias_in(6, 12, pick, rows_scratch, shifted, bias)
    dbias[...] = jnp.zeros_like(dbias)
    raw_q[...] = jnp.zeros_like(raw_q)
    raw_p[...] = jnp.zeros_like(raw_p)

    for copy in local:
        copy.wait()
    def halves_in(slot, source, lo):
        for i in range(HEADS):
            part = get_head(bias, source, i)[lo : lo + HALF, lo : lo + HALF]
            away = jnp.full((HALF, HALF), -1e9, F32)
            top = jnp.concatenate([part, away], axis=1)
            low = jnp.concatenate([away, part], axis=1)
            put_head(bias, slot, i, jnp.concatenate([top, low], axis=0))

    def halves_grad(slot, target, lo):
        zero = jnp.zeros((HALF, HALF), F32)
        for i in range(HEADS):
            both = get_head(dbias, slot, i)
            part = both[:HALF, :HALF] + both[HALF:, HALF:]
            part = jnp.concatenate([zero, part] if lo else [part, zero], axis=1)
            none = jnp.zeros((HALF, WIN), F32)
            part = jnp.concatenate([none, part] if lo else [part, none], axis=0)
            old = get_head(dbias, target, i) if target != slot else 0.0
            put_head(dbias, target, i, old + part)

    @pl.when(first)
    def _():
        for copy in polar:
            copy.wait()
        halves_in(2, 0, HALF)

    @pl.when(final)
    def _():
        halves_in(1, 1, 0)

    rest = (gain_ref[...], shift_ref[...], wqkv, wqkv_t, wproj, wproj_t, raw_q, raw_p, held_h, held_d)
    full = 2 * WPB // GROUP
    half = WPB // 2 // GROUP
    steps = jnp.where(first, full + half, jnp.where(final, full // 2 + half, full))

    def place(v, r, side, spare):
        halved = (first & (v == full)) | (final & (v == full // 2))
        row = jnp.where(halved, jnp.where(first, 0, 9), 3 + 6 * (v // (full // 2)) + 3 * side)
        window = jnp.where(halved, 2 * r + side, lax.rem(v, full // 2) * GROUP + r)
        return jnp.where(spare, FROWS + 3 * side, row), HALO + window * WLANES

    def laying(v, unit, out, spare=False):
        move = pieces_out if out else pieces_in
        at = functools.partial(lambda r, side: place(v, r, side, spare))
        both = zip(move(fx, xw, at, unit), move(fg, gw, at, unit))
        return [step for pair in both for step in pair]

    held_h[...] = jnp.zeros_like(held_h)
    held_d[...] = jnp.zeros_like(held_d)

    def start(r, _):
        for frame, tokens in ((fx, xw), (fg, gw)):
            for step in pieces_in(frame, tokens, lambda _, side: place(0, r, side, False), r, 1):
                step()
        return 0

    lax.fori_loop(0, GROUP, start, 0)
    for copy in sides:
        copy.wait_recv()

    def group(u, _):
        @pl.when((u == full // 2 - 1) & (lat < lats - 1))
        def _():
            for copy in ups + diags:
                copy.wait_recv()

        slot = jnp.minimum(u // (WPB // GROUP), 2)
        us = [GROUP * u + r for r in range(GROUP)]
        behind = jnp.maximum(u - 1, 0)
        early = laying(behind, GROUP * behind, True, u == 0)
        late = laying(jnp.minimum(u + 1, steps - 1), GROUP * (u + 1), False)
        attend(xw, gw, us, bias, dbias, slot, *rest, early, late)
        return 0

    lax.fori_loop(0, steps, group, 0)
    weight_sums(raw_q, held_h[...], held_d[...])

    downs, crosses, backs, tops = [], [], [], []
    for n, frame in enumerate((fx, fg)):
        rows = frame.at[0:3, :, HALO:OWN]
        side = frame.at[3:12, :, 0:HALO]
        corner = frame.at[0:3, :, 0:HALO]
        sems = [(ret_send.at[2 * r + n], ret_recv.at[2 * r + n]) for r in range(4)]
        downs.append(copy_to(frame.at[12:15, :, HALO:OWN], rows, *sems[0], lat + 1, lon))
        crosses.append(copy_to(frame.at[12:15, :, OWN:FRAME], corner, *sems[1], lat + 1, east))
        backs.append(copy_to(frame.at[3:12, :, OWN:FRAME], side, *sems[2], lat, east))
        tops.append(copy_to(frame.at[0:3, :, OWN:FRAME], corner, *sems[3], lat, east))

    def finish_out(r, _):
        for frame, tokens in ((fx, xw), (fg, gw)):
            at = lambda _, side: place(steps - 1, r, side, False)
            for step in pieces_out(frame, tokens, at, GROUP * (steps - 1) + r, 1):
                step()
        return 0

    lax.fori_loop(0, GROUP, finish_out, 0)

    @pl.when(lat < lats - 1)
    def _():
        for copy in downs + crosses:
            copy.start()

    @pl.when(first)
    def _():
        for copy in tops:
            copy.start()

    for copy in backs:
        copy.start()

    raw = jnp.concatenate([raw_q[...], raw_p[...]], axis=1)
    for m in range(PARTS):
        row = []
        for col in range(m * PTILES, m * PTILES + PTILES):
            r, c = col // 6 * 16, col % 6 * 128
            row.append(raw[r : r + 16, c : c + 128] if col < WTILES else jnp.zeros((16, 128), F32))
        chunk = jnp.concatenate(row, axis=1)
        mine_w[m] = chunk
        part_w[m] = chunk.astype(BF16)

    def member(m):
        return base + lax.rem(m, 2), m // 2

    def w_out(m):
        return copy_to(part_w.at[m], part_w_in.at[own], w_send.at[m], w_recv.at[own], *member(m))

    def w_in(m):
        return copy_to(part_w.at[m], part_w_in.at[m], w_send.at[m], w_recv.at[m], *member(m))

    each(0, PARTS, own, lambda m: w_out(m).start())

    @pl.when(first)
    def _():
        halves_grad(2, 0, HALF)

    @pl.when(final)
    def _():
        halves_grad(1, 1, 0)

    grads = bias_out(dbias, natural)
    for j in range(lons):
        chunk = grads[:, j * TCHUNK : (j + 1) * TCHUNK]
        mine_t[j] = chunk
        part_t[j] = chunk.astype(BF16)

    def t_out(o):
        return copy_to(part_t.at[o], part_t_in.at[lon], t_send.at[o], t_recv.at[lon], lat, o)

    def t_in(o):
        return copy_to(part_t.at[o], part_t_in.at[o], t_send.at[o], t_recv.at[o], lat, o)

    each(0, lons, lon, lambda o: t_out(o).start())

    def add_w(d, total):
        m = lax.rem(own + d, PARTS)
        w_in(m).wait_recv()
        return total + part_w_in[m].astype(F32)

    chip = lat // 2
    cross[chip] = lax.fori_loop(1, PARTS, add_w, mine_w[own]).astype(BF16)

    def cross_out(a):
        at = cross.at[chip]
        return copy_to(at, at, tile_send.at[a], tile_recv.at[chip], 2 * a + core, lon)

    def cross_in(a):
        at = cross.at[a]
        return copy_to(at, at, tile_send.at[a], tile_recv.at[a], 2 * a + core, lon)

    each(0, lats // 2, chip, lambda a: cross_out(a).start())

    def add_t(d, total):
        o = lax.rem(lon + d, lons)
        t_in(o).wait_recv()
        return total + part_t_in[o].astype(F32)

    sum_t[lon] = lax.fori_loop(1, lons, add_t, mine_t[lon]).astype(BF16)

    def tb_out(o):
        return copy_to(sum_t.at[lon], sum_t.at[lon], tb_send.at[o], tb_recv.at[lon], lat, o)

    def tb_in(o):
        return copy_to(sum_t.at[o], sum_t.at[o], tb_send.at[o], tb_recv.at[o], lat, o)

    each(0, lons, lon, lambda o: tb_out(o).start())

    each(0, lats // 2, chip, lambda a: cross_in(a).wait_recv())
    total = cross[0].astype(F32)
    for a in range(1, lats // 2):
        total = total + cross[a].astype(F32)
    sum_w[own] = total.astype(BF16)

    def wb_out(m):
        return copy_to(sum_w.at[own], sum_w.at[own], wb_send.at[m], wb_recv.at[own], *member(m))

    def wb_in(m):
        return copy_to(sum_w.at[m], sum_w.at[m], wb_send.at[m], wb_recv.at[m], *member(m))

    each(0, PARTS, own, lambda m: wb_out(m).start())

    each(0, lons, lon, lambda o: tb_in(o).wait_recv())
    whole = jnp.concatenate([sum_t[j].astype(F32) for j in range(lons)], axis=1)
    square = jnp.sum(whole * whole).reshape(1, 1)
    squares[lat] = jnp.broadcast_to(square, (8, 128))

    def sq_out(a):
        return copy_to(squares.at[lat], squares.at[lat], sq_send.at[a], sq_recv.at[lat], a, lon)

    def sq_in(a):
        return copy_to(squares.at[a], squares.at[a], sq_send.at[a], sq_recv.at[a], a, lon)

    each(0, lats, lat, lambda a: sq_out(a).start())

    for copy in backs:
        copy.wait()

    @pl.when(lat > 0)
    def _():
        for copy in downs + crosses:
            copy.wait_recv()

    @pl.when(lat < lats - 1)
    def _():
        for copy in downs + crosses:
            copy.wait_send()

    @pl.when(first)
    def _():
        for copy in tops:
            copy.wait()

    leave = [
        pltpu.make_async_copy(frame.at[0:12, :, 0:OWN], out, own_sem.at[n])
        for n, (frame, out) in enumerate(((fx, x_out), (fg, g_out)))
    ]
    for copy in leave:
        copy.start()

    each(0, lats, lat, lambda a: sq_in(a).wait_recv())
    each(0, PARTS, own, lambda m: wb_in(m).wait_recv())

    def sent_w(m):
        w_out(m).wait_send()
        wb_out(m).wait_send()

    def sent_t(o):
        t_out(o).wait_send()
        tb_out(o).wait_send()

    each(0, PARTS, own, sent_w)
    each(0, lons, lon, sent_t)
    each(0, lats // 2, chip, lambda a: cross_out(a).wait_send())
    each(0, lats, lat, lambda a: sq_out(a).wait_send())

    for copy in sides:
        copy.wait_send()

    @pl.when(lat > 0)
    def _():
        for copy in ups + diags:
            copy.wait_send()

    for copy in leave:
        copy.wait()


def finish_kernel(lats, lons, x, g, sum_w, sum_t, squares, x_out, g_out, q_out, p_out, b_out, xs, gs, ws, ts, ss, grad_q, grad_p, grad_bias, sems):
    small = [(sum_w, ws), (sum_t, ts), (squares, ss)]
    moves = []
    for src, mid, dst in ((x, xs, x_out), (g, gs, g_out)):
        for r in range(0, 12, 3):
            part = slice(r, r + 3)
            moves.append((src.at[part], mid.at[part], dst.at[part]))
    into = [pltpu.make_async_copy(m[0], m[1], sems.at[n]) for n, m in enumerate(moves)]
    away = [pltpu.make_async_copy(m[1], m[2], sems.at[8 + n]) for n, m in enumerate(moves)]
    small = [pltpu.make_async_copy(*pair, sems.at[16 + n]) for n, pair in enumerate(small)]
    ends = ((grad_q, q_out), (grad_p, p_out), (grad_bias, b_out))
    ends = [pltpu.make_async_copy(*pair, sems.at[19 + n]) for n, pair in enumerate(ends)]
    for copy in small + into:
        copy.start()
    for copy in small:
        copy.wait()
    cols = []
    square = jnp.zeros((16, 128), F32)
    for col in range(WTILES):
        m, t = col // PTILES, col % PTILES
        piece = ws[m, :, t * 128 : t * 128 + 128].astype(F32)
        square = square + piece * piece
        cols.append(piece)
    rms = jnp.sqrt(jnp.sum(square).reshape(1, 1) / (4 * C * C) + 1e-6)
    inverse = 1.0 / rms
    for r in range(12):
        row = jnp.concatenate(cols[r * 6 : r * 6 + 6], axis=1) * inverse
        grad_q[r * 16 : r * 16 + 16] = row[:, : 3 * C]
        grad_p[r * 16 : r * 16 + 16] = row[:, 3 * C :]
    ends[0].start()
    ends[1].start()
    for first, second in zip(into, away):
        first.wait()
        second.start()
    table_squares = jnp.zeros((1, 1), F32)
    for a in range(lats):
        table_squares = table_squares + ss[a][0:1, 0:1]
    table_rms = jnp.sqrt(table_squares / (lats * 2 * HEADS * POS) + 1e-6)
    whole = jnp.concatenate([ts[j].astype(F32) for j in range(lons)], axis=1)
    whole = whole[:, :POS] * (1.0 / table_rms)
    for i in range(HEADS):
        grad_bias[i] = whole[2 * i : 2 * i + 2]
    ends[2].start()
    for copy in away + ends:
        copy.wait()


def finish(lats, lons, *results):
    hbm = pl.BlockSpec(memory_space=pl.ANY)
    shapes = [
        jax.ShapeDtypeStruct((12, 2, OWN), BF16),
        jax.ShapeDtypeStruct((12, 2, OWN), BF16),
        jax.ShapeDtypeStruct((C, 3 * C), F32),
        jax.ShapeDtypeStruct((C, C), F32),
        jax.ShapeDtypeStruct((HEADS, 2, POS), F32),
    ]
    return pl.pallas_call(
        functools.partial(finish_kernel, lats, lons),
        in_specs=[hbm] * 5,
        out_specs=[hbm] * 5,
        out_shape=shapes,
        scratch_shapes=[pltpu.VMEM(a.shape, a.dtype) for a in list(results) + shapes[2:]]
        + [pltpu.SemaphoreType.DMA((22,))],
        compiler_params=pltpu.CompilerParams(vmem_limit_bytes=56 * 2**20),
        name="finish",
    )(*results)


def on_device(inputs, cotangent, norm_gain, norm_shift, w_qkv, w_proj, bias_table):
    lats = lax.axis_size("lat")
    lons = lax.axis_size("lon")
    vmem = pl.BlockSpec(memory_space=pltpu.VMEM)
    hbm = pl.BlockSpec(memory_space=pl.ANY)
    shape = jax.ShapeDtypeStruct
    units = 2 * WPB + WPB // 2 + GROUP
    sems = pltpu.SemaphoreType.DMA
    counts = [4, 6, 6, 8, 8] + [PARTS] * 2 + [lons] * 2 + [lats // 2] * 2 + [PARTS] * 2 + [lons] * 2 + [lats] * 2
    results = pl.pallas_call(
        functools.partial(kernel, lats, lons),
        in_specs=[hbm, hbm] + [vmem] * 5,
        out_specs=[hbm, hbm] + [vmem] * 3,
        out_shape=[
            shape((12, 2, OWN), BF16),
            shape((12, 2, OWN), BF16),
            shape((PARTS, 16, PTILES * 128), BF16),
            shape((lons, 16, TCHUNK), BF16),
            shape((lats, 8, 128), F32),
        ],
        scratch_shapes=[
            pltpu.VMEM((FROWS + 6, 2, FRAME), BF16),
            pltpu.VMEM((FROWS + 6, 2, FRAME), BF16),
            pltpu.VMEM((units, 2, WIN, 128), F32),
            pltpu.VMEM((units, 2, WIN, 128), F32),
            pltpu.VMEM((3, WIN, 896), F32),
            pltpu.VMEM((3, WIN, 896), F32),
            pltpu.VMEM((12, 16, ROWPAD), F32),
            pltpu.VMEM((3, WIN, 128), F32),
            pltpu.VMEM((3, 12 * WIN, 128), F32),
            pltpu.VMEM((16, 3328), F32),
            pltpu.VMEM((3 * C, C), BF16),
            pltpu.VMEM((C, C), BF16),
            pltpu.VMEM((C, 3 * C), F32),
            pltpu.VMEM((C, C), F32),
            pltpu.VMEM((C, GROUP * WIN), BF16),
            pltpu.VMEM((GROUP * WIN, 3 * C), BF16),
            pltpu.VMEM((PARTS, 16, PTILES * 128), F32),
            pltpu.VMEM((PARTS, 16, PTILES * 128), BF16),
            pltpu.VMEM((PARTS, 16, PTILES * 128), BF16),
            pltpu.VMEM((lats // 2, 16, PTILES * 128), BF16),
            pltpu.VMEM((lons, 16, TCHUNK), F32),
            pltpu.VMEM((lons, 16, TCHUNK), BF16),
            pltpu.VMEM((lons, 16, TCHUNK), BF16),
        ]
        + [sems((n,)) for n in counts],
        compiler_params=pltpu.CompilerParams(
            collective_id=0, has_side_effects=True, vmem_limit_bytes=56 * 2**20
        ),
        name="windows",
    )(
        inputs.transpose(1, 0, 2),
        cotangent.transpose(1, 0, 2),
        norm_gain.reshape(1, C),
        norm_shift.reshape(1, C),
        w_qkv,
        w_proj,
        bias_table.transpose(1, 0, 2),
    )
    x_out, g_out, grad_q, grad_p, grad_bias = finish(lats, lons, *results)
    x_out, g_out, grad_bias = (a.transpose(1, 0, 2) for a in (x_out, g_out, grad_bias))
    return x_out, g_out, grad_q, grad_p, grad_bias


def solution(mesh):
    return jax.shard_map(
        on_device,
        mesh=mesh,
        in_specs=(
            P(None, "lat", "lon"),
            P(None, "lat", "lon"),
            P(),
            P(),
            P(),
            P(),
            P("lat", None, None),
        ),
        out_specs=(P(None, "lat", "lon"), P(None, "lat", "lon"), P(), P(), P("lat", None, None)),
        check_vma=False,
    )
```
